32 devices in a mesh: trench: 8 (over y, x, core), tblock: 4 (over z).
Axes of the slice: x: 2, y: 2, z: 4, core: 2. Of those that a mesh axis runs over, the one named last changes fastest.
Arguments:
- adjoint_eta: float32 [4, 30, 128, 512], P('tblock', None, 'trench'), may hold values from -6 to 6
- adjoint_flow: float32 [4, 30, 128, 512], P('tblock', None, 'trench'), may hold values from -6 to 6
- residual: float32 [4, 8, 8, 4, 32], P('tblock', 'trench'), may hold values from -6 to 6
- sensor_cell: int32 [8, 8, 32], replicated, may hold values from 0 to 8191
- sensor_count: int32 [8, 8], replicated, may hold values from 0 to 32, as said below
- depth_class: int32 [128, 512], P('trench'), may hold values from 0 to 7
- speed_table: float32 [8], replicated, may hold values from 0.1 to 0.3
- damping: float32 [30], replicated, may hold values from 0.6 to 1
- profile: float32 [30], replicated, may hold values from 0.3 to 1
- band_weight: float32 [8], replicated, may hold values from 0.3 to 1
Outputs:
- uplift_grad: float32 [16, 128, 512], P(None, ('trench', 'tblock'))
The draws below stay inside these ranges and needn't reach their ends.
Inputs may be any that keep to these rules, and one draw needn't show every extreme that they name: `sensor_cell`: column index inside the owning tile, row times 512 plus column. `sensor_count`: in every draw some owning tile receives 32 live slots from every source tile.
All inputs are finite; a program needn't handle non-finite values.
Results may differ from the reference program's by a relative error of at most 0.0001.
Values sent between devices are 32-bit elements; how exact they have to be, the bound alone decides.
No kernel may reach another device: no remote copies, remote signals or barrier semaphores. Data moves between devices by JAX's collectives and lax.ppermute only.
A program may use at most 64 MiB of HBM per device.

```python
import math
import jax
import jax.numpy as jnp
from jax import lax

LEVELS = 30
CX = 16
NY = 512
STEPS = 4
CAP = 32
NCLASS = 8
BAND = 8
NOWN = 8
NWIN = 4
NX = 128


def draw_sensor_count(key, part):
    first, second, third, fourth = jax.random.split(key, 4)
    base = jax.random.randint(first, (NOWN, NOWN), 0, CAP // 2 + 1, dtype=jnp.int32)
    heavy_owner = jax.random.randint(second, (NOWN,), 0, 4, dtype=jnp.int32) == 0
    higher = jax.random.randint(third, (NOWN, NOWN), CAP // 2, CAP + 1, dtype=jnp.int32)
    counted = jnp.where(heavy_owner[None, :], higher, base)
    full_owner = jax.random.randint(fourth, (), 0, NOWN, dtype=jnp.int32)
    columns = jnp.arange(NOWN, dtype=jnp.int32)
    return jnp.where(columns[None, :] == full_owner, jnp.int32(CAP), counted).astype(jnp.int32)


def plant(array, stream_key, low, high):
    extent = array.shape
    place = [jax.random.randint(jax.random.fold_in(stream_key, axis), (), 0, extent[axis]) for axis in range(len(extent))]
    array = array.at[tuple(place)].set(low)
    longest = extent.index(max(extent))
    place[longest] = (place[longest] + 1) % extent[longest]
    return array.at[tuple(place)].set(high)


def block_levels(stream_key, extent, cuts, smallest, high):
    loudness = 1.0
    for position, blocks in cuts:
        draws = jax.random.uniform(jax.random.fold_in(jax.random.fold_in(stream_key, 6), position), (blocks,), jnp.float32, smallest / len(cuts), high / len(cuts))
        loudness = loudness * jnp.repeat(jnp.exp(draws), extent[position] // blocks).reshape((-1,) + (1,) * (len(extent) - 1 - position))
    return loudness


def gaussian(key, shape, deviation, limit, cuts=(), kind=jnp.bfloat16):
    factor_of = block_levels(key, shape, cuts, -0.22, 0.18) if cuts else 1.0
    drawn = jax.random.normal(key, shape, jnp.float32) * deviation * factor_of
    return jnp.minimum(jnp.maximum(drawn, -limit), limit).astype(kind)


def setup_inputs(seed: int = 0) -> dict:
    arg_keys = jax.random.split(jax.random.key(seed), 11)
    adjoint_eta = gaussian(arg_keys[0], (NWIN, LEVELS, NX, NY), 1.0, 6.0, ((0, 4), (2, 8)), jnp.float32)
    adjoint_flow = gaussian(arg_keys[1], (NWIN, LEVELS, NX, NY), 1.0, 6.0, ((0, 4), (2, 8)), jnp.float32)
    residual = gaussian(arg_keys[2], (NWIN, NOWN, NOWN, STEPS, CAP), 1.0, 6.0, ((0, 4), (1, 8)), jnp.float32)
    sensor_cell = plant(jax.random.randint(arg_keys[3], (NOWN, NOWN, CAP), 0, CX * NY), jax.random.fold_in(arg_keys[3], 1), 0, (CX * NY) - 1).astype(jnp.int32)
    sensor_count = draw_sensor_count(jax.random.fold_in(arg_keys[10], 71), 0)
    depth_class = plant(jax.random.randint(arg_keys[5], (NX, NY), 0, NCLASS), jax.random.fold_in(arg_keys[5], 1), 0, NCLASS - 1).astype(jnp.int32)
    speed_table = jnp.clip(jax.random.uniform(arg_keys[6], (NCLASS,), jnp.float32, 0.1, 0.3), 0.1, 0.3)
    damping = jnp.clip(jax.random.uniform(arg_keys[7], (LEVELS,), jnp.float32, 0.6, 1.0), 0.6, 1.0)
    profile = jnp.clip(jax.random.uniform(arg_keys[8], (LEVELS,), jnp.float32, 0.3, 1.0), 0.3, 1.0)
    band_weight = jnp.clip(jax.random.uniform(arg_keys[9], (BAND,), jnp.float32, 0.3, 1.0), 0.3, 1.0)
    return dict(adjoint_eta=adjoint_eta, adjoint_flow=adjoint_flow, residual=residual, sensor_cell=sensor_cell, sensor_count=sensor_count, depth_class=depth_class, speed_table=speed_table, damping=damping, profile=profile, band_weight=band_weight)


VERT = 0.2

def lookup(depth_class, speed_table):
    classes = jnp.arange(speed_table.shape[0], dtype=jnp.int32)
    return lax.optimization_barrier(jnp.sum(jnp.where(depth_class[..., None] == classes, speed_table, jnp.float32(0.0)), axis=-1))

def advance(widened, displace, momentum, celerity, inject, damping):
    across_pad = jnp.pad(displace, ((0, 0), (0, 0), (1, 1)))
    laplace = widened[:, 2:] + widened[:, :-2] + across_pad[:, :, 2:] + across_pad[:, :, :-2] - 4.0 * displace
    level_pad = jnp.pad(displace, ((1, 1), (0, 0), (0, 0)))
    vertical = level_pad[2:] + level_pad[:-2] - 2.0 * displace
    levels = displace.shape[0]
    bottom = (jnp.arange(levels, dtype=jnp.int32) == levels - 1).astype(jnp.float32)
    momentum = damping[:, None, None] * momentum + celerity[None] * laplace + VERT * vertical + bottom[:, None, None] * inject[None]
    return (displace + momentum, momentum)

def prior(series, band_weight):
    width_band = band_weight.shape[0]
    length = series.shape[0]
    padded = jnp.pad(series, ((0, width_band - 1), (0, 0), (0, 0)))
    result = jnp.zeros_like(series)
    for offset in range(width_band):
        result = result + band_weight[offset] * padded[offset:offset + length]
    return result

def reference(adjoint_eta, adjoint_flow, residual, sensor_cell, sensor_count, depth_class, speed_table, damping, profile, band_weight):
    celerity = lookup(depth_class, speed_table)
    level_scale = 1.0 / math.sqrt(LEVELS)
    slot_ids = jnp.arange(CAP, dtype=jnp.int32)
    alive_mask = (slot_ids[None, None, :] < sensor_count[:, :, None]).astype(jnp.float32)
    owners = jnp.arange(NOWN, dtype=jnp.int32)
    target = (owners[None, :, None] * (CX * NY) + sensor_cell).reshape(-1).astype(jnp.int32)
    series_list = []
    for window in range(NWIN):
        values = residual[window] * alive_mask[:, :, None, :]
        values = jnp.transpose(values, (2, 0, 1, 3)).reshape(STEPS, -1)
        inject_all = jnp.zeros((STEPS, NX * NY), jnp.float32).at[:, target].add(values).reshape(STEPS, NX, NY)
        displace = adjoint_eta[window]
        momentum = adjoint_flow[window]
        pieces = [None] * STEPS
        for step_back in range(STEPS):
            moment = STEPS - 1 - step_back
            widened = jnp.pad(displace, ((0, 0), (1, 1), (0, 0)))
            displace, momentum = advance(widened, displace, momentum, celerity, inject_all[moment], damping)
            pieces[moment] = lax.optimization_barrier(jnp.sum(profile[:, None, None] * momentum, axis=0)) * level_scale
        series_list.extend(pieces)
    series = jnp.stack(series_list, 0)
    return prior(series, band_weight)
```

```python
import functools
import math

import jax
import jax.numpy as jnp
from jax import lax
from jax.experimental import pallas as pl
from jax.experimental.pallas import tpu as pltpu
from jax.sharding import PartitionSpec as P

VERT = 0.2
STEPS = 4
PAD = 8
VMEM = pltpu.VMEM
SMEM = pltpu.SMEM
LIMIT = 32 * 1024 * 1024

FIELDS = [(4, 4), (4, 3), (4, 2), (3, 2), (4, 1), (3, 1), (2, 1), (4, 0), (3, 0), (2, 0), (1, 0)]
HALO = [4, 3, 2, 2, 1, 1, 1]
HALO_AT = [4, 8, 11, 13, 15, 16, 17]
CEL_AT = 18
CEL_HALO = 3
ROWS = 24


def split(x):
    hi = x.astype(jnp.bfloat16)
    return hi, (x - hi.astype(jnp.float32)).astype(jnp.bfloat16)


def dot(a, b, dims=((1,), (0,))):
    return lax.dot_general(a, b, (dims, ((), ())), preferred_element_type=jnp.float32)


def contract_kernel(
    eta, flow, residual, count, depth, table, damping, profile,
    fields, send, cel, coef,
    eta_v, flow_v, sems,
):
    me = lax.axis_index("trench")
    tiles = send.shape[0]
    levels, rows, across = eta.shape
    halves = rows // 8
    copies = []
    for h in range(halves):
        cut = pl.ds(8 * h, 8)
        for which, (src, dst) in enumerate(((eta, eta_v), (flow, flow_v))):
            copy = pltpu.make_async_copy(src.at[:, cut, :], dst.at[h], sems.at[2 * h + which])
            copy.start()
            copies.append(copy)

    classes = depth[...]
    speed = jnp.zeros(classes.shape, jnp.float32)
    for c in range(table.shape[0]):
        speed = jnp.where(classes == c, table[c], speed)
    cel[...] = speed

    lane = lax.broadcasted_iota(jnp.int32, (8, 128), 1)
    sub = lax.broadcasted_iota(jnp.int32, (8, 128), 0)
    inside = lane < levels
    fill = jnp.zeros((1, 128 - levels), jnp.float32)
    keep = jnp.broadcast_to(jnp.concatenate([damping[...], fill], axis=1), (8, 128))
    weight = jnp.broadcast_to(jnp.concatenate([profile[...], fill], axis=1), (8, 128))
    u = jnp.zeros((8, 128), jnp.float32)
    v = jnp.where(sub == 0, weight * (1.0 / math.sqrt(levels)), 0.0)
    us, vs = [u], [v]
    for r in range(STEPS):
        s = u + v
        bottom = jnp.sum(jnp.where(lane == levels - 1, s, 0.0), axis=1, keepdims=True)
        coef[8 * r : 8 * r + 8, :] = jnp.broadcast_to(bottom, (8, coef.shape[1]))
        vertical = pltpu.roll(s, 1, 1) + pltpu.roll(s, 127, 1) - 2.0 * s
        u = jnp.where(inside, u + VERT * vertical + pltpu.roll(s, 1, 0), 0.0)
        v = s * keep
        us.append(u)
        vs.append(v)

    wide = levels * 8
    spread = (
        lax.broadcasted_iota(jnp.int32, (128, wide), 1) // 8
        == lax.broadcasted_iota(jnp.int32, (128, wide), 0)
    ).astype(jnp.bfloat16)
    count_f = len(FIELDS) + 1
    diagonal = (
        lax.broadcasted_iota(jnp.int32, (8 * count_f, wide), 1) % 8
        == lax.broadcasted_iota(jnp.int32, (8 * count_f, wide), 0) % 8
    )

    def matrix(vectors):
        blocks = [jnp.broadcast_to(vectors[n][k : k + 1, :], (8, 128)) for n, k in FIELDS]
        blocks.append(jnp.zeros((8, 128), jnp.float32))
        hi, lo = split(jnp.concatenate(blocks, axis=0))
        zero = jnp.zeros((8 * count_f, wide), jnp.float32)
        hi = jnp.where(diagonal, dot(hi, spread), zero).astype(jnp.bfloat16)
        lo = jnp.where(diagonal, dot(lo, spread), zero).astype(jnp.bfloat16)
        return hi, jnp.concatenate([hi, lo], axis=0)

    w_eta, both_eta = matrix(us)
    w_flow, both_flow = matrix(vs)

    slots = residual.shape[2]
    slot = lax.broadcasted_iota(jnp.int32, (residual.shape[1], slots), 1)
    for o in range(tiles):
        send[o, 0:4, :] = jnp.zeros((4, across), jnp.float32)
        send[o, CEL_AT + CEL_HALO : ROWS, :] = jnp.zeros((ROWS - CEL_AT - CEL_HALO, across), jnp.float32)
    for o in range(tiles):
        live = jnp.where(slot < count[me, o], residual[o], 0.0)
        for d in range(3):
            target = o + 1 - d
            if 0 <= target < tiles:
                send[target, 0:4, 128 * d : 128 * d + slots] = live

    for h in range(halves):
        copies[2 * h].wait()
        hi, lo = split(eta_v[h].reshape(wide, across))
        total = dot(both_eta, hi)
        part = dot(w_eta, lo)
        copies[2 * h + 1].wait()
        hi, lo = split(flow_v[h].reshape(wide, across))
        total += dot(both_flow, hi)
        part += dot(w_flow, lo)
        part = part + total[: 8 * count_f] + total[8 * count_f :]
        for f in range(len(FIELDS)):
            fields[f, 8 * h : 8 * h + 8, :] = part[8 * f : 8 * f + 8]

    def edge(o, last):
        for f, width in enumerate(HALO):
            start = rows - width if last else 0
            send[o, HALO_AT[f] : HALO_AT[f] + width, :] = fields[f, start : start + width, :]
        start = rows - CEL_HALO if last else 0
        send[o, CEL_AT : CEL_AT + CEL_HALO, :] = cel[start : start + CEL_HALO, :]

    for o in range(tiles):
        @pl.when(o < me)
        def _():
            edge(o, False)

        @pl.when(o >= me)
        def _():
            edge(o, True)


def sensors_kernel(rows, cells, hot, place, buffer):
    me = lax.axis_index("trench")
    tiles = cells.shape[0]
    slots = cells.shape[2]
    across = hot.shape[0]
    per = 128 // slots
    buffer[...] = jnp.zeros(buffer.shape, jnp.int32)
    for d in range(3):
        owner = jnp.clip(me + d - 1, 0, tiles - 1)
        for s in range(tiles):
            buffer[d * tiles + s : d * tiles + s + 1, 0:slots] = cells[s, pl.ds(owner, 1), :]
    for d in range(3):
        for g in range(tiles // per):
            row = jnp.zeros((1, 128), jnp.int32)
            for p in range(per):
                at = d * tiles + g * per + p
                row = row + pltpu.roll(jnp.broadcast_to(buffer[at : at + 1, :], (8, 128)), slots * p, 1)[0:1]
            lanes = slice((d * (tiles // per) + g) * 128, (d * (tiles // per) + g + 1) * 128)
            place[:, lanes] = jnp.broadcast_to(row // across + (rows * (d - 1) + PAD), (8, 128))
            column = jnp.broadcast_to(row % across, (across, 128))
            hot[:, lanes] = jnp.where(
                column == lax.broadcasted_iota(jnp.int32, (across, 128), 0), 1.0, 0.0
            ).astype(jnp.bfloat16)


def advance_kernel(slots, fields, got, hot, place, cel, coef, out, ext, cel_ext):
    me = lax.axis_index("trench")
    tiles = got.shape[0]
    rows, across = cel.shape
    tall = rows + 2 * PAD
    blocks = out.shape[0]
    before = jnp.maximum(me - 1, 0)
    after = jnp.minimum(me + 1, tiles - 1)
    has_before = me > 0
    has_after = me < tiles - 1

    def extend(store, own, at, width):
        store(0, PAD, jnp.zeros((PAD, across), jnp.float32))
        store(PAD + rows, tall, jnp.zeros((PAD, across), jnp.float32))
        store(PAD, PAD + rows, own)
        store(PAD - width, PAD, jnp.where(has_before, got[before, at : at + width, :], 0.0))
        store(PAD + rows, PAD + rows + width, jnp.where(has_after, got[after, at : at + width, :], 0.0))

    for f, width in enumerate(HALO):
        def store(a, b, value, f=f):
            ext[f, a:b, :] = value
        extend(store, fields[f], HALO_AT[f], width)

    def store_cel(a, b, value):
        cel_ext[a:b, :] = value
    extend(store_cel, cel[...], CEL_AT, CEL_HALO)

    per = 128 // slots
    groups = tiles // per
    parts = []
    for d in range(3):
        for g in range(groups):
            value = jnp.zeros((4, 128), jnp.float32)
            for p in range(per):
                block = got[g * per + p, 0:4, 128 * d : 128 * d + 128]
                value = value + (pltpu.roll(block, slots * p, 1) if p else block)
            if d == 0:
                value = jnp.where(has_before, value, 0.0)
            if d == 2:
                value = jnp.where(has_after, value, 0.0)
            parts.append(value)
    values = jnp.concatenate(parts, axis=1)
    lanes = values.shape[1]
    here = lax.broadcasted_iota(jnp.int32, (tall, lanes), 0) == jnp.broadcast_to(place[0:1, :], (tall, lanes))
    left = jnp.concatenate(
        [jnp.where(here, jnp.broadcast_to(values[t : t + 1, :], (tall, lanes)), 0.0) for t in range(STEPS)], axis=0
    )
    hi, lo = split(left)
    planes = dot(hi, hot[...], ((1,), (1,))) + dot(lo, hot[...], ((1,), (1,)))
    inject = [planes[tall * t : tall * t + tall] for t in range(STEPS)]

    lane = lax.broadcasted_iota(jnp.int32, (tall, across), 1)
    first = lane == 0
    last = lane == across - 1
    speed = cel_ext[...]

    def horizontal(z):
        around = pltpu.roll(z, 1, 0) + pltpu.roll(z, tall - 1, 0)
        around += jnp.where(first, 0.0, pltpu.roll(z, 1, 1))
        around += jnp.where(last, 0.0, pltpu.roll(z, across - 1, 1))
        return speed * (around - 4.0 * z)

    def injected(n, k, a, b):
        total = None
        for tau in range(1, n - k + 1):
            r = n - tau
            term = coef[8 * r + k : 8 * r + k + 1, :] * inject[STEPS - tau][a:b]
            total = term if total is None else total + term
        return total

    base = horizontal(ext[0])
    for n in range(1, STEPS + 1):
        z = base
        for k in range(n - 1, 0, -1):
            z = horizontal(z + ext[FIELDS.index((n, k))] + injected(n, k, 0, tall))
        own = z[PAD : PAD + rows] + fields[FIELDS.index((n, 0))] + injected(n, 0, PAD, PAD + rows)
        t = STEPS - n
        part = rows // blocks
        for b in range(blocks):
            out[b, part * t : part * t + part, :] = own[part * b : part * b + part]


def prior_kernel(got, weight, out):
    windows = got.shape[0]
    part = out.shape[1]
    length = out.shape[0]
    series = [got[i // STEPS, part * (i % STEPS) : part * (i % STEPS) + part, :] for i in range(length)]
    for k in range(length):
        total = weight[0] * series[k]
        for j in range(1, min(weight.shape[0], length - k)):
            total += weight[j] * series[k + j]
        out[k] = total


def shape(*dims, dtype=jnp.float32):
    return jax.ShapeDtypeStruct(dims, dtype)


def spec(space):
    return pl.BlockSpec(memory_space=space)


def body(
    adjoint_eta,
    adjoint_flow,
    residual,
    sensor_cell,
    sensor_count,
    depth_class,
    speed_table,
    damping,
    profile,
    band_weight,
):
    tiles = lax.axis_size("trench")
    blocks = lax.axis_size("tblock")
    levels, rows, across = adjoint_eta.shape[1:]
    slots = residual.shape[-1]
    lanes = 3 * tiles * slots
    params = pltpu.CompilerParams(vmem_limit_bytes=LIMIT)

    fields, send, cel, coef = pl.pallas_call(
        contract_kernel,
        out_shape=(
            shape(len(FIELDS), rows, across),
            shape(tiles, ROWS, across),
            shape(rows, across),
            shape(8 * STEPS, across),
        ),
        in_specs=[spec(pl.ANY), spec(pl.ANY), spec(VMEM), spec(SMEM), spec(VMEM), spec(SMEM), spec(VMEM), spec(VMEM)],
        out_specs=(spec(VMEM),) * 4,
        scratch_shapes=[
            VMEM((rows // 8, levels, 8, across), jnp.float32),
            VMEM((rows // 8, levels, 8, across), jnp.float32),
            pltpu.SemaphoreType.DMA((2 * (rows // 8),)),
        ],
        compiler_params=params,
        name="contract",
    )(
        adjoint_eta[0], adjoint_flow[0], residual[0, 0], sensor_count, depth_class, speed_table,
        damping[None], profile[None],
    )
    got = lax.all_to_all(send, "trench", split_axis=0, concat_axis=0, tiled=True)
    hot, place = pl.pallas_call(
        functools.partial(sensors_kernel, rows),
        out_shape=(shape(across, lanes, dtype=jnp.bfloat16), shape(8, lanes, dtype=jnp.int32)),
        in_specs=[spec(VMEM)],
        out_specs=(spec(VMEM),) * 2,
        scratch_shapes=[VMEM((3 * tiles, 128), jnp.int32)],
        compiler_params=params,
        name="sensors",
    )(sensor_cell)
    series = pl.pallas_call(
        functools.partial(advance_kernel, slots),
        out_shape=shape(blocks, STEPS * rows // blocks, across),
        in_specs=[spec(VMEM)] * 6,
        out_specs=spec(VMEM),
        scratch_shapes=[
            VMEM((len(HALO), rows + 2 * PAD, across), jnp.float32),
            VMEM((rows + 2 * PAD, across), jnp.float32),
        ],
        compiler_params=params,
        name="advance",
    )(fields, got, hot, place, cel, coef)
    whole = lax.all_to_all(series, "tblock", split_axis=0, concat_axis=0, tiled=True)
    return pl.pallas_call(
        prior_kernel,
        out_shape=shape(STEPS * blocks, rows // blocks, across),
        in_specs=[spec(VMEM), spec(SMEM)],
        out_specs=spec(VMEM),
        compiler_params=params,
        name="prior",
    )(whole, band_weight)


def solution(mesh):
    in_specs = (
        P("tblock", None, "trench", None),
        P("tblock", None, "trench", None),
        P("tblock", "trench", None, None, None),
        P(),
        P(),
        P("trench", None),
        P(),
        P(),
        P(),
        P(),
    )
    out_specs = P(None, ("trench", "tblock"), None)
    return jax.shard_map(body, mesh=mesh, in_specs=in_specs, out_specs=out_specs, check_vma=False)
```

```python
import functools
import math

import jax
import jax.numpy as jnp
from jax import lax
from jax.experimental import pallas as pl
from jax.experimental.pallas import tpu as pltpu
from jax.sharding import PartitionSpec as P

VERT = 0.2
STEPS = 4
PAD = 8
VMEM = pltpu.VMEM
SMEM = pltpu.SMEM
LIMIT = 32 * 1024 * 1024
LIMIT_CONTRACT = 63_000_000

SHIFT = 1.2

FIELDS = [(4, 4), (4, 3), (4, 2), (3, 2), (4, 1), (3, 1), (2, 1), (4, 0), (3, 0), (2, 0), (1, 0)]
HALO = [4, 3, 2, 2, 1, 1, 1]
HALO_AT = [0, 4, 7, 9, 11, 12, 13]
CEL_AT = 14
CEL_HALO = 3
ROWS = 17


def split(x):
    hi = x.astype(jnp.bfloat16)
    return hi, (x - hi.astype(jnp.float32)).astype(jnp.bfloat16)


def dot(a, b, dims=((1,), (0,))):
    return lax.dot_general(a, b, (dims, ((), ())), preferred_element_type=jnp.float32)


def contract_kernel(
    eta, flow, depth, table, damping, profile,
    fields, send_even, send_odd, cel, coef,
    eta_v, flow_v, depth_v, table_s, damping_v, profile_v, sems,
):
    levels, rows, across = eta.shape[1:]
    halves = rows // 8
    copies = []

    def fetch(src, dst):
        copy = pltpu.make_async_copy(src, dst, sems.at[len(copies)])
        copy.start()
        copies.append(copy)
        return copy

    small = [fetch(damping, damping_v), fetch(profile, profile_v), fetch(table, table_s), fetch(depth, depth_v)]
    large = []
    for h in range(halves):
        cut = pl.ds(8 * h, 8)
        large.append(fetch(eta.at[0, :, cut, :], eta_v.at[h]))
        large.append(fetch(flow.at[0, :, cut, :], flow_v.at[h]))
    for copy in small:
        copy.wait()

    classes = depth_v[...]
    speed = jnp.zeros(classes.shape, jnp.float32)
    for c in range(table_s.shape[0]):
        speed = jnp.where(classes == c, table_s[c], speed)
    cel[...] = speed

    lane = lax.broadcasted_iota(jnp.int32, (8, 128), 1)
    sub = lax.broadcasted_iota(jnp.int32, (8, 128), 0)
    inside = lane < levels
    fill = jnp.zeros((1, 128 - levels), jnp.float32)
    keep = jnp.broadcast_to(jnp.concatenate([damping_v[...], fill], axis=1), (8, 128))
    weight = jnp.broadcast_to(jnp.concatenate([profile_v[...], fill], axis=1), (8, 128))
    u = jnp.zeros((8, 128), jnp.float32)
    v = jnp.where(sub == 0, weight * (1.0 / math.sqrt(levels)), 0.0)
    us, vs = [u], [v]
    for r in range(STEPS):
        s = u + v
        bottom = jnp.sum(jnp.where(lane == levels - 1, s, 0.0), axis=1, keepdims=True)
        coef[8 * r : 8 * r + 8, :] = jnp.broadcast_to(bottom, (8, coef.shape[1]))
        vertical = pltpu.roll(s, 1, 1) + pltpu.roll(s, 127, 1) - 2.0 * s
        u = jnp.where(inside, u + VERT * vertical - SHIFT * s + pltpu.roll(s, 1, 0), 0.0)
        v = s * keep
        us.append(u)
        vs.append(v)

    wide = levels * 8
    spread = (
        lax.broadcasted_iota(jnp.int32, (128, wide), 1) // 8
        == lax.broadcasted_iota(jnp.int32, (128, wide), 0)
    ).astype(jnp.bfloat16)
    count_f = len(FIELDS) + 1
    diagonal = (
        lax.broadcasted_iota(jnp.int32, (8 * count_f, wide), 1) % 8
        == lax.broadcasted_iota(jnp.int32, (8 * count_f, wide), 0) % 8
    )

    def matrix(vectors):
        blocks = [jnp.broadcast_to(vectors[n][k : k + 1, :], (8, 128)) for n, k in FIELDS]
        blocks.append(jnp.zeros((8, 128), jnp.float32))
        hi, lo = split(jnp.concatenate(blocks, axis=0))
        zero = jnp.zeros((8 * count_f, wide), jnp.float32)
        hi = jnp.where(diagonal, dot(hi, spread), zero).astype(jnp.bfloat16)
        lo = jnp.where(diagonal, dot(lo, spread), zero).astype(jnp.bfloat16)
        return hi, jnp.concatenate([hi, lo], axis=0)

    w_eta, both_eta = matrix(us)
    w_flow, both_flow = matrix(vs)

    for h in range(halves):
        large[2 * h].wait()
        hi, lo = split(eta_v[h].reshape(wide, across))
        total = dot(both_eta, hi)
        part = dot(w_eta, lo)
        large[2 * h + 1].wait()
        hi, lo = split(flow_v[h].reshape(wide, across))
        total += dot(both_flow, hi)
        part += dot(w_flow, lo)
        part = part + total[: 8 * count_f] + total[8 * count_f :]
        for f in range(len(FIELDS)):
            fields[f, 8 * h : 8 * h + 8, :] = part[8 * f : 8 * f + 8]

    def edge(send, last):
        for f, width in enumerate(HALO):
            start = rows - width if last else 0
            send[HALO_AT[f] : HALO_AT[f] + width, :] = fields[f, start : start + width, :]
        start = rows - CEL_HALO if last else 0
        send[CEL_AT : CEL_AT + CEL_HALO, :] = cel[start : start + CEL_HALO, :]

    odd = lax.axis_index("trench") % 2

    @pl.when(odd == 0)
    def _():
        edge(send_even, True)
        edge(send_odd, False)

    @pl.when(odd == 1)
    def _():
        edge(send_even, False)
        edge(send_odd, True)


def sensors_kernel(rows, residual, cells, count, planes):
    me = lax.axis_index("trench")
    tiles, _, steps, slots = residual.shape
    across = planes.shape[1]
    tall = rows + 2 * PAD
    slot = lax.broadcasted_iota(jnp.int32, (steps, slots), 1)
    values, places, columns = [], [], []
    for d in range(3):
        owner = me + d - 1
        inside = (owner >= 0) & (owner < tiles)
        owner = jnp.clip(owner, 0, tiles - 1)
        for s in range(tiles):
            live = jnp.where(inside, count[s, owner], 0)
            values.append(jnp.where(slot < live, residual[s, owner], 0.0))
            cell = cells[s, pl.ds(owner, 1), :]
            places.append(cell // across + (rows * (d - 1) + PAD))
            columns.append(cell % across)
    values = jnp.concatenate(values, axis=1)
    places = jnp.concatenate(places, axis=1)
    columns = jnp.concatenate(columns, axis=1)
    lanes = values.shape[1]
    here = lax.broadcasted_iota(jnp.int32, (tall, lanes), 0) == places
    left = jnp.concatenate([jnp.where(here, values[t : t + 1, :], 0.0) for t in range(steps)], axis=0)
    hot = jnp.where(lax.broadcasted_iota(jnp.int32, (across, lanes), 0) == columns, 1.0, 0.0).astype(jnp.bfloat16)
    hi, lo = split(left)
    planes[...] = dot(hi, hot, ((1,), (1,))) + dot(lo, hot, ((1,), (1,)))


def advance_kernel(fields, got_even, got_odd, planes, cel, coef, *refs):
    outs, (stage, ext, cel_ext) = refs[:-3], refs[-3:]
    rows, across = cel.shape
    tall = rows + 2 * PAD
    part = rows // len(outs)
    odd = lax.axis_index("trench") % 2 == 1
    before = jnp.where(odd, got_even[...], got_odd[...])
    after = jnp.where(odd, got_odd[...], got_even[...])

    def extend(store, own, at, width):
        store(0, PAD, jnp.zeros((PAD, across), jnp.float32))
        store(PAD + rows, tall, jnp.zeros((PAD, across), jnp.float32))
        store(PAD, PAD + rows, own)
        store(PAD - width, PAD, before[at : at + width])
        store(PAD + rows, PAD + rows + width, after[at : at + width])

    for f, width in enumerate(HALO):
        def store(a, b, value, f=f):
            ext[f, a:b, :] = value
        extend(store, fields[f], HALO_AT[f], width)

    def store_cel(a, b, value):
        cel_ext[a:b, :] = value
    extend(store_cel, cel[...], CEL_AT, CEL_HALO)

    inject = [planes[tall * t : tall * t + tall, :] for t in range(STEPS)]

    lane = lax.broadcasted_iota(jnp.int32, (tall, across), 1)
    first = lane == 0
    last = lane == across - 1
    speed = cel_ext[...]

    def horizontal(z):
        around = pltpu.roll(z, 1, 0) + pltpu.roll(z, tall - 1, 0)
        around += jnp.where(first, 0.0, pltpu.roll(z, 1, 1))
        around += jnp.where(last, 0.0, pltpu.roll(z, across - 1, 1))
        return speed * (around - 4.0 * z) + SHIFT * z

    def injected(n, k, a, b):
        total = None
        for tau in range(1, n - k + 1):
            r = n - tau
            term = coef[8 * r + k : 8 * r + k + 1, :] * inject[STEPS - tau][a:b]
            total = term if total is None else total + term
        return total

    base = horizontal(ext[0])
    for n in range(1, STEPS + 1):
        z = base
        for k in range(n - 1, 0, -1):
            z = horizontal(z + ext[FIELDS.index((n, k))] + injected(n, k, 0, tall))
        own = z[PAD : PAD + rows] + fields[FIELDS.index((n, 0))] + injected(n, 0, PAD, PAD + rows)
        t = STEPS - n
        for b in range(len(outs)):
            stage[b, part * t : part * t + part, :] = own[part * b : part * b + part]
    block = lax.axis_index("tblock")
    for r, out in enumerate(outs):
        out[...] = stage[block ^ r]


def prior_kernel(*refs):
    gots, weight, out, whole = refs[:-3], refs[-3], refs[-2], refs[-1]
    block = lax.axis_index("tblock")
    for r, got in enumerate(gots):
        whole[block ^ r] = got[...]
    part = out.shape[1]
    length = out.shape[0]
    series = [whole[i // STEPS, part * (i % STEPS) : part * (i % STEPS) + part, :] for i in range(length)]
    for k in range(length):
        total = weight[0] * series[k]
        for j in range(1, min(weight.shape[0], length - k)):
            total += weight[j] * series[k + j]
        out[k] = total


def shape(*dims, dtype=jnp.float32):
    return jax.ShapeDtypeStruct(dims, dtype)


def spec(space):
    return pl.BlockSpec(memory_space=space)


def body(
    adjoint_eta,
    adjoint_flow,
    residual,
    sensor_cell,
    sensor_count,
    depth_class,
    speed_table,
    damping,
    profile,
    band_weight,
):
    tiles = lax.axis_size("trench")
    blocks = lax.axis_size("tblock")
    levels, rows, across = adjoint_eta.shape[1:]
    tall = rows + 2 * PAD
    params = pltpu.CompilerParams(vmem_limit_bytes=LIMIT)

    rows_of_all = lax.all_gather(residual[0, 0], "trench", axis=0)
    fields, send_even, send_odd, cel, coef = pl.pallas_call(
        contract_kernel,
        out_shape=(
            shape(len(FIELDS), rows, across),
            shape(ROWS, across),
            shape(ROWS, across),
            shape(rows, across),
            shape(8 * STEPS, across),
        ),
        in_specs=[spec(pltpu.HBM)] * 6,
        out_specs=(spec(VMEM),) * 5,
        scratch_shapes=[
            VMEM((rows // 8, levels, 8, across), jnp.float32),
            VMEM((rows // 8, levels, 8, across), jnp.float32),
            VMEM((rows, across), jnp.int32),
            SMEM(speed_table.shape, jnp.float32),
            VMEM((1, levels), jnp.float32),
            VMEM((1, levels), jnp.float32),
            pltpu.SemaphoreType.DMA((4 + 2 * (rows // 8),)),
        ],
        compiler_params=pltpu.CompilerParams(vmem_limit_bytes=LIMIT_CONTRACT),
        name="contract",
    )(adjoint_eta, adjoint_flow, depth_class, speed_table, damping[None], profile[None])

    def swap(x, axis, pairs):
        return lax.ppermute(x, axis, pairs + [(j, i) for i, j in pairs])

    got_even = swap(send_even, "trench", [(i, i + 1) for i in range(0, tiles - 1, 2)])
    got_odd = swap(send_odd, "trench", [(i, i + 1) for i in range(1, tiles - 1, 2)])
    planes = pl.pallas_call(
        functools.partial(sensors_kernel, rows),
        out_shape=shape(STEPS * tall, across),
        in_specs=[spec(VMEM), spec(VMEM), spec(SMEM)],
        out_specs=spec(VMEM),
        compiler_params=params,
        name="sensors",
    )(rows_of_all, sensor_cell, sensor_count)
    series = pl.pallas_call(
        advance_kernel,
        out_shape=(shape(STEPS * rows // blocks, across),) * blocks,
        in_specs=[spec(VMEM)] * 6,
        out_specs=(spec(VMEM),) * blocks,
        scratch_shapes=[
            VMEM((blocks, STEPS * rows // blocks, across), jnp.float32),
            VMEM((len(HALO), tall, across), jnp.float32),
            VMEM((tall, across), jnp.float32),
        ],
        compiler_params=params,
        name="advance",
    )(fields, got_even, got_odd, planes, cel, coef)
    gots = [series[0]]
    for r in range(1, blocks):
        gots.append(lax.ppermute(series[r], "tblock", [(i, i ^ r) for i in range(blocks)]))
    return pl.pallas_call(
        prior_kernel,
        out_shape=shape(STEPS * blocks, rows // blocks, across),
        in_specs=[spec(VMEM)] * blocks + [spec(SMEM)],
        out_specs=spec(VMEM),
        scratch_shapes=[VMEM((blocks, STEPS * rows // blocks, across), jnp.float32)],
        compiler_params=params,
        name="prior",
    )(*gots, band_weight)


def solution(mesh):
    in_specs = (
        P("tblock", None, "trench", None),
        P("tblock", None, "trench", None),
        P("tblock", "trench", None, None, None),
        P(),
        P(),
        P("trench", None),
        P(),
        P(),
        P(),
        P(),
    )
    out_specs = P(None, ("trench", "tblock"), None)
    return jax.shard_map(body, mesh=mesh, in_specs=in_specs, out_specs=out_specs, check_vma=False)
```

```python
import functools
import math

import jax
import jax.numpy as jnp
from jax import lax
from jax.experimental import pallas as pl
from jax.experimental.pallas import tpu as pltpu
from jax.sharding import PartitionSpec as P

VERT = 0.2
STEPS = 4
PAD = 8
VMEM = pltpu.VMEM
SMEM = pltpu.SMEM
LIMIT = 32 * 1024 * 1024
LIMIT_CONTRACT = 63_000_000

SHIFT = 1.2

FIELDS = [(4, 4), (4, 3), (4, 2), (3, 2), (4, 1), (3, 1), (2, 1), (4, 0), (3, 0), (2, 0), (1, 0)]
HALO = [4, 3, 2, 2, 1, 1, 1]
HALO_AT = [0, 4, 7, 9, 11, 12, 13]
CEL_AT = 14
CEL_HALO = 3
ROWS = 17


def split(x):
    hi = x.astype(jnp.bfloat16)
    return hi, (x - hi.astype(jnp.float32)).astype(jnp.bfloat16)


def dot(a, b, dims=((1,), (0,))):
    return lax.dot_general(a, b, (dims, ((), ())), preferred_element_type=jnp.float32)


def contract_kernel(
    eta, flow, depth, table, damping, profile,
    fields, send_even, send_odd, cel, coef,
    eta_v, flow_v, depth_v, table_s, damping_v, profile_v, sems,
):
    levels, rows, across = eta.shape[1:]
    halves = rows // 8
    copies = []

    def fetch(src, dst):
        copy = pltpu.make_async_copy(src, dst, sems.at[len(copies)])
        copy.start()
        copies.append(copy)
        return copy

    small = [fetch(damping, damping_v), fetch(profile, profile_v), fetch(table, table_s), fetch(depth, depth_v)]
    large = []
    for h in range(halves):
        cut = pl.ds(8 * h, 8)
        large.append(fetch(eta.at[0, :, cut, :], eta_v.at[h]))
        large.append(fetch(flow.at[0, :, cut, :], flow_v.at[h]))
    for copy in small:
        copy.wait()

    classes = depth_v[...]
    speed = jnp.zeros(classes.shape, jnp.float32)
    for c in range(table_s.shape[0]):
        speed = jnp.where(classes == c, table_s[c], speed)
    cel[...] = speed

    lane = lax.broadcasted_iota(jnp.int32, (8, 128), 1)
    sub = lax.broadcasted_iota(jnp.int32, (8, 128), 0)
    inside = lane < levels
    fill = jnp.zeros((1, 128 - levels), jnp.float32)
    keep = jnp.broadcast_to(jnp.concatenate([damping_v[...], fill], axis=1), (8, 128))
    weight = jnp.broadcast_to(jnp.concatenate([profile_v[...], fill], axis=1), (8, 128))
    u = jnp.zeros((8, 128), jnp.float32)
    v = jnp.where(sub == 0, weight * (1.0 / math.sqrt(levels)), 0.0)
    us, vs = [u], [v]
    for r in range(STEPS):
        s = u + v
        bottom = jnp.sum(jnp.where(lane == levels - 1, s, 0.0), axis=1, keepdims=True)
        coef[8 * r : 8 * r + 8, :] = jnp.broadcast_to(bottom, (8, coef.shape[1]))
        vertical = pltpu.roll(s, 1, 1) + pltpu.roll(s, 127, 1) - 2.0 * s
        u = jnp.where(inside, u + VERT * vertical - SHIFT * s + pltpu.roll(s, 1, 0), 0.0)
        v = s * keep
        us.append(u)
        vs.append(v)

    wide = levels * 8
    spread = (
        lax.broadcasted_iota(jnp.int32, (128, wide), 1) // 8
        == lax.broadcasted_iota(jnp.int32, (128, wide), 0)
    ).astype(jnp.bfloat16)
    count_f = len(FIELDS) + 1
    diagonal = (
        lax.broadcasted_iota(jnp.int32, (8 * count_f, wide), 1) % 8
        == lax.broadcasted_iota(jnp.int32, (8 * count_f, wide), 0) % 8
    )

    def matrix(vectors):
        blocks = [jnp.broadcast_to(vectors[n][k : k + 1, :], (8, 128)) for n, k in FIELDS]
        blocks.append(jnp.zeros((8, 128), jnp.float32))
        hi, lo = split(jnp.concatenate(blocks, axis=0))
        zero = jnp.zeros((8 * count_f, wide), jnp.float32)
        hi = jnp.where(diagonal, dot(hi, spread), zero).astype(jnp.bfloat16)
        lo = jnp.where(diagonal, dot(lo, spread), zero).astype(jnp.bfloat16)
        return hi, jnp.concatenate([hi, lo], axis=0)

    w_eta, both_eta = matrix(us)
    w_flow, both_flow = matrix(vs)

    for h in range(halves):
        large[2 * h].wait()
        hi, lo = split(eta_v[h].reshape(wide, across))
        total = dot(both_eta, hi)
        part = dot(w_eta, lo)
        large[2 * h + 1].wait()
        hi, lo = split(flow_v[h].reshape(wide, across))
        total += dot(both_flow, hi)
        part += dot(w_flow, lo)
        part = part + total[: 8 * count_f] + total[8 * count_f :]
        for f in range(len(FIELDS)):
            fields[f, 8 * h : 8 * h + 8, :] = part[8 * f : 8 * f + 8]

    def edge(send, last):
        for f, width in enumerate(HALO):
            start = rows - width if last else 0
            send[HALO_AT[f] : HALO_AT[f] + width, :] = fields[f, start : start + width, :]
        start = rows - CEL_HALO if last else 0
        send[CEL_AT : CEL_AT + CEL_HALO, :] = cel[start : start + CEL_HALO, :]

    odd = lax.axis_index("trench") % 2

    @pl.when(odd == 0)
    def _():
        edge(send_even, True)
        edge(send_odd, False)

    @pl.when(odd == 1)
    def _():
        edge(send_even, False)
        edge(send_odd, True)


def sensors_kernel(rows, *refs):
    gots, (cells, count, planes) = refs[:-3], refs[-3:]
    me = lax.axis_index("trench")
    tiles, steps, slots = gots[0].shape
    across = planes.shape[1]
    tall = rows + 2 * PAD
    slot = lax.broadcasted_iota(jnp.int32, (steps, slots), 1)
    values, places, columns = [], [], []
    for d in range(3):
        owner = me + d - 1
        inside = (owner >= 0) & (owner < tiles)
        owner = jnp.clip(owner, 0, tiles - 1)
        for r, got in enumerate(gots):
            s = me ^ r
            live = jnp.where(inside, count[s, owner], 0)
            values.append(jnp.where(slot < live, got[owner], 0.0))
            cell = cells[s, pl.ds(owner, 1), :]
            places.append(cell // across + (rows * (d - 1) + PAD))
            columns.append(cell % across)
    values = jnp.concatenate(values, axis=1)
    places = jnp.concatenate(places, axis=1)
    columns = jnp.concatenate(columns, axis=1)
    lanes = values.shape[1]
    here = lax.broadcasted_iota(jnp.int32, (tall, lanes), 0) == places
    left = jnp.concatenate([jnp.where(here, values[t : t + 1, :], 0.0) for t in range(steps)], axis=0)
    hot = jnp.where(lax.broadcasted_iota(jnp.int32, (across, lanes), 0) == columns, 1.0, 0.0).astype(jnp.bfloat16)
    hi, lo = split(left)
    planes[...] = dot(hi, hot, ((1,), (1,))) + dot(lo, hot, ((1,), (1,)))


def advance_kernel(fields, got_even, got_odd, planes, cel, coef, *refs):
    outs, (stage, ext, cel_ext) = refs[:-3], refs[-3:]
    rows, across = cel.shape
    tall = rows + 2 * PAD
    part = rows // len(outs)
    odd = lax.axis_index("trench") % 2 == 1
    before = jnp.where(odd, got_even[...], got_odd[...])
    after = jnp.where(odd, got_odd[...], got_even[...])

    def extend(store, own, at, width):
        store(0, PAD, jnp.zeros((PAD, across), jnp.float32))
        store(PAD + rows, tall, jnp.zeros((PAD, across), jnp.float32))
        store(PAD, PAD + rows, own)
        store(PAD - width, PAD, before[at : at + width])
        store(PAD + rows, PAD + rows + width, after[at : at + width])

    for f, width in enumerate(HALO):
        def store(a, b, value, f=f):
            ext[f, a:b, :] = value
        extend(store, fields[f], HALO_AT[f], width)

    def store_cel(a, b, value):
        cel_ext[a:b, :] = value
    extend(store_cel, cel[...], CEL_AT, CEL_HALO)

    inject = [planes[tall * t : tall * t + tall, :] for t in range(STEPS)]

    lane = lax.broadcasted_iota(jnp.int32, (tall, across), 1)
    first = lane == 0
    last = lane == across - 1
    speed = cel_ext[...]

    def horizontal(z):
        around = pltpu.roll(z, 1, 0) + pltpu.roll(z, tall - 1, 0)
        around += jnp.where(first, 0.0, pltpu.roll(z, 1, 1))
        around += jnp.where(last, 0.0, pltpu.roll(z, across - 1, 1))
        return speed * (around - 4.0 * z) + SHIFT * z

    def injected(n, k, a, b):
        total = None
        for tau in range(1, n - k + 1):
            r = n - tau
            term = coef[8 * r + k : 8 * r + k + 1, :] * inject[STEPS - tau][a:b]
            total = term if total is None else total + term
        return total

    base = horizontal(ext[0])
    for n in range(1, STEPS + 1):
        z = base
        for k in range(n - 1, 0, -1):
            z = horizontal(z + ext[FIELDS.index((n, k))] + injected(n, k, 0, tall))
        own = z[PAD : PAD + rows] + fields[FIELDS.index((n, 0))] + injected(n, 0, PAD, PAD + rows)
        t = STEPS - n
        for b in range(len(outs)):
            stage[b, part * t : part * t + part, :] = own[part * b : part * b + part]
    block = lax.axis_index("tblock")
    for r, out in enumerate(outs):
        out[...] = stage[block ^ r]


def prior_kernel(*refs):
    gots, weight, out, whole = refs[:-3], refs[-3], refs[-2], refs[-1]
    block = lax.axis_index("tblock")
    for r, got in enumerate(gots):
        whole[block ^ r] = got[...]
    part = out.shape[1]
    length = out.shape[0]
    series = [whole[i // STEPS, part * (i % STEPS) : part * (i % STEPS) + part, :] for i in range(length)]
    for k in range(length):
        total = weight[0] * series[k]
        for j in range(1, min(weight.shape[0], length - k)):
            total += weight[j] * series[k + j]
        out[k] = total


def shape(*dims, dtype=jnp.float32):
    return jax.ShapeDtypeStruct(dims, dtype)


def spec(space):
    return pl.BlockSpec(memory_space=space)


def body(
    adjoint_eta,
    adjoint_flow,
    residual,
    sensor_cell,
    sensor_count,
    depth_class,
    speed_table,
    damping,
    profile,
    band_weight,
):
    tiles = lax.axis_size("trench")
    blocks = lax.axis_size("tblock")
    levels, rows, across = adjoint_eta.shape[1:]
    tall = rows + 2 * PAD
    params = pltpu.CompilerParams(vmem_limit_bytes=LIMIT)

    def swaps(parts, axis):
        devices = lax.axis_size(axis)
        moved = [lax.ppermute(parts[r], axis, [(i, i ^ r) for i in range(devices)]) for r in range(1, devices)]
        return [parts[0]] + moved

    residuals = swaps([residual[0, 0]] * tiles, "trench")
    fields, send_even, send_odd, cel, coef = pl.pallas_call(
        contract_kernel,
        out_shape=(
            shape(len(FIELDS), rows, across),
            shape(ROWS, across),
            shape(ROWS, across),
            shape(rows, across),
            shape(8 * STEPS, across),
        ),
        in_specs=[spec(pltpu.HBM)] * 6,
        out_specs=(spec(VMEM),) * 5,
        scratch_shapes=[
            VMEM((rows // 8, levels, 8, across), jnp.float32),
            VMEM((rows // 8, levels, 8, across), jnp.float32),
            VMEM((rows, across), jnp.int32),
            SMEM(speed_table.shape, jnp.float32),
            VMEM((1, levels), jnp.float32),
            VMEM((1, levels), jnp.float32),
            pltpu.SemaphoreType.DMA((4 + 2 * (rows // 8),)),
        ],
        compiler_params=pltpu.CompilerParams(vmem_limit_bytes=LIMIT_CONTRACT),
        cost_estimate=pl.CostEstimate(flops=10**9, bytes_accessed=10**7, transcendentals=0),
        name="contract",
    )(adjoint_eta, adjoint_flow, depth_class, speed_table, damping[None], profile[None])

    def swap(x, axis, pairs):
        return lax.ppermute(x, axis, pairs + [(j, i) for i, j in pairs])

    got_even = swap(send_even, "trench", [(i, i + 1) for i in range(0, tiles - 1, 2)])
    got_odd = swap(send_odd, "trench", [(i, i + 1) for i in range(1, tiles - 1, 2)])
    planes = pl.pallas_call(
        functools.partial(sensors_kernel, rows),
        out_shape=shape(STEPS * tall, across),
        in_specs=[spec(VMEM)] * (tiles + 1) + [spec(SMEM)],
        out_specs=spec(VMEM),
        compiler_params=params,
        cost_estimate=pl.CostEstimate(flops=10**8, bytes_accessed=4 * 10**6, transcendentals=0),
        name="sensors",
    )(*residuals, sensor_cell, sensor_count)
    series = pl.pallas_call(
        advance_kernel,
        out_shape=(shape(STEPS * rows // blocks, across),) * blocks,
        in_specs=[spec(VMEM)] * 6,
        out_specs=(spec(VMEM),) * blocks,
        scratch_shapes=[
            VMEM((blocks, STEPS * rows // blocks, across), jnp.float32),
            VMEM((len(HALO), tall, across), jnp.float32),
            VMEM((tall, across), jnp.float32),
        ],
        compiler_params=params,
        name="advance",
    )(fields, got_even, got_odd, planes, cel, coef)
    gots = swaps(series, "tblock")
    return pl.pallas_call(
        prior_kernel,
        out_shape=shape(STEPS * blocks, rows // blocks, across),
        in_specs=[spec(VMEM)] * blocks + [spec(SMEM)],
        out_specs=spec(VMEM),
        scratch_shapes=[VMEM((blocks, STEPS * rows // blocks, across), jnp.float32)],
        compiler_params=params,
        name="prior",
    )(*gots, band_weight)


def solution(mesh):
    in_specs = (
        P("tblock", None, "trench", None),
        P("tblock", None, "trench", None),
        P("tblock", "trench", None, None, None),
        P(),
        P(),
        P("trench", None),
        P(),
        P(),
        P(),
        P(),
    )
    out_specs = P(None, ("trench", "tblock"), None)
    return jax.shard_map(body, mesh=mesh, in_specs=in_specs, out_specs=out_specs, check_vma=False)
```

```python
import functools
import math

import jax
import jax.numpy as jnp
from jax import lax
from jax.experimental import pallas as pl
from jax.experimental.pallas import tpu as pltpu
from jax.sharding import PartitionSpec as P

VERT = 0.2
STEPS = 4
PAD = 8
VMEM = pltpu.VMEM
SMEM = pltpu.SMEM
LIMIT = 32 * 1024 * 1024
LIMIT_CONTRACT = 63_000_000

SHIFT = 1.2

FIELDS = [(4, 4), (4, 3), (4, 2), (3, 2), (4, 1), (3, 1), (2, 1), (4, 0), (3, 0), (2, 0), (1, 0)]
HALO = [4, 3, 2, 2, 1, 1, 1]
HALO_AT = [0, 4, 7, 9, 11, 12, 13]
CEL_AT = 14
CEL_HALO = 3
ROWS = 17


def split(x):
    hi = x.astype(jnp.bfloat16)
    return hi, (x - hi.astype(jnp.float32)).astype(jnp.bfloat16)


def dot(a, b, dims=((1,), (0,))):
    return lax.dot_general(a, b, (dims, ((), ())), preferred_element_type=jnp.float32)


def contract_kernel(
    eta, flow, depth, table, damping, profile, cells, count,
    fields, edges, cel, coef, hot, places,
    eta_v, flow_v, depth_v, table_s, damping_v, profile_v, cells_v, count_s, sems,
):
    levels, rows, across = eta.shape[1:]
    halves = rows // 8
    copies = []

    def fetch(src, dst):
        copy = pltpu.make_async_copy(src, dst, sems.at[len(copies)])
        copy.start()
        copies.append(copy)
        return copy

    small = [fetch(damping, damping_v), fetch(profile, profile_v), fetch(table, table_s), fetch(depth, depth_v)]
    small += [fetch(cells, cells_v), fetch(count, count_s)]
    large = []
    for h in range(halves):
        cut = pl.ds(8 * h, 8)
        large.append(fetch(eta.at[0, :, cut, :], eta_v.at[h]))
        large.append(fetch(flow.at[0, :, cut, :], flow_v.at[h]))
    for copy in small:
        copy.wait()

    classes = depth_v[...]
    speed = jnp.zeros(classes.shape, jnp.float32)
    for c in range(table_s.shape[0]):
        speed = jnp.where(classes == c, table_s[c], speed)
    cel[...] = speed

    lane = lax.broadcasted_iota(jnp.int32, (8, 128), 1)
    sub = lax.broadcasted_iota(jnp.int32, (8, 128), 0)
    inside = lane < levels
    fill = jnp.zeros((1, 128 - levels), jnp.float32)
    keep = jnp.broadcast_to(jnp.concatenate([damping_v[...], fill], axis=1), (8, 128))
    weight = jnp.broadcast_to(jnp.concatenate([profile_v[...], fill], axis=1), (8, 128))
    u = jnp.zeros((8, 128), jnp.float32)
    v = jnp.where(sub == 0, weight * (1.0 / math.sqrt(levels)), 0.0)
    us, vs = [u], [v]
    for r in range(STEPS):
        s = u + v
        bottom = jnp.sum(jnp.where(lane == levels - 1, s, 0.0), axis=1, keepdims=True)
        coef[8 * r : 8 * r + 8, :] = jnp.broadcast_to(bottom, (8, coef.shape[1]))
        vertical = pltpu.roll(s, 1, 1) + pltpu.roll(s, 127, 1) - 2.0 * s
        u = jnp.where(inside, u + VERT * vertical - SHIFT * s + pltpu.roll(s, 1, 0), 0.0)
        v = s * keep
        us.append(u)
        vs.append(v)

    wide = levels * 8
    spread = (
        lax.broadcasted_iota(jnp.int32, (128, wide), 1) // 8
        == lax.broadcasted_iota(jnp.int32, (128, wide), 0)
    ).astype(jnp.bfloat16)
    count_f = len(FIELDS) + 1
    diagonal = (
        lax.broadcasted_iota(jnp.int32, (8 * count_f, wide), 1) % 8
        == lax.broadcasted_iota(jnp.int32, (8 * count_f, wide), 0) % 8
    )

    def matrix(vectors):
        blocks = [jnp.broadcast_to(vectors[n][k : k + 1, :], (8, 128)) for n, k in FIELDS]
        blocks.append(jnp.zeros((8, 128), jnp.float32))
        hi, lo = split(jnp.concatenate(blocks, axis=0))
        zero = jnp.zeros((8 * count_f, wide), jnp.float32)
        hi = jnp.where(diagonal, dot(hi, spread), zero).astype(jnp.bfloat16)
        lo = jnp.where(diagonal, dot(lo, spread), zero).astype(jnp.bfloat16)
        return hi, jnp.concatenate([hi, lo], axis=0)

    w_eta, both_eta = matrix(us)
    w_flow, both_flow = matrix(vs)

    me = lax.axis_index("trench")
    tiles, _, slots = cells_v.shape
    slot = lax.broadcasted_iota(jnp.int32, (1, slots), 1)
    rows_at, columns = [], []
    for source in sources(me, tiles):
        for d in range(3):
            owner = me + d - 1
            inside = (owner >= 0) & (owner < tiles)
            owner = jnp.clip(owner, 0, tiles - 1)
            live = jnp.where(inside, count_s[source, owner], 0)
            cell = cells_v[source, pl.ds(owner, 1), :]
            rows_at.append(jnp.where(slot < live, cell // across + (rows * (d - 1) + PAD), -1))
            columns.append(cell % across)
    places[...] = jnp.broadcast_to(jnp.concatenate(rows_at, axis=1), places.shape)
    columns = jnp.concatenate(columns, axis=1)
    hot[...] = jnp.where(lax.broadcasted_iota(jnp.int32, hot.shape, 0) == columns, 1.0, 0.0).astype(jnp.bfloat16)

    for h in range(halves):
        large[2 * h].wait()
        hi, lo = split(eta_v[h].reshape(wide, across))
        total = dot(both_eta, hi)
        part = dot(w_eta, lo)
        large[2 * h + 1].wait()
        hi, lo = split(flow_v[h].reshape(wide, across))
        total += dot(both_flow, hi)
        part += dot(w_flow, lo)
        part = part + total[: 8 * count_f] + total[8 * count_f :]
        for f in range(len(FIELDS)):
            fields[f, 8 * h : 8 * h + 8, :] = part[8 * f : 8 * f + 8]

    def edge(at, last):
        for f, width in enumerate(HALO):
            start = rows - width if last else 0
            edges[at + HALO_AT[f] : at + HALO_AT[f] + width, :] = fields[f, start : start + width, :]
        start = rows - CEL_HALO if last else 0
        edges[at + CEL_AT : at + CEL_AT + CEL_HALO, :] = cel[start : start + CEL_HALO, :]

    @pl.when(me % 2 == 0)
    def _():
        edge(0, True)
        edge(ROWS, False)

    @pl.when(me % 2 == 1)
    def _():
        edge(0, False)
        edge(ROWS, True)


def sources(me, tiles):
    return [me ^ r ^ core for r in range(0, tiles, 2) for core in range(2)]


def carries_edge(r):
    return (r // 2) & (r // 2 + 1) == 0


def residual_rows(owner, tiles, own, partner):
    near = [jnp.clip(owner + d - 1, 0, tiles - 1) for d in range(3)]
    return jnp.concatenate([source[o] for source in (own, partner) for o in near], axis=1)


def relay_kernel(own, partner, edges, *outs):
    me = lax.axis_index("trench")
    tiles = own.shape[0]
    for r, out in zip(range(2, tiles, 2), outs):
        values = residual_rows(me ^ r, tiles, own, partner)
        fill = jnp.zeros((STEPS, out.shape[1] - values.shape[1]), jnp.float32)
        out[0:STEPS, :] = jnp.concatenate([values, fill], axis=1)
        if carries_edge(r):
            out[STEPS : STEPS + ROWS, :] = edges[ROWS : 2 * ROWS, :]


def advance_kernel(blocks, fields, cel, coef, hot, places, own, partner, edges, *refs):
    cross, outs, (stage, ext, cel_ext) = refs[: -3 - blocks], refs[-3 - blocks : -3], refs[-3:]
    me = lax.axis_index("trench")
    tiles = own.shape[0]
    rows, across = cel.shape
    tall = rows + 2 * PAD
    part = rows // blocks
    odd = me % 2 == 1
    chip = me // 2
    facing = jnp.where(odd, chip + 1, chip - 1)
    inner = edges[0:ROWS, :]
    outer = jnp.zeros(inner.shape, jnp.float32)
    for r, got in zip(range(2, tiles, 2), cross):
        if carries_edge(r):
            match = (facing >= 0) & (facing < tiles // 2) & (chip ^ facing == r // 2)
            outer = jnp.where(match, got[STEPS : STEPS + ROWS, :], outer)
    before = jnp.where(odd, inner, outer)
    after = jnp.where(odd, outer, inner)

    per = 6 * own.shape[2]
    values = [residual_rows(me, tiles, own, partner)] + [got[0:STEPS, 0:per] for got in cross]
    values = jnp.concatenate(values, axis=1)
    here = lax.broadcasted_iota(jnp.int32, (tall, values.shape[1]), 0) == places[0:1, :]
    left = jnp.concatenate([jnp.where(here, values[t : t + 1, :], 0.0) for t in range(STEPS)], axis=0)
    hi, lo = split(left)
    planes = dot(hi, hot[...], ((1,), (1,))) + dot(lo, hot[...], ((1,), (1,)))
    inject = [planes[tall * t : tall * t + tall] for t in range(STEPS)]

    def extend(store, own, at, width):
        store(0, PAD, jnp.zeros((PAD, across), jnp.float32))
        store(PAD + rows, tall, jnp.zeros((PAD, across), jnp.float32))
        store(PAD, PAD + rows, own)
        store(PAD - width, PAD, before[at : at + width])
        store(PAD + rows, PAD + rows + width, after[at : at + width])

    for f, width in enumerate(HALO):
        def store(a, b, value, f=f):
            ext[f, a:b, :] = value
        extend(store, fields[f], HALO_AT[f], width)

    def store_cel(a, b, value):
        cel_ext[a:b, :] = value
    extend(store_cel, cel[...], CEL_AT, CEL_HALO)

    lane = lax.broadcasted_iota(jnp.int32, (tall, across), 1)
    first = lane == 0
    last = lane == across - 1
    speed = cel_ext[...]

    def horizontal(z):
        around = pltpu.roll(z, 1, 0) + pltpu.roll(z, tall - 1, 0)
        around += jnp.where(first, 0.0, pltpu.roll(z, 1, 1))
        around += jnp.where(last, 0.0, pltpu.roll(z, across - 1, 1))
        return speed * (around - 4.0 * z) + SHIFT * z

    def injected(n, k, a, b):
        total = None
        for tau in range(1, n - k + 1):
            r = n - tau
            term = coef[8 * r + k : 8 * r + k + 1, :] * inject[STEPS - tau][a:b]
            total = term if total is None else total + term
        return total

    base = horizontal(ext[0])
    for n in range(1, STEPS + 1):
        z = base
        for k in range(n - 1, 0, -1):
            z = horizontal(z + ext[FIELDS.index((n, k))] + injected(n, k, 0, tall))
        own = z[PAD : PAD + rows] + fields[FIELDS.index((n, 0))] + injected(n, 0, PAD, PAD + rows)
        t = STEPS - n
        for b in range(blocks):
            stage[b, part * t : part * t + part, :] = own[part * b : part * b + part]
    block = lax.axis_index("tblock")
    for r, out in enumerate(outs):
        out[...] = stage[block ^ r]


def prior_kernel(*refs):
    gots, weight, out, whole = refs[:-3], refs[-3], refs[-2], refs[-1]
    block = lax.axis_index("tblock")
    for r, got in enumerate(gots):
        whole[block ^ r] = got[...]
    part = out.shape[1]
    length = out.shape[0]
    series = [whole[i // STEPS, part * (i % STEPS) : part * (i % STEPS) + part, :] for i in range(length)]
    for k in range(length):
        total = weight[0] * series[k]
        for j in range(1, min(weight.shape[0], length - k)):
            total += weight[j] * series[k + j]
        out[k] = total


def shape(*dims, dtype=jnp.float32):
    return jax.ShapeDtypeStruct(dims, dtype)


def spec(space):
    return pl.BlockSpec(memory_space=space)


def body(
    adjoint_eta,
    adjoint_flow,
    residual,
    sensor_cell,
    sensor_count,
    depth_class,
    speed_table,
    damping,
    profile,
    band_weight,
):
    tiles = lax.axis_size("trench")
    blocks = lax.axis_size("tblock")
    levels, rows, across = adjoint_eta.shape[1:]
    tall = rows + 2 * PAD
    params = pltpu.CompilerParams(vmem_limit_bytes=LIMIT)

    def swaps(parts, axis):
        devices = lax.axis_size(axis)
        moved = [lax.ppermute(parts[r], axis, [(i, i ^ r) for i in range(devices)]) for r in range(1, devices)]
        return [parts[0]] + moved

    own = residual[0, 0]
    slots = own.shape[2]
    lanes = 3 * tiles * slots

    def swap(x, r):
        return lax.ppermute(x, "trench", [(i, i ^ r) for i in range(tiles)])

    partner = swap(own, 1)
    fields, edges, cel, coef, hot, places = pl.pallas_call(
        contract_kernel,
        out_shape=(
            shape(len(FIELDS), rows, across),
            shape(2 * ROWS, across),
            shape(rows, across),
            shape(8 * STEPS, across),
            shape(across, lanes, dtype=jnp.bfloat16),
            shape(8, lanes, dtype=jnp.int32),
        ),
        in_specs=[spec(pltpu.HBM)] * 8,
        out_specs=(spec(VMEM),) * 6,
        scratch_shapes=[
            VMEM((rows // 8, levels, 8, across), jnp.float32),
            VMEM((rows // 8, levels, 8, across), jnp.float32),
            VMEM((rows, across), jnp.int32),
            SMEM(speed_table.shape, jnp.float32),
            VMEM((1, levels), jnp.float32),
            VMEM((1, levels), jnp.float32),
            VMEM(sensor_cell.shape, jnp.int32),
            SMEM(sensor_count.shape, jnp.int32),
            pltpu.SemaphoreType.DMA((6 + 2 * (rows // 8),)),
        ],
        compiler_params=pltpu.CompilerParams(vmem_limit_bytes=LIMIT_CONTRACT),
        cost_estimate=pl.CostEstimate(flops=10**9, bytes_accessed=10**7, transcendentals=0),
        name="contract",
    )(adjoint_eta, adjoint_flow, depth_class, speed_table, damping[None], profile[None], sensor_cell, sensor_count)

    edges = swap(edges, 1)
    relays = pl.pallas_call(
        relay_kernel,
        out_shape=[
            shape(STEPS + ROWS, across) if carries_edge(r) else shape(STEPS, -(-6 * slots // 128) * 128)
            for r in range(2, tiles, 2)
        ],
        in_specs=[spec(VMEM)] * 3,
        out_specs=[spec(VMEM)] * (tiles // 2 - 1),
        compiler_params=params,
        name="relay",
    )(own, partner, edges)
    cross = [swap(relay, r) for relay, r in zip(relays, range(2, tiles, 2))]
    series = pl.pallas_call(
        functools.partial(advance_kernel, blocks),
        out_shape=(shape(STEPS * rows // blocks, across),) * blocks,
        in_specs=[spec(VMEM)] * (8 + len(cross)),
        out_specs=(spec(VMEM),) * blocks,
        scratch_shapes=[
            VMEM((blocks, STEPS * rows // blocks, across), jnp.float32),
            VMEM((len(HALO), tall, across), jnp.float32),
            VMEM((tall, across), jnp.float32),
        ],
        compiler_params=params,
        name="advance",
    )(fields, cel, coef, hot, places, own, partner, edges, *cross)
    gots = swaps(series, "tblock")
    return pl.pallas_call(
        prior_kernel,
        out_shape=shape(STEPS * blocks, rows // blocks, across),
        in_specs=[spec(VMEM)] * blocks + [spec(SMEM)],
        out_specs=spec(VMEM),
        scratch_shapes=[VMEM((blocks, STEPS * rows // blocks, across), jnp.float32)],
        compiler_params=params,
        name="prior",
    )(*gots, band_weight)


def solution(mesh):
    in_specs = (
        P("tblock", None, "trench", None),
        P("tblock", None, "trench", None),
        P("tblock", "trench", None, None, None),
        P(),
        P(),
        P("trench", None),
        P(),
        P(),
        P(),
        P(),
    )
    out_specs = P(None, ("trench", "tblock"), None)
    return jax.shard_map(body, mesh=mesh, in_specs=in_specs, out_specs=out_specs, check_vma=False)
```

```python
import functools
import math

import jax
import jax.numpy as jnp
from jax import lax
from jax.experimental import pallas as pl
from jax.experimental.pallas import tpu as pltpu
from jax.sharding import PartitionSpec as P

VERT = 0.2
STEPS = 4
PAD = 8
VMEM = pltpu.VMEM
SMEM = pltpu.SMEM
LIMIT = 32 * 1024 * 1024

SHIFT = 1.2

FIELDS = [(4, 4), (4, 3), (4, 2), (3, 2), (4, 1), (3, 1), (2, 1), (4, 0), (3, 0), (2, 0), (1, 0)]
HALO = [4, 3, 2, 2, 1, 1, 1]
HALO_AT = [0, 4, 7, 9, 11, 12, 13]
CEL_AT = 14
CEL_HALO = 3
ROWS = 17


def split(x):
    hi = x.astype(jnp.bfloat16)
    return hi, (x - hi.astype(jnp.float32)).astype(jnp.bfloat16)


def dot(a, b, dims=((1,), (0,))):
    return lax.dot_general(a, b, (dims, ((), ())), preferred_element_type=jnp.float32)


def contract_kernel(
    eta, flow, depth, table, damping, profile, cells, count, residual,
    fields, edges, cel, coef, hot, places,
    eta_v, flow_v, depth_v, table_s, damping_v, profile_v, cells_v, count_s, own, sems,
):
    levels, rows, across = eta.shape[1:]
    halves = rows // 8
    copies = []

    def fetch(src, dst):
        copy = pltpu.make_async_copy(src, dst, sems.at[len(copies)])
        copy.start()
        copies.append(copy)
        return copy

    small = [fetch(damping, damping_v), fetch(profile, profile_v), fetch(table, table_s), fetch(depth, depth_v)]
    small += [fetch(cells, cells_v), fetch(count, count_s), fetch(residual, own)]
    large = []
    for h in range(halves):
        cut = pl.ds(8 * h, 8)
        large.append(fetch(eta.at[0, :, cut, :], eta_v.at[h]))
        large.append(fetch(flow.at[0, :, cut, :], flow_v.at[h]))
    for copy in small:
        copy.wait()

    classes = depth_v[...]
    speed = jnp.zeros(classes.shape, jnp.float32)
    for c in range(table_s.shape[0]):
        speed = jnp.where(classes == c, table_s[c], speed)
    cel[...] = speed

    lane = lax.broadcasted_iota(jnp.int32, (8, 128), 1)
    sub = lax.broadcasted_iota(jnp.int32, (8, 128), 0)
    inside = lane < levels
    fill = jnp.zeros((1, 128 - levels), jnp.float32)
    keep = jnp.broadcast_to(jnp.concatenate([damping_v[...], fill], axis=1), (8, 128))
    weight = jnp.broadcast_to(jnp.concatenate([profile_v[...], fill], axis=1), (8, 128))
    u = jnp.zeros((8, 128), jnp.float32)
    v = jnp.where(sub == 0, weight * (1.0 / math.sqrt(levels)), 0.0)
    us, vs = [u], [v]
    for r in range(STEPS):
        s = u + v
        bottom = jnp.sum(jnp.where(lane == levels - 1, s, 0.0), axis=1, keepdims=True)
        coef[8 * r : 8 * r + 8, :] = jnp.broadcast_to(bottom, (8, coef.shape[1]))
        vertical = pltpu.roll(s, 1, 1) + pltpu.roll(s, 127, 1) - 2.0 * s
        u = jnp.where(inside, u + VERT * vertical - SHIFT * s + pltpu.roll(s, 1, 0), 0.0)
        v = s * keep
        us.append(u)
        vs.append(v)

    wide = levels * 8
    spread = (
        lax.broadcasted_iota(jnp.int32, (128, wide), 1) // 8
        == lax.broadcasted_iota(jnp.int32, (128, wide), 0)
    ).astype(jnp.bfloat16)
    count_f = len(FIELDS) + 1
    diagonal = (
        lax.broadcasted_iota(jnp.int32, (8 * count_f, wide), 1) % 8
        == lax.broadcasted_iota(jnp.int32, (8 * count_f, wide), 0) % 8
    )

    def matrix(vectors):
        blocks = [jnp.broadcast_to(vectors[n][k : k + 1, :], (8, 128)) for n, k in FIELDS]
        blocks.append(jnp.zeros((8, 128), jnp.float32))
        hi, lo = split(jnp.concatenate(blocks, axis=0))
        zero = jnp.zeros((8 * count_f, wide), jnp.float32)
        hi = jnp.where(diagonal, dot(hi, spread), zero).astype(jnp.bfloat16)
        lo = jnp.where(diagonal, dot(lo, spread), zero).astype(jnp.bfloat16)
        return hi, jnp.concatenate([hi, lo], axis=0)

    w_eta, both_eta = matrix(us)
    w_flow, both_flow = matrix(vs)

    me = lax.axis_index("trench")
    tiles, _, slots = cells_v.shape
    slot = lax.broadcasted_iota(jnp.int32, (1, slots), 1)
    listed = []
    for source in sources(me, tiles):
        for d in range(3):
            owner = me + d - 1
            inside = (owner >= 0) & (owner < tiles)
            owner = jnp.clip(owner, 0, tiles - 1)
            live = jnp.where(inside, count_s[source, owner], 0)
            listed.append(jnp.where(slot < live, cells_v[source, pl.ds(owner, 1), :], -1))
    listed = jnp.concatenate(listed, axis=1)
    tile = (lax.broadcasted_iota(jnp.int32, listed.shape, 1) // slots) % 3
    bits = across.bit_length() - 1
    at = jnp.where(listed < 0, -1, (listed >> bits) + (rows * (tile - 1) + PAD))
    places[...] = jnp.broadcast_to(at, places.shape)
    columns = listed & (across - 1)
    hot[...] = jnp.where(lax.broadcasted_iota(jnp.int32, hot.shape, 0) == columns, 1.0, 0.0).astype(jnp.bfloat16)

    for q in range(tiles // 2):
        row, lane_at = packed(q, across)
        values = residual_rows(me ^ 1 ^ (2 * q), own)
        edges[row : row + STEPS, lane_at : lane_at + 128] = jnp.concatenate(
            [values, jnp.zeros((STEPS, 128 - values.shape[1]), jnp.float32)], axis=1
        )

    for h in range(halves):
        large[2 * h].wait()
        hi, lo = split(eta_v[h].reshape(wide, across))
        total = dot(both_eta, hi)
        part = dot(w_eta, lo)
        large[2 * h + 1].wait()
        hi, lo = split(flow_v[h].reshape(wide, across))
        total += dot(both_flow, hi)
        part += dot(w_flow, lo)
        part = part + total[: 8 * count_f] + total[8 * count_f :]
        for f in range(len(FIELDS)):
            fields[f, 8 * h : 8 * h + 8, :] = part[8 * f : 8 * f + 8]

    def edge(at, last):
        for f, width in enumerate(HALO):
            start = rows - width if last else 0
            edges[at + HALO_AT[f] : at + HALO_AT[f] + width, :] = fields[f, start : start + width, :]
        start = rows - CEL_HALO if last else 0
        edges[at + CEL_AT : at + CEL_AT + CEL_HALO, :] = cel[start : start + CEL_HALO, :]

    @pl.when(me % 2 == 0)
    def _():
        edge(0, True)
        edge(ROWS, False)

    @pl.when(me % 2 == 1)
    def _():
        edge(0, False)
        edge(ROWS, True)


def sources(me, tiles):
    return [me ^ r ^ core for r in range(0, tiles, 2) for core in range(2)]


def carries_edge(r):
    return (r // 2) & (r // 2 + 1) == 0


def residual_rows(owner, own):
    tiles = own.shape[0]
    return jnp.concatenate([own[jnp.clip(owner + d - 1, 0, tiles - 1)] for d in range(3)], axis=1)


def packed(q, across):
    per = across // 128
    return 2 * ROWS + STEPS * (q // per), 128 * (q % per)


def both_rows(owner, q, own, edges):
    row, lane_at = packed(q, edges.shape[1])
    slots = own.shape[2]
    return jnp.concatenate(
        [residual_rows(owner, own), edges[row : row + STEPS, lane_at : lane_at + 3 * slots]], axis=1
    )


def relay_kernel(own, edges, *outs):
    me = lax.axis_index("trench")
    for q, out in enumerate(outs, 1):
        values = both_rows(me ^ (2 * q), q, own, edges)
        fill = jnp.zeros((STEPS, out.shape[1] - values.shape[1]), jnp.float32)
        out[0:STEPS, :] = jnp.concatenate([values, fill], axis=1)
        if carries_edge(2 * q):
            out[STEPS : STEPS + ROWS, :] = edges[ROWS : 2 * ROWS, :]


def advance_kernel(blocks, fields, cel, coef, hot, places, own, edges, *refs):
    cross, outs, (stage, ext, cel_ext) = refs[: -3 - blocks], refs[-3 - blocks : -3], refs[-3:]
    me = lax.axis_index("trench")
    tiles = own.shape[0]
    rows, across = cel.shape
    tall = rows + 2 * PAD
    part = rows // blocks
    odd = me % 2 == 1
    chip = me // 2
    facing = jnp.where(odd, chip + 1, chip - 1)
    inner = edges[0:ROWS, :]
    outer = jnp.zeros(inner.shape, jnp.float32)
    for r, got in zip(range(2, tiles, 2), cross):
        if carries_edge(r):
            match = (facing >= 0) & (facing < tiles // 2) & (chip ^ facing == r // 2)
            outer = jnp.where(match, got[STEPS : STEPS + ROWS, :], outer)
    before = jnp.where(odd, inner, outer)
    after = jnp.where(odd, outer, inner)

    per = 6 * own.shape[2]
    values = [both_rows(me, 0, own, edges)] + [got[0:STEPS, 0:per] for got in cross]
    values = jnp.concatenate(values, axis=1)
    here = lax.broadcasted_iota(jnp.int32, (tall, values.shape[1]), 0) == places[0:1, :]
    left = jnp.concatenate([jnp.where(here, values[t : t + 1, :], 0.0) for t in range(STEPS)], axis=0)
    hi, lo = split(left)
    planes = dot(hi, hot[...], ((1,), (1,))) + dot(lo, hot[...], ((1,), (1,)))
    inject = [planes[tall * t : tall * t + tall] for t in range(STEPS)]

    def extend(store, own, at, width):
        store(0, PAD, jnp.zeros((PAD, across), jnp.float32))
        store(PAD + rows, tall, jnp.zeros((PAD, across), jnp.float32))
        store(PAD, PAD + rows, own)
        store(PAD - width, PAD, before[at : at + width])
        store(PAD + rows, PAD + rows + width, after[at : at + width])

    for f, width in enumerate(HALO):
        def store(a, b, value, f=f):
            ext[f, a:b, :] = value
        extend(store, fields[f], HALO_AT[f], width)

    def store_cel(a, b, value):
        cel_ext[a:b, :] = value
    extend(store_cel, cel[...], CEL_AT, CEL_HALO)

    lane = lax.broadcasted_iota(jnp.int32, (tall, across), 1)
    first = lane == 0
    last = lane == across - 1
    speed = cel_ext[...]

    def horizontal(z):
        around = pltpu.roll(z, 1, 0) + pltpu.roll(z, tall - 1, 0)
        around += jnp.where(first, 0.0, pltpu.roll(z, 1, 1))
        around += jnp.where(last, 0.0, pltpu.roll(z, across - 1, 1))
        return speed * (around - 4.0 * z) + SHIFT * z

    def injected(n, k, a, b):
        total = None
        for tau in range(1, n - k + 1):
            r = n - tau
            term = coef[8 * r + k : 8 * r + k + 1, :] * inject[STEPS - tau][a:b]
            total = term if total is None else total + term
        return total

    base = horizontal(ext[0])
    for n in range(1, STEPS + 1):
        z = base
        for k in range(n - 1, 0, -1):
            z = horizontal(z + ext[FIELDS.index((n, k))] + injected(n, k, 0, tall))
        own = z[PAD : PAD + rows] + fields[FIELDS.index((n, 0))] + injected(n, 0, PAD, PAD + rows)
        t = STEPS - n
        for b in range(blocks):
            stage[b, part * t : part * t + part, :] = own[part * b : part * b + part]
    block = lax.axis_index("tblock")
    for r, out in enumerate(outs):
        out[...] = stage[block ^ r]


def prior_kernel(*refs):
    gots, weight, out, whole = refs[:-3], refs[-3], refs[-2], refs[-1]
    block = lax.axis_index("tblock")
    for r, got in enumerate(gots):
        whole[block ^ r] = got[...]
    part = out.shape[1]
    length = out.shape[0]
    width = weight.shape[0]
    if 2 * part != 8:
        series = [whole[i // STEPS, part * (i % STEPS) : part * (i % STEPS) + part, :] for i in range(length)]
        for k in range(length):
            out[k] = sum(weight[j] * series[k + j] for j in range(min(width, length - k)))
        return
    pairs = length // 2
    even = [whole[p // 2, 8 * (p % 2) : 8 * (p % 2) + 8, :] for p in range(pairs)]
    half = lax.broadcasted_iota(jnp.int32, even[0].shape, 0) < part
    turned = [pltpu.roll(x, part, 0) for x in even] + [jnp.zeros(even[0].shape, jnp.float32)]
    odd = [jnp.where(half, turned[p], turned[p + 1]) for p in range(pairs)]
    for p in range(pairs):
        total = None
        for j in range(width):
            if p + j // 2 < pairs:
                term = weight[j] * (odd if j % 2 else even)[p + j // 2]
                total = term if total is None else total + term
        out[2 * p] = total[:part]
        out[2 * p + 1] = total[part:]


def shape(*dims, dtype=jnp.float32):
    return jax.ShapeDtypeStruct(dims, dtype)


def spec(space):
    return pl.BlockSpec(memory_space=space)


def body(
    adjoint_eta,
    adjoint_flow,
    residual,
    sensor_cell,
    sensor_count,
    depth_class,
    speed_table,
    damping,
    profile,
    band_weight,
):
    tiles = lax.axis_size("trench")
    blocks = lax.axis_size("tblock")
    levels, rows, across = adjoint_eta.shape[1:]
    tall = rows + 2 * PAD
    params = pltpu.CompilerParams(vmem_limit_bytes=LIMIT)

    def swaps(parts, axis):
        devices = lax.axis_size(axis)
        moved = {r: lax.ppermute(parts[r], axis, [(i, i ^ r) for i in range(devices)]) for r in range(devices - 1, 0, -1)}
        return [parts[0]] + [moved[r] for r in range(1, devices)]

    own = residual[0, 0]
    slots = own.shape[2]
    lanes = 3 * tiles * slots

    def swap(x, r):
        return lax.ppermute(x, "trench", [(i, i ^ r) for i in range(tiles)])

    fields, edges, cel, coef, hot, places = pl.pallas_call(
        contract_kernel,
        out_shape=(
            shape(len(FIELDS), rows, across),
            shape(2 * ROWS + STEPS * -(-64 * tiles // across), across),
            shape(rows, across),
            shape(8 * STEPS, across),
            shape(across, lanes, dtype=jnp.bfloat16),
            shape(8, lanes, dtype=jnp.int32),
        ),
        in_specs=[spec(pltpu.HBM)] * 9,
        out_specs=(spec(VMEM),) * 6,
        scratch_shapes=[
            VMEM((rows // 8, levels, 8, across), jnp.float32),
            VMEM((rows // 8, levels, 8, across), jnp.float32),
            VMEM((rows, across), jnp.int32),
            SMEM(speed_table.shape, jnp.float32),
            VMEM((1, levels), jnp.float32),
            VMEM((1, levels), jnp.float32),
            VMEM(sensor_cell.shape, jnp.int32),
            SMEM(sensor_count.shape, jnp.int32),
            VMEM(own.shape, jnp.float32),
            pltpu.SemaphoreType.DMA((7 + 2 * (rows // 8),)),
        ],
        compiler_params=params,
        cost_estimate=pl.CostEstimate(flops=10**9, bytes_accessed=10**7, transcendentals=0),
        name="contract",
    )(
        *[
            pltpu.with_memory_space_constraint(x, pltpu.HBM)
            for x in (
                adjoint_eta, adjoint_flow, depth_class, speed_table, damping[None], profile[None],
                sensor_cell, sensor_count, own,
            )
        ]
    )

    edges = swap(edges, 1)
    relays = pl.pallas_call(
        relay_kernel,
        out_shape=[
            shape(STEPS + ROWS, across) if carries_edge(r) else shape(STEPS, -(-6 * slots // 128) * 128)
            for r in range(2, tiles, 2)
        ],
        in_specs=[spec(VMEM)] * 2,
        out_specs=[spec(VMEM)] * (tiles // 2 - 1),
        compiler_params=params,
        name="relay",
    )(own, edges)
    cross = [swap(relay, r) for relay, r in zip(relays, range(2, tiles, 2))]
    series = pl.pallas_call(
        functools.partial(advance_kernel, blocks),
        out_shape=(shape(STEPS * rows // blocks, across),) * blocks,
        in_specs=[spec(VMEM)] * (7 + len(cross)),
        out_specs=(spec(VMEM),) * blocks,
        scratch_shapes=[
            VMEM((blocks, STEPS * rows // blocks, across), jnp.float32),
            VMEM((len(HALO), tall, across), jnp.float32),
            VMEM((tall, across), jnp.float32),
        ],
        compiler_params=params,
        name="advance",
    )(fields, cel, coef, hot, places, own, edges, *cross)
    gots = swaps(series, "tblock")
    return pl.pallas_call(
        prior_kernel,
        out_shape=shape(STEPS * blocks, rows // blocks, across),
        in_specs=[spec(VMEM)] * blocks + [spec(SMEM)],
        out_specs=spec(VMEM),
        scratch_shapes=[VMEM((blocks, STEPS * rows // blocks, across), jnp.float32)],
        compiler_params=params,
        name="prior",
    )(*gots, band_weight)


def solution(mesh):
    in_specs = (
        P("tblock", None, "trench", None),
        P("tblock", None, "trench", None),
        P("tblock", "trench", None, None, None),
        P(),
        P(),
        P("trench", None),
        P(),
        P(),
        P(),
        P(),
    )
    out_specs = P(None, ("trench", "tblock"), None)
    return jax.shard_map(body, mesh=mesh, in_specs=in_specs, out_specs=out_specs, check_vma=False)
```

```python
import functools
import math

import jax
import jax.numpy as jnp
from jax import lax
from jax.experimental import pallas as pl
from jax.experimental.pallas import tpu as pltpu
from jax.sharding import PartitionSpec as P

VERT = 0.2
STEPS = 4
PAD = 8
VMEM = pltpu.VMEM
SMEM = pltpu.SMEM
LIMIT = 32 * 1024 * 1024

SHIFT = 1.2

FIELDS = [(4, 4), (4, 3), (4, 2), (3, 2), (4, 1), (3, 1), (2, 1), (4, 0), (3, 0), (2, 0), (1, 0)]
HALO = [4, 3, 2, 2, 1, 1, 1]
HALO_AT = [0, 4, 7, 9, 11, 12, 13]
CEL_AT = 14
CEL_HALO = 3
ROWS = 17


def split(x):
    hi = x.astype(jnp.bfloat16)
    return hi, (x - hi.astype(jnp.float32)).astype(jnp.bfloat16)


def dot(a, b, dims=((1,), (0,))):
    return lax.dot_general(a, b, (dims, ((), ())), preferred_element_type=jnp.float32)


def contract_kernel(
    eta, flow, depth, table, damping, profile, cells, count, residual,
    fields, edges, outer, cel, coef, hot, places,
    eta_v, flow_v, depth_v, table_s, damping_v, profile_v, cells_v, count_s, own, sems,
):
    levels, rows, across = eta.shape[1:]
    halves = rows // 8
    copies = []

    def fetch(src, dst):
        copy = pltpu.make_async_copy(src, dst, sems.at[len(copies)])
        copy.start()
        copies.append(copy)
        return copy

    small = [fetch(damping, damping_v), fetch(profile, profile_v), fetch(table, table_s), fetch(depth, depth_v)]
    small += [fetch(cells, cells_v), fetch(count, count_s), fetch(residual, own)]
    large = []
    for h in range(halves):
        cut = pl.ds(8 * h, 8)
        large.append(fetch(eta.at[0, :, cut, :], eta_v.at[h]))
        large.append(fetch(flow.at[0, :, cut, :], flow_v.at[h]))
    for copy in small:
        copy.wait()

    classes = depth_v[...]
    speed = jnp.zeros(classes.shape, jnp.float32)
    for c in range(table_s.shape[0]):
        speed = jnp.where(classes == c, table_s[c], speed)
    cel[...] = speed

    lane = lax.broadcasted_iota(jnp.int32, (8, 128), 1)
    sub = lax.broadcasted_iota(jnp.int32, (8, 128), 0)
    inside = lane < levels
    fill = jnp.zeros((1, 128 - levels), jnp.float32)
    keep = jnp.broadcast_to(jnp.concatenate([damping_v[...], fill], axis=1), (8, 128))
    weight = jnp.broadcast_to(jnp.concatenate([profile_v[...], fill], axis=1), (8, 128))
    u = jnp.zeros((8, 128), jnp.float32)
    v = jnp.where(sub == 0, weight * (1.0 / math.sqrt(levels)), 0.0)
    us, vs = [u], [v]
    for r in range(STEPS):
        s = u + v
        bottom = jnp.sum(jnp.where(lane == levels - 1, s, 0.0), axis=1, keepdims=True)
        coef[8 * r : 8 * r + 8, :] = jnp.broadcast_to(bottom, (8, coef.shape[1]))
        vertical = pltpu.roll(s, 1, 1) + pltpu.roll(s, 127, 1) - 2.0 * s
        u = jnp.where(inside, u + VERT * vertical - SHIFT * s + pltpu.roll(s, 1, 0), 0.0)
        v = s * keep
        us.append(u)
        vs.append(v)

    wide = levels * 8
    spread = (
        lax.broadcasted_iota(jnp.int32, (128, wide), 1) // 8
        == lax.broadcasted_iota(jnp.int32, (128, wide), 0)
    ).astype(jnp.bfloat16)
    count_f = len(FIELDS) + 1
    diagonal = (
        lax.broadcasted_iota(jnp.int32, (8 * count_f, wide), 1) % 8
        == lax.broadcasted_iota(jnp.int32, (8 * count_f, wide), 0) % 8
    )

    def matrix(vectors):
        blocks = [jnp.broadcast_to(vectors[n][k : k + 1, :], (8, 128)) for n, k in FIELDS]
        blocks.append(jnp.zeros((8, 128), jnp.float32))
        hi, lo = split(jnp.concatenate(blocks, axis=0))
        zero = jnp.zeros((8 * count_f, wide), jnp.float32)
        hi = jnp.where(diagonal, dot(hi, spread), zero).astype(jnp.bfloat16)
        lo = jnp.where(diagonal, dot(lo, spread), zero).astype(jnp.bfloat16)
        return hi, jnp.concatenate([hi, lo], axis=0)

    w_eta, both_eta = matrix(us)
    w_flow, both_flow = matrix(vs)

    me = lax.axis_index("trench")
    tiles, _, slots = cells_v.shape
    slot = lax.broadcasted_iota(jnp.int32, (1, slots), 1)
    listed = []
    for source in sources(me, tiles):
        for d in range(3):
            owner = me + d - 1
            inside = (owner >= 0) & (owner < tiles)
            owner = jnp.clip(owner, 0, tiles - 1)
            live = jnp.where(inside, count_s[source, owner], 0)
            listed.append(jnp.where(slot < live, cells_v[source, pl.ds(owner, 1), :], -1))
    listed = jnp.concatenate(listed, axis=1)
    tile = (lax.broadcasted_iota(jnp.int32, listed.shape, 1) // slots) % 3
    bits = across.bit_length() - 1
    at = jnp.where(listed < 0, -1, (listed >> bits) + (rows * (tile - 1) + PAD))
    places[...] = jnp.broadcast_to(at, places.shape)
    columns = listed & (across - 1)
    hot[...] = jnp.where(lax.broadcasted_iota(jnp.int32, hot.shape, 0) == columns, 1.0, 0.0).astype(jnp.bfloat16)

    for q in range(tiles // 2):
        row, lane_at = packed(q, across)
        values = residual_rows(met(me ^ 1, q, tiles), own)
        edges[row : row + STEPS, lane_at : lane_at + 128] = jnp.concatenate(
            [values, jnp.zeros((STEPS, 128 - values.shape[1]), jnp.float32)], axis=1
        )

    for h in range(halves):
        large[2 * h].wait()
        hi, lo = split(eta_v[h].reshape(wide, across))
        total = dot(both_eta, hi)
        part = dot(w_eta, lo)
        large[2 * h + 1].wait()
        hi, lo = split(flow_v[h].reshape(wide, across))
        total += dot(both_flow, hi)
        part += dot(w_flow, lo)
        part = part + total[: 8 * count_f] + total[8 * count_f :]
        for f in range(len(FIELDS)):
            fields[f, 8 * h : 8 * h + 8, :] = part[8 * f : 8 * f + 8]

    def edge(out, last):
        for f, width in enumerate(HALO):
            start = rows - width if last else 0
            out[HALO_AT[f] : HALO_AT[f] + width, :] = fields[f, start : start + width, :]
        start = rows - CEL_HALO if last else 0
        out[CEL_AT : CEL_AT + CEL_HALO, :] = cel[start : start + CEL_HALO, :]

    @pl.when(me % 2 == 0)
    def _():
        edge(edges, True)
        edge(outer, False)

    @pl.when(me % 2 == 1)
    def _():
        edge(edges, False)
        edge(outer, True)


def met(me, d, tiles):
    odd = me % 2
    chip = (me // 2 + jnp.where(odd == 1, d, tiles // 2 - d)) % (tiles // 2)
    return jnp.where(d == 0, me, 2 * chip + 1 - odd)


def sources(me, tiles):
    return [met(me, d, tiles) ^ core for d in range(tiles // 2) for core in range(2)]


def residual_rows(owner, own):
    tiles = own.shape[0]
    return jnp.concatenate([own[jnp.clip(owner + d - 1, 0, tiles - 1)] for d in range(3)], axis=1)


def packed(q, across):
    per = across // 128
    return ROWS + STEPS * (q // per), 128 * (q % per)


def both_rows(owner, q, own, edges):
    row, lane_at = packed(q, edges.shape[1])
    slots = own.shape[2]
    return jnp.concatenate(
        [residual_rows(owner, own), edges[row : row + STEPS, lane_at : lane_at + 3 * slots]], axis=1
    )


def relay_kernel(own, edges, outer, *outs):
    me = lax.axis_index("trench")
    tiles = own.shape[0]
    for d, out in enumerate(outs, 1):
        values = both_rows(met(me, d, tiles), d, own, edges)
        fill = jnp.zeros((STEPS, out.shape[1] - values.shape[1]), jnp.float32)
        out[0:STEPS, :] = jnp.concatenate([values, fill], axis=1)
        if d == 1:
            out[STEPS : STEPS + ROWS, :] = outer[...]


def advance_kernel(blocks, fields, cel, coef, hot, places, own, edges, *refs):
    cross, outs, (stage, ext, cel_ext) = refs[: -3 - blocks], refs[-3 - blocks : -3], refs[-3:]
    me = lax.axis_index("trench")
    tiles = own.shape[0]
    rows, across = cel.shape
    tall = rows + 2 * PAD
    part = rows // blocks
    odd = me % 2 == 1
    facing = me // 2 + jnp.where(odd, 1, -1)
    inner = edges[0:ROWS, :]
    outer = jnp.zeros(inner.shape, jnp.float32)
    if cross:
        outer = jnp.where((facing >= 0) & (facing < tiles // 2), cross[0][STEPS : STEPS + ROWS, :], outer)
    before = jnp.where(odd, inner, outer)
    after = jnp.where(odd, outer, inner)

    per = 6 * own.shape[2]
    values = [both_rows(me, 0, own, edges)] + [got[0:STEPS, 0:per] for got in cross]
    values = jnp.concatenate(values, axis=1)
    here = lax.broadcasted_iota(jnp.int32, (tall, values.shape[1]), 0) == places[0:1, :]
    left = jnp.concatenate([jnp.where(here, values[t : t + 1, :], 0.0) for t in range(STEPS)], axis=0)
    hi, lo = split(left)
    planes = dot(hi, hot[...], ((1,), (1,))) + dot(lo, hot[...], ((1,), (1,)))
    inject = [planes[tall * t : tall * t + tall] for t in range(STEPS)]

    def extend(store, own, at, width):
        store(0, PAD, jnp.zeros((PAD, across), jnp.float32))
        store(PAD + rows, tall, jnp.zeros((PAD, across), jnp.float32))
        store(PAD, PAD + rows, own)
        store(PAD - width, PAD, before[at : at + width])
        store(PAD + rows, PAD + rows + width, after[at : at + width])

    for f, width in enumerate(HALO):
        def store(a, b, value, f=f):
            ext[f, a:b, :] = value
        extend(store, fields[f], HALO_AT[f], width)

    def store_cel(a, b, value):
        cel_ext[a:b, :] = value
    extend(store_cel, cel[...], CEL_AT, CEL_HALO)

    lane = lax.broadcasted_iota(jnp.int32, (tall, across), 1)
    first = lane == 0
    last = lane == across - 1
    speed = cel_ext[...]

    def horizontal(z):
        around = pltpu.roll(z, 1, 0) + pltpu.roll(z, tall - 1, 0)
        around += jnp.where(first, 0.0, pltpu.roll(z, 1, 1))
        around += jnp.where(last, 0.0, pltpu.roll(z, across - 1, 1))
        return speed * (around - 4.0 * z) + SHIFT * z

    def injected(n, k, a, b):
        total = None
        for tau in range(1, n - k + 1):
            r = n - tau
            term = coef[8 * r + k : 8 * r + k + 1, :] * inject[STEPS - tau][a:b]
            total = term if total is None else total + term
        return total

    base = horizontal(ext[0])
    for n in range(1, STEPS + 1):
        z = base
        for k in range(n - 1, 0, -1):
            z = horizontal(z + ext[FIELDS.index((n, k))] + injected(n, k, 0, tall))
        own = z[PAD : PAD + rows] + fields[FIELDS.index((n, 0))] + injected(n, 0, PAD, PAD + rows)
        t = STEPS - n
        for b in range(blocks):
            stage[b, part * t : part * t + part, :] = own[part * b : part * b + part]
    block = lax.axis_index("tblock")
    for r, out in enumerate(outs):
        out[...] = stage[block ^ r]


def prior_kernel(*refs):
    gots, weight, out, whole = refs[:-3], refs[-3], refs[-2], refs[-1]
    block = lax.axis_index("tblock")
    for r, got in enumerate(reversed(gots)):
        whole[block ^ r] = got[...]
    part = out.shape[1]
    length = out.shape[0]
    width = weight.shape[0]
    if 2 * part != 8:
        series = [whole[i // STEPS, part * (i % STEPS) : part * (i % STEPS) + part, :] for i in range(length)]
        for k in range(length):
            out[k] = sum(weight[j] * series[k + j] for j in range(min(width, length - k)))
        return
    pairs = length // 2
    even = [whole[p // 2, 8 * (p % 2) : 8 * (p % 2) + 8, :] for p in range(pairs)]
    half = lax.broadcasted_iota(jnp.int32, even[0].shape, 0) < part
    turned = [pltpu.roll(x, part, 0) for x in even] + [jnp.zeros(even[0].shape, jnp.float32)]
    odd = [jnp.where(half, turned[p], turned[p + 1]) for p in range(pairs)]
    for p in range(pairs):
        total = None
        for j in range(width):
            if p + j // 2 < pairs:
                term = weight[j] * (odd if j % 2 else even)[p + j // 2]
                total = term if total is None else total + term
        out[2 * p] = total[:part]
        out[2 * p + 1] = total[part:]


def shape(*dims, dtype=jnp.float32):
    return jax.ShapeDtypeStruct(dims, dtype)


def spec(space):
    return pl.BlockSpec(memory_space=space)


def body(
    adjoint_eta,
    adjoint_flow,
    residual,
    sensor_cell,
    sensor_count,
    depth_class,
    speed_table,
    damping,
    profile,
    band_weight,
):
    tiles = lax.axis_size("trench")
    blocks = lax.axis_size("tblock")
    levels, rows, across = adjoint_eta.shape[1:]
    tall = rows + 2 * PAD
    params = pltpu.CompilerParams(vmem_limit_bytes=LIMIT)

    def swaps(parts, axis):
        devices = lax.axis_size(axis)
        moved = {r: lax.ppermute(parts[r], axis, [(i, i ^ r) for i in range(devices)]) for r in range(devices - 1, 0, -1)}
        return [parts[0]] + [moved[r] for r in range(1, devices)]

    own = residual[0, 0]
    slots = own.shape[2]
    lanes = 3 * tiles * slots

    chips = tiles // 2

    def meet(x, d):
        pairs = [(2 * c + 1, 2 * ((c + d) % chips)) for c in range(chips)]
        return lax.ppermute(x, "trench", pairs + [(j, i) for i, j in pairs])

    fields, edges, outer, cel, coef, hot, places = pl.pallas_call(
        contract_kernel,
        out_shape=(
            shape(len(FIELDS), rows, across),
            shape(ROWS + STEPS * -(-64 * tiles // across), across),
            shape(ROWS, across),
            shape(rows, across),
            shape(8 * STEPS, across),
            shape(across, lanes, dtype=jnp.bfloat16),
            shape(8, lanes, dtype=jnp.int32),
        ),
        in_specs=[spec(pltpu.HBM)] * 9,
        out_specs=(spec(VMEM),) * 7,
        scratch_shapes=[
            VMEM((rows // 8, levels, 8, across), jnp.float32),
            VMEM((rows // 8, levels, 8, across), jnp.float32),
            VMEM((rows, across), jnp.int32),
            SMEM(speed_table.shape, jnp.float32),
            VMEM((1, levels), jnp.float32),
            VMEM((1, levels), jnp.float32),
            VMEM(sensor_cell.shape, jnp.int32),
            SMEM(sensor_count.shape, jnp.int32),
            VMEM(own.shape, jnp.float32),
            pltpu.SemaphoreType.DMA((7 + 2 * (rows // 8),)),
        ],
        compiler_params=params,
        cost_estimate=pl.CostEstimate(flops=10**9, bytes_accessed=10**7, transcendentals=0),
        name="contract",
    )(
        *[
            pltpu.with_memory_space_constraint(x, pltpu.HBM)
            for x in (
                adjoint_eta, adjoint_flow, depth_class, speed_table, damping[None], profile[None],
                sensor_cell, sensor_count, own,
            )
        ]
    )

    edges = meet(edges, 0)
    relays = pl.pallas_call(
        relay_kernel,
        out_shape=[
            shape(STEPS + ROWS, across) if d == 1 else shape(STEPS, -(-6 * slots // 128) * 128)
            for d in range(1, chips)
        ],
        in_specs=[spec(VMEM)] * 3,
        out_specs=[spec(VMEM)] * (chips - 1),
        compiler_params=params,
        name="relay",
    )(own, edges, outer)
    cross = [meet(relay, d) for d, relay in enumerate(relays, 1)]
    series = pl.pallas_call(
        functools.partial(advance_kernel, blocks),
        out_shape=(shape(STEPS * rows // blocks, across),) * blocks,
        in_specs=[spec(VMEM)] * (7 + len(cross)),
        out_specs=(spec(VMEM),) * blocks,
        scratch_shapes=[
            VMEM((blocks, STEPS * rows // blocks, across), jnp.float32),
            VMEM((len(HALO), tall, across), jnp.float32),
            VMEM((tall, across), jnp.float32),
        ],
        compiler_params=params,
        name="advance",
    )(fields, cel, coef, hot, places, own, edges, *cross)
    gots = swaps(series, "tblock")
    return pl.pallas_call(
        prior_kernel,
        out_shape=shape(STEPS * blocks, rows // blocks, across),
        in_specs=[spec(VMEM)] * blocks + [spec(SMEM)],
        out_specs=spec(VMEM),
        scratch_shapes=[VMEM((blocks, STEPS * rows // blocks, across), jnp.float32)],
        compiler_params=params,
        name="prior",
    )(*reversed(gots), band_weight)


def solution(mesh):
    in_specs = (
        P("tblock", None, "trench", None),
        P("tblock", None, "trench", None),
        P("tblock", "trench", None, None, None),
        P(),
        P(),
        P("trench", None),
        P(),
        P(),
        P(),
        P(),
    )
    out_specs = P(None, ("trench", "tblock"), None)
    return jax.shard_map(body, mesh=mesh, in_specs=in_specs, out_specs=out_specs, check_vma=False)
```

```python
import functools
import math

import jax
import jax.numpy as jnp
from jax import lax
from jax.experimental import pallas as pl
from jax.experimental.pallas import tpu as pltpu
from jax.sharding import PartitionSpec as P

VERT = 0.2
STEPS = 4
PAD = 8
VMEM = pltpu.VMEM
SMEM = pltpu.SMEM
LIMIT = 32 * 1024 * 1024

SHIFT = 1.2

FIELDS = [(4, 4), (4, 3), (4, 2), (3, 2), (4, 1), (3, 1), (2, 1), (4, 0), (3, 0), (2, 0), (1, 0)]
HALO = [4, 3, 2, 2, 1, 1, 1]
HALO_AT = [0, 4, 7, 9, 11, 12, 13]
CEL_AT = 14
CEL_HALO = 3
ROWS = 17


def split(x):
    hi = x.astype(jnp.bfloat16)
    return hi, (x - hi.astype(jnp.float32)).astype(jnp.bfloat16)


def dot(a, b, dims=((1,), (0,))):
    return lax.dot_general(a, b, (dims, ((), ())), preferred_element_type=jnp.float32)


def contract_kernel(
    eta, flow, depth, table, damping, profile, band, residual,
    fields, inner, outer, cel, coef, factor, own,
    eta_v, flow_v, depth_v, table_s, damping_v, profile_v, band_v, sems,
):
    levels, rows, across = eta.shape[1:]
    halves = rows // 8
    copies = []

    def fetch(src, dst):
        copy = pltpu.make_async_copy(src, dst, sems.at[len(copies)])
        copy.start()
        copies.append(copy)
        return copy

    small = [fetch(damping, damping_v), fetch(profile, profile_v), fetch(table, table_s), fetch(depth, depth_v)]
    small += [fetch(band, band_v), fetch(residual, own)]
    large = []
    for h in range(halves):
        cut = pl.ds(8 * h, 8)
        large.append(fetch(eta.at[0, :, cut, :], eta_v.at[h]))
        large.append(fetch(flow.at[0, :, cut, :], flow_v.at[h]))
    for copy in small:
        copy.wait()

    classes = depth_v[...]
    speed = jnp.zeros(classes.shape, jnp.float32)
    for c in range(table_s.shape[0]):
        speed = jnp.where(classes == c, table_s[c], speed)
    cel[...] = speed
    for j in range(factor.shape[0]):
        factor[j : j + 1, :] = jnp.broadcast_to(band_v[:, j : j + 1], (1, across))

    lane = lax.broadcasted_iota(jnp.int32, (8, 128), 1)
    sub = lax.broadcasted_iota(jnp.int32, (8, 128), 0)
    inside = lane < levels
    fill = jnp.zeros((1, 128 - levels), jnp.float32)
    keep = jnp.broadcast_to(jnp.concatenate([damping_v[...], fill], axis=1), (8, 128))
    weight = jnp.broadcast_to(jnp.concatenate([profile_v[...], fill], axis=1), (8, 128))
    u = jnp.zeros((8, 128), jnp.float32)
    v = jnp.where(sub == 0, weight * (1.0 / math.sqrt(levels)), 0.0)
    us, vs = [u], [v]
    for r in range(STEPS):
        s = u + v
        bottom = jnp.sum(jnp.where(lane == levels - 1, s, 0.0), axis=1, keepdims=True)
        coef[8 * r : 8 * r + 8, :] = jnp.broadcast_to(bottom, (8, coef.shape[1]))
        vertical = pltpu.roll(s, 1, 1) + pltpu.roll(s, 127, 1) - 2.0 * s
        u = jnp.where(inside, u + VERT * vertical - SHIFT * s + pltpu.roll(s, 1, 0), 0.0)
        v = s * keep
        us.append(u)
        vs.append(v)

    wide = levels * 8
    spread = (
        lax.broadcasted_iota(jnp.int32, (128, wide), 1) // 8
        == lax.broadcasted_iota(jnp.int32, (128, wide), 0)
    ).astype(jnp.bfloat16)
    count_f = len(FIELDS) + 1
    diagonal = (
        lax.broadcasted_iota(jnp.int32, (8 * count_f, wide), 1) % 8
        == lax.broadcasted_iota(jnp.int32, (8 * count_f, wide), 0) % 8
    )

    def matrix(vectors):
        blocks = [jnp.broadcast_to(vectors[n][k : k + 1, :], (8, 128)) for n, k in FIELDS]
        blocks.append(jnp.zeros((8, 128), jnp.float32))
        hi, lo = split(jnp.concatenate(blocks, axis=0))
        zero = jnp.zeros((8 * count_f, wide), jnp.float32)
        hi = jnp.where(diagonal, dot(hi, spread), zero).astype(jnp.bfloat16)
        lo = jnp.where(diagonal, dot(lo, spread), zero).astype(jnp.bfloat16)
        return hi, jnp.concatenate([hi, lo], axis=0)

    w_eta, both_eta = matrix(us)
    w_flow, both_flow = matrix(vs)

    for h in range(halves):
        large[2 * h].wait()
        hi, lo = split(eta_v[h].reshape(wide, across))
        total = dot(both_eta, hi)
        part = dot(w_eta, lo)
        large[2 * h + 1].wait()
        hi, lo = split(flow_v[h].reshape(wide, across))
        total += dot(both_flow, hi)
        part += dot(w_flow, lo)
        part = part + total[: 8 * count_f] + total[8 * count_f :]
        for f in range(len(FIELDS)):
            fields[f, 8 * h : 8 * h + 8, :] = part[8 * f : 8 * f + 8]

    def edge(out, last):
        for f, width in enumerate(HALO):
            start = rows - width if last else 0
            out[HALO_AT[f] : HALO_AT[f] + width, :] = fields[f, start : start + width, :]
        start = rows - CEL_HALO if last else 0
        out[CEL_AT : CEL_AT + CEL_HALO, :] = cel[start : start + CEL_HALO, :]

    odd = lax.axis_index("trench") % 2

    @pl.when(odd == 0)
    def _():
        edge(inner, True)
        edge(outer, False)

    @pl.when(odd == 1)
    def _():
        edge(inner, False)
        edge(outer, True)


def met(me, d, tiles):
    odd = me % 2
    chip = (me // 2 + jnp.where(odd == 1, d, tiles // 2 - d)) % (tiles // 2)
    return jnp.where(d == 0, me, 2 * chip + 1 - odd)


def sources(me, tiles):
    return [met(me, d, tiles) ^ core for d in range(tiles // 2) for core in range(2)]


def residual_rows(owner, own):
    tiles = own.shape[0]
    return jnp.concatenate([own[jnp.clip(owner + d - 1, 0, tiles - 1)] for d in range(3)], axis=1)


def both_rows(owner, own, partner):
    return jnp.concatenate([residual_rows(owner, own), residual_rows(owner, partner)], axis=1)


def relay_kernel(own, partner, outer, *outs):
    me = lax.axis_index("trench")
    tiles = own.shape[0]
    for d, out in enumerate(outs, 1):
        values = both_rows(met(me, d, tiles), own, partner)
        fill = jnp.zeros((STEPS, out.shape[1] - values.shape[1]), jnp.float32)
        out[0:STEPS, :] = jnp.concatenate([values, fill], axis=1)
        if d == 1:
            out[STEPS : STEPS + ROWS, :] = outer[...]


def sensors_kernel(rows, cells, count, hot, places):
    me = lax.axis_index("trench")
    tiles, _, slots = cells.shape
    across = hot.shape[0]
    slot = lax.broadcasted_iota(jnp.int32, (1, slots), 1)
    listed = []
    for source in sources(me, tiles):
        for d in range(3):
            owner = me + d - 1
            inside = (owner >= 0) & (owner < tiles)
            owner = jnp.clip(owner, 0, tiles - 1)
            live = jnp.where(inside, count[source, owner], 0)
            listed.append(jnp.where(slot < live, cells[source, pl.ds(owner, 1), :], -1))
    listed = jnp.concatenate(listed, axis=1)
    tile = (lax.broadcasted_iota(jnp.int32, listed.shape, 1) // slots) % 3
    bits = across.bit_length() - 1
    at = jnp.where(listed < 0, -1, (listed >> bits) + (rows * (tile - 1) + PAD))
    places[...] = jnp.broadcast_to(at, places.shape)
    columns = listed & (across - 1)
    hot[...] = jnp.where(lax.broadcasted_iota(jnp.int32, hot.shape, 0) == columns, 1.0, 0.0).astype(jnp.bfloat16)


def advance_kernel(blocks, fields, cel, coef, hot, places, own, partner, facing_in, *refs):
    cross, outs, (stage, ext, cel_ext) = refs[: -3 - blocks], refs[-3 - blocks : -3], refs[-3:]
    me = lax.axis_index("trench")
    tiles = own.shape[0]
    rows, across = cel.shape
    tall = rows + 2 * PAD
    part = rows // blocks
    odd = me % 2 == 1
    facing = me // 2 + jnp.where(odd, 1, -1)
    inner = facing_in[...]
    outer = jnp.zeros(inner.shape, jnp.float32)
    if cross:
        outer = jnp.where((facing >= 0) & (facing < tiles // 2), cross[0][STEPS : STEPS + ROWS, :], outer)
    before = jnp.where(odd, inner, outer)
    after = jnp.where(odd, outer, inner)

    per = 6 * own.shape[2]
    values = [both_rows(me, own, partner)] + [got[0:STEPS, 0:per] for got in cross]
    values = jnp.concatenate(values, axis=1)
    here = lax.broadcasted_iota(jnp.int32, (tall, values.shape[1]), 0) == places[0:1, :]
    left = jnp.concatenate([jnp.where(here, values[t : t + 1, :], 0.0) for t in range(STEPS)], axis=0)
    planes = dot(jnp.concatenate(split(left), axis=0), hot[...], ((1,), (1,)))
    planes = planes[: STEPS * tall] + planes[STEPS * tall :]
    inject = [planes[tall * t : tall * t + tall] for t in range(STEPS)]

    def extend(store, own, at, width):
        store(0, PAD, jnp.zeros((PAD, across), jnp.float32))
        store(PAD + rows, tall, jnp.zeros((PAD, across), jnp.float32))
        store(PAD, PAD + rows, own)
        store(PAD - width, PAD, before[at : at + width])
        store(PAD + rows, PAD + rows + width, after[at : at + width])

    for f, width in enumerate(HALO):
        def store(a, b, value, f=f):
            ext[f, a:b, :] = value
        extend(store, fields[f], HALO_AT[f], width)

    def store_cel(a, b, value):
        cel_ext[a:b, :] = value
    extend(store_cel, cel[...], CEL_AT, CEL_HALO)

    lane = lax.broadcasted_iota(jnp.int32, (tall, across), 1)
    first = lane == 0
    last = lane == across - 1
    speed = cel_ext[...]

    def horizontal(z):
        around = pltpu.roll(z, 1, 0) + pltpu.roll(z, tall - 1, 0)
        around += jnp.where(first, 0.0, pltpu.roll(z, 1, 1))
        around += jnp.where(last, 0.0, pltpu.roll(z, across - 1, 1))
        return speed * (around - 4.0 * z) + SHIFT * z

    def injected(n, k, a, b):
        total = None
        for tau in range(1, n - k + 1):
            r = n - tau
            term = coef[8 * r + k : 8 * r + k + 1, :] * inject[STEPS - tau][a:b]
            total = term if total is None else total + term
        return total

    base = horizontal(ext[0])
    for n in range(1, STEPS + 1):
        z = base
        for k in range(n - 1, 0, -1):
            z = horizontal(z + ext[FIELDS.index((n, k))] + injected(n, k, 0, tall))
        own = z[PAD : PAD + rows] + fields[FIELDS.index((n, 0))] + injected(n, 0, PAD, PAD + rows)
        t = STEPS - n
        for b in range(blocks):
            stage[b, part * t : part * t + part, :] = own[part * b : part * b + part]
    block = lax.axis_index("tblock")
    for r, out in enumerate(outs):
        out[...] = stage[block ^ r]


def prior_kernel(*refs):
    gots, (weight, out, whole, done, sems) = refs[:-5], refs[-5:]
    block = lax.axis_index("tblock")
    for r, got in enumerate(reversed(gots)):
        whole[block ^ r] = got[...]
    part = out.shape[1]
    length = out.shape[0]
    width = weight.shape[0]
    factor = [weight[j : j + 1, :] for j in range(width)]
    copies = []

    def finish(p):
        if (p + 1) % (length // 4) == 0:
            cut = pl.ds(p + 1 - length // 4, length // 4)
            copies.append(pltpu.make_async_copy(done.at[cut], out.at[cut], sems.at[len(copies)]))
            copies[-1].start()

    if 2 * part != 8:
        series = [whole[i // STEPS, part * (i % STEPS) : part * (i % STEPS) + part, :] for i in range(length)]
        for k in range(length):
            done[k] = sum(factor[j] * series[k + j] for j in range(min(width, length - k)))
            finish(k)
        for copy in copies:
            copy.wait()
        return
    pairs = length // 2
    even = [whole[p // 2, 8 * (p % 2) : 8 * (p % 2) + 8, :] for p in range(pairs)]
    half = lax.broadcasted_iota(jnp.int32, even[0].shape, 0) < part
    turned = [pltpu.roll(x, part, 0) for x in even] + [jnp.zeros(even[0].shape, jnp.float32)]
    odd = [jnp.where(half, turned[p], turned[p + 1]) for p in range(pairs)]
    for p in range(pairs):
        total = None
        for j in range(width):
            if p + j // 2 < pairs:
                term = factor[j] * (odd if j % 2 else even)[p + j // 2]
                total = term if total is None else total + term
        done[2 * p] = total[:part]
        done[2 * p + 1] = total[part:]
        finish(2 * p + 1)
    for copy in copies:
        copy.wait()


def shape(*dims, dtype=jnp.float32):
    return jax.ShapeDtypeStruct(dims, dtype)


def spec(space):
    return pl.BlockSpec(memory_space=space)


def body(
    adjoint_eta,
    adjoint_flow,
    residual,
    sensor_cell,
    sensor_count,
    depth_class,
    speed_table,
    damping,
    profile,
    band_weight,
):
    tiles = lax.axis_size("trench")
    blocks = lax.axis_size("tblock")
    levels, rows, across = adjoint_eta.shape[1:]
    tall = rows + 2 * PAD
    params = pltpu.CompilerParams(vmem_limit_bytes=LIMIT)

    def swaps(parts, axis):
        devices = lax.axis_size(axis)
        moved = {r: lax.ppermute(parts[r], axis, [(i, i ^ r) for i in range(devices)]) for r in range(devices - 1, 0, -1)}
        return [parts[0]] + [moved[r] for r in range(1, devices)]

    own = residual[0, 0]
    slots = own.shape[2]
    lanes = 3 * tiles * slots

    chips = tiles // 2

    def meet(x, d):
        pairs = [(2 * c + 1, 2 * ((c + d) % chips)) for c in range(chips)]
        return lax.ppermute(x, "trench", pairs + [(j, i) for i, j in pairs])

    partner = meet(own, 0)
    fields, inner, outer, cel, coef, factor, own = pl.pallas_call(
        contract_kernel,
        out_shape=(
            shape(len(FIELDS), rows, across),
            shape(ROWS, across),
            shape(ROWS, across),
            shape(rows, across),
            shape(8 * STEPS, across),
            shape(band_weight.shape[0], across),
            shape(*own.shape),
        ),
        in_specs=[spec(pltpu.HBM)] * 8,
        out_specs=(spec(VMEM),) * 7,
        scratch_shapes=[
            VMEM((rows // 8, levels, 8, across), jnp.float32),
            VMEM((rows // 8, levels, 8, across), jnp.float32),
            VMEM((rows, across), jnp.int32),
            SMEM(speed_table.shape, jnp.float32),
            VMEM((1, levels), jnp.float32),
            VMEM((1, levels), jnp.float32),
            VMEM((1, band_weight.shape[0]), jnp.float32),
            pltpu.SemaphoreType.DMA((6 + 2 * (rows // 8),)),
        ],
        compiler_params=params,
        cost_estimate=pl.CostEstimate(flops=10**9, bytes_accessed=10**7, transcendentals=0),
        name="contract",
    )(
        *[
            pltpu.with_memory_space_constraint(x, pltpu.HBM)
            for x in (
                adjoint_eta, adjoint_flow, depth_class, speed_table, damping[None], profile[None],
                band_weight[None], own,
            )
        ]
    )
    facing_in = meet(inner, 0)
    relays = pl.pallas_call(
        relay_kernel,
        out_shape=[
            shape(STEPS + ROWS, across) if d == 1 else shape(STEPS, -(-6 * slots // 128) * 128)
            for d in range(1, chips)
        ],
        in_specs=[spec(VMEM)] * 3,
        out_specs=[spec(VMEM)] * (chips - 1),
        compiler_params=params,
        name="relay",
    )(own, partner, outer)
    cross = [meet(relay, d) for d, relay in enumerate(relays, 1)]
    hot, places = pl.pallas_call(
        functools.partial(sensors_kernel, rows),
        out_shape=(shape(across, lanes, dtype=jnp.bfloat16), shape(8, lanes, dtype=jnp.int32)),
        in_specs=[spec(VMEM), spec(SMEM)],
        out_specs=(spec(VMEM),) * 2,
        compiler_params=params,
        cost_estimate=pl.CostEstimate(flops=10**6, bytes_accessed=2 * 10**6, transcendentals=0),
        name="sensors",
    )(sensor_cell, sensor_count)
    series = pl.pallas_call(
        functools.partial(advance_kernel, blocks),
        out_shape=(shape(STEPS * rows // blocks, across),) * blocks,
        in_specs=[spec(VMEM)] * (8 + len(cross)),
        out_specs=(spec(VMEM),) * blocks,
        scratch_shapes=[
            VMEM((blocks, STEPS * rows // blocks, across), jnp.float32),
            VMEM((len(HALO), tall, across), jnp.float32),
            VMEM((tall, across), jnp.float32),
        ],
        compiler_params=params,
        name="advance",
    )(fields, cel, coef, hot, places, own, partner, facing_in, *cross)
    gots = swaps(series, "tblock")
    return pl.pallas_call(
        prior_kernel,
        out_shape=shape(STEPS * blocks, rows // blocks, across),
        in_specs=[spec(VMEM)] * (blocks + 1),
        out_specs=spec(pl.ANY),
        scratch_shapes=[
            VMEM((blocks, STEPS * rows // blocks, across), jnp.float32),
            VMEM((STEPS * blocks, rows // blocks, across), jnp.float32),
            pltpu.SemaphoreType.DMA((4,)),
        ],
        compiler_params=params,
        name="prior",
    )(*reversed(gots), factor)


def solution(mesh):
    in_specs = (
        P("tblock", None, "trench", None),
        P("tblock", None, "trench", None),
        P("tblock", "trench", None, None, None),
        P(),
        P(),
        P("trench", None),
        P(),
        P(),
        P(),
        P(),
    )
    out_specs = P(None, ("trench", "tblock"), None)
    return jax.shard_map(body, mesh=mesh, in_specs=in_specs, out_specs=out_specs, check_vma=False)
```

```python
import functools
import math

import jax
import jax.numpy as jnp
from jax import lax
from jax.experimental import pallas as pl
from jax.experimental.pallas import tpu as pltpu
from jax.sharding import PartitionSpec as P

VERT = 0.2
STEPS = 4
PAD = 8
VMEM = pltpu.VMEM
SMEM = pltpu.SMEM
LIMIT = 32 * 1024 * 1024

SHIFT = 1.2

FIELDS = [(4, 4), (4, 3), (4, 2), (3, 2), (4, 1), (3, 1), (2, 1), (4, 0), (3, 0), (2, 0), (1, 0)]
HALO = [4, 3, 2, 2, 1, 1, 1]
HALO_AT = [0, 4, 7, 9, 11, 12, 13]
CEL_AT = 14
CEL_HALO = 3
ROWS = 17


def split(x):
    hi = x.astype(jnp.bfloat16)
    return hi, (x - hi.astype(jnp.float32)).astype(jnp.bfloat16)


def dot(a, b, dims=((1,), (0,))):
    return lax.dot_general(a, b, (dims, ((), ())), preferred_element_type=jnp.float32)


def prepare_kernel(
    depth, table, damping, profile, band, cells, count, residual, eta, flow,
    w_eta, w_flow, cel, coef, factor, hot, places, hot_next, places_next, own, eta_v, flow_v,
    depth_v, table_s, damping_v, profile_v, band_v, cells_v, count_s, sems,
):
    rows, across = cel.shape
    levels = damping.shape[1]
    copies = [
        pltpu.make_async_copy(src, dst, sems.at[i])
        for i, (src, dst) in enumerate((
            (damping, damping_v), (profile, profile_v), (table, table_s), (depth, depth_v),
            (band, band_v), (cells, cells_v), (count, count_s), (residual, own), (eta, eta_v), (flow, flow_v),
        ))
    ]
    for copy in copies:
        copy.start()
    for copy in copies[:-2]:
        copy.wait()

    classes = depth_v[...]
    speed = jnp.zeros(classes.shape, jnp.float32)
    for c in range(table_s.shape[0]):
        speed = jnp.where(classes == c, table_s[c], speed)
    cel[...] = speed
    for j in range(factor.shape[0]):
        factor[j : j + 1, :] = jnp.broadcast_to(band_v[:, j : j + 1], (1, across))

    lane = lax.broadcasted_iota(jnp.int32, (8, 128), 1)
    sub = lax.broadcasted_iota(jnp.int32, (8, 128), 0)
    inside = lane < levels
    fill = jnp.zeros((1, 128 - levels), jnp.float32)
    keep = jnp.broadcast_to(jnp.concatenate([damping_v[...], fill], axis=1), (8, 128))
    weight = jnp.broadcast_to(jnp.concatenate([profile_v[...], fill], axis=1), (8, 128))
    u = jnp.zeros((8, 128), jnp.float32)
    v = jnp.where(sub == 0, weight * (1.0 / math.sqrt(levels)), 0.0)
    us, vs = [u], [v]
    for r in range(STEPS):
        s = u + v
        bottom = jnp.sum(jnp.where(lane == levels - 1, s, 0.0), axis=1, keepdims=True)
        coef[8 * r : 8 * r + 8, :] = jnp.broadcast_to(bottom, (8, coef.shape[1]))
        vertical = pltpu.roll(s, 1, 1) + pltpu.roll(s, 127, 1) - 2.0 * s
        u = jnp.where(inside, u + VERT * vertical - SHIFT * s + pltpu.roll(s, 1, 0), 0.0)
        v = s * keep
        us.append(u)
        vs.append(v)

    wide = w_eta.shape[1]
    spread = (
        lax.broadcasted_iota(jnp.int32, (128, wide), 1) // 8
        == lax.broadcasted_iota(jnp.int32, (128, wide), 0)
    ).astype(jnp.bfloat16)
    count_f = len(FIELDS) + 1
    diagonal = (
        lax.broadcasted_iota(jnp.int32, (8 * count_f, wide), 1) % 8
        == lax.broadcasted_iota(jnp.int32, (8 * count_f, wide), 0) % 8
    )

    def matrix(vectors):
        blocks = [jnp.broadcast_to(vectors[n][k : k + 1, :], (8, 128)) for n, k in FIELDS]
        blocks.append(jnp.zeros((8, 128), jnp.float32))
        hi, lo = split(jnp.concatenate(blocks, axis=0))
        zero = jnp.zeros((8 * count_f, wide), jnp.float32)
        hi = jnp.where(diagonal, dot(hi, spread), zero).astype(jnp.bfloat16)
        lo = jnp.where(diagonal, dot(lo, spread), zero).astype(jnp.bfloat16)
        return jnp.concatenate([hi, lo], axis=0)

    w_eta[...] = matrix(us)
    w_flow[...] = matrix(vs)

    me = lax.axis_index("trench")
    tiles, _, slots = cells_v.shape
    slot = lax.broadcasted_iota(jnp.int32, (1, slots), 1)
    bits = across.bit_length() - 1

    def list_slots(ds, hot, places):
        listed = []
        for source in sources(me, tiles, ds):
            for d in range(3):
                owner = me + d - 1
                inside = (owner >= 0) & (owner < tiles)
                owner = jnp.clip(owner, 0, tiles - 1)
                live = jnp.where(inside, count_s[source, owner], 0)
                listed.append(jnp.where(slot < live, cells_v[source, pl.ds(owner, 1), :], -1))
        listed = jnp.concatenate(listed, axis=1)
        tile = (lax.broadcasted_iota(jnp.int32, listed.shape, 1) // slots) % 3
        at = jnp.where(listed < 0, -1, (listed >> bits) + (rows * (tile - 1) + PAD))
        places[...] = jnp.broadcast_to(at, places.shape)
        columns = listed & (across - 1)
        hot[...] = jnp.where(lax.broadcasted_iota(jnp.int32, hot.shape, 0) == columns, 1.0, 0.0).astype(jnp.bfloat16)

    list_slots([0] + list(range(2, tiles // 2)), hot, places)
    list_slots([1], hot_next, places_next)
    for copy in copies[-2:]:
        copy.wait()


def contract_kernel(eta, flow, w_eta, w_flow, cel, own, partner, after, fields, inner, outer):
    levels, rows, across = eta.shape[1:]
    wide = w_eta.shape[1]
    half = w_eta.shape[0] // 2
    for h in range(rows // 8):
        hi, lo = split(eta[0, :, 8 * h : 8 * h + 8, :].reshape(wide, across))
        total = dot(w_eta[...], hi)
        part = dot(w_eta[0:half, :], lo)
        hi, lo = split(flow[0, :, 8 * h : 8 * h + 8, :].reshape(wide, across))
        total += dot(w_flow[...], hi)
        part += dot(w_flow[0:half, :], lo)
        part = part + total[:half] + total[half:]
        for f in range(len(FIELDS)):
            fields[f, 8 * h : 8 * h + 8, :] = part[8 * f : 8 * f + 8]

    me = lax.axis_index("trench")
    values = both_rows(met(me, 1, own.shape[0]), own, partner)
    fill = jnp.zeros((STEPS, across - values.shape[1]), jnp.float32)
    outer[0:STEPS, :] = jnp.concatenate([values, fill], axis=1)

    def edge(out, at, last):
        for f, width in enumerate(HALO):
            start = rows - width if last else 0
            out[at + HALO_AT[f] : at + HALO_AT[f] + width, :] = fields[f, start : start + width, :]
        start = rows - CEL_HALO if last else 0
        out[at + CEL_AT : at + CEL_AT + CEL_HALO, :] = cel[start : start + CEL_HALO, :]

    @pl.when(me % 2 == 0)
    def _():
        edge(inner, 0, True)
        edge(outer, STEPS, False)

    @pl.when(me % 2 == 1)
    def _():
        edge(inner, 0, False)
        edge(outer, STEPS, True)


def met(me, d, tiles):
    odd = me % 2
    chip = (me // 2 + jnp.where(odd == 1, d, tiles // 2 - d)) % (tiles // 2)
    return jnp.where(d == 0, me, 2 * chip + 1 - odd)


def sources(me, tiles, ds):
    return [met(me, d, tiles) ^ core for d in ds for core in range(2)]


def residual_rows(owner, own):
    tiles = own.shape[0]
    return jnp.concatenate([own[jnp.clip(owner + d - 1, 0, tiles - 1)] for d in range(3)], axis=1)


def both_rows(owner, own, partner):
    return jnp.concatenate([residual_rows(owner, own), residual_rows(owner, partner)], axis=1)


def relay_kernel(own, partner, *outs):
    me = lax.axis_index("trench")
    for d, out in enumerate(outs, 2):
        values = both_rows(met(me, d, own.shape[0]), own, partner)
        fill = jnp.zeros((STEPS, out.shape[1] - values.shape[1]), jnp.float32)
        out[...] = jnp.concatenate([values, fill], axis=1)


def planes_of(values, hot, places, tall):
    here = lax.broadcasted_iota(jnp.int32, (tall, values.shape[1]), 0) == places[0:1, :]
    left = jnp.concatenate([jnp.where(here, values[t : t + 1, :], 0.0) for t in range(STEPS)], axis=0)
    both = dot(jnp.concatenate(split(left), axis=0), hot[...], ((1,), (1,)))
    return both[: STEPS * tall] + both[STEPS * tall :]


def inject_kernel(hot, places, own, partner, *refs):
    far, planes = refs[:-1], refs[-1]
    per = 6 * own.shape[2]
    values = [both_rows(lax.axis_index("trench"), own, partner)] + [got[:, 0:per] for got in far]
    planes[...] = planes_of(jnp.concatenate(values, axis=1), hot, places, planes.shape[0] // STEPS)


def advance_kernel(slots, tiles, fields, cel, coef, hot, places, facing_in, facing_out, planes, *refs):
    outs, (stage, ext, cel_ext) = refs[:-3], refs[-3:]
    blocks = len(outs)
    me = lax.axis_index("trench")
    rows, across = cel.shape
    tall = rows + 2 * PAD
    part = rows // blocks
    odd = me % 2 == 1
    facing = me // 2 + jnp.where(odd, 1, -1)
    inner = facing_in[...]
    outer = jnp.where((facing >= 0) & (facing < tiles // 2), facing_out[STEPS : STEPS + ROWS, :], 0.0)
    before = jnp.where(odd, inner, outer)
    after = jnp.where(odd, outer, inner)

    all_planes = planes[...] + planes_of(facing_out[0:STEPS, 0 : 6 * slots], hot, places, tall)
    inject = [all_planes[tall * t : tall * t + tall] for t in range(STEPS)]

    def extend(store, own, at, width):
        store(0, PAD, jnp.zeros((PAD, across), jnp.float32))
        store(PAD + rows, tall, jnp.zeros((PAD, across), jnp.float32))
        store(PAD, PAD + rows, own)
        store(PAD - width, PAD, before[at : at + width])
        store(PAD + rows, PAD + rows + width, after[at : at + width])

    for f, width in enumerate(HALO):
        def store(a, b, value, f=f):
            ext[f, a:b, :] = value
        extend(store, fields[f], HALO_AT[f], width)

    def store_cel(a, b, value):
        cel_ext[a:b, :] = value
    extend(store_cel, cel[...], CEL_AT, CEL_HALO)

    lane = lax.broadcasted_iota(jnp.int32, (tall, across), 1)
    first = lane == 0
    last = lane == across - 1
    speed = cel_ext[...]

    def horizontal(z):
        around = pltpu.roll(z, 1, 0) + pltpu.roll(z, tall - 1, 0)
        around += jnp.where(first, 0.0, pltpu.roll(z, 1, 1))
        around += jnp.where(last, 0.0, pltpu.roll(z, across - 1, 1))
        return speed * (around - 4.0 * z) + SHIFT * z

    def injected(n, k, a, b):
        total = None
        for tau in range(1, n - k + 1):
            r = n - tau
            term = coef[8 * r + k : 8 * r + k + 1, :] * inject[STEPS - tau][a:b]
            total = term if total is None else total + term
        return total

    base = horizontal(ext[0])
    for n in range(1, STEPS + 1):
        z = base
        for k in range(n - 1, 0, -1):
            z = horizontal(z + ext[FIELDS.index((n, k))] + injected(n, k, 0, tall))
        own = z[PAD : PAD + rows] + fields[FIELDS.index((n, 0))] + injected(n, 0, PAD, PAD + rows)
        t = STEPS - n
        for b in range(blocks):
            stage[b, part * t : part * t + part, :] = own[part * b : part * b + part]
    block = lax.axis_index("tblock")
    for r, out in enumerate(outs):
        out[...] = stage[block ^ r]


def prior_kernel(*refs):
    gots, (weight, out, whole, done, sems) = refs[:-5], refs[-5:]
    block = lax.axis_index("tblock")
    for r, got in enumerate(reversed(gots)):
        whole[block ^ r] = got[...]
    part = out.shape[1]
    length = out.shape[0]
    width = weight.shape[0]
    factor = [weight[j : j + 1, :] for j in range(width)]
    copies = []

    def finish(p):
        if (p + 1) % (length // 4) == 0:
            cut = pl.ds(p + 1 - length // 4, length // 4)
            copies.append(pltpu.make_async_copy(done.at[cut], out.at[cut], sems.at[len(copies)]))
            copies[-1].start()

    if 2 * part != 8:
        series = [whole[i // STEPS, part * (i % STEPS) : part * (i % STEPS) + part, :] for i in range(length)]
        for k in range(length):
            done[k] = sum(factor[j] * series[k + j] for j in range(min(width, length - k)))
            finish(k)
        for copy in copies:
            copy.wait()
        return
    pairs = length // 2
    even = [whole[p // 2, 8 * (p % 2) : 8 * (p % 2) + 8, :] for p in range(pairs)]
    half = lax.broadcasted_iota(jnp.int32, even[0].shape, 0) < part
    turned = [pltpu.roll(x, part, 0) for x in even] + [jnp.zeros(even[0].shape, jnp.float32)]
    odd = [jnp.where(half, turned[p], turned[p + 1]) for p in range(pairs)]
    for p in range(pairs):
        total = None
        for j in range(width):
            if p + j // 2 < pairs:
                term = factor[j] * (odd if j % 2 else even)[p + j // 2]
                total = term if total is None else total + term
        done[2 * p] = total[:part]
        done[2 * p + 1] = total[part:]
        finish(2 * p + 1)
    for copy in copies:
        copy.wait()


def shape(*dims, dtype=jnp.float32):
    return jax.ShapeDtypeStruct(dims, dtype)


def spec(space):
    return pl.BlockSpec(memory_space=space)


def body(
    adjoint_eta,
    adjoint_flow,
    residual,
    sensor_cell,
    sensor_count,
    depth_class,
    speed_table,
    damping,
    profile,
    band_weight,
):
    tiles = lax.axis_size("trench")
    blocks = lax.axis_size("tblock")
    levels, rows, across = adjoint_eta.shape[1:]
    tall = rows + 2 * PAD
    params = pltpu.CompilerParams(vmem_limit_bytes=LIMIT)

    def swaps(parts, axis):
        devices = lax.axis_size(axis)
        moved = {r: lax.ppermute(parts[r], axis, [(i, i ^ r) for i in range(devices)]) for r in range(devices - 1, 0, -1)}
        return [parts[0]] + [moved[r] for r in range(1, devices)]

    own = residual[0, 0]
    slots = own.shape[2]
    chips = tiles // 2

    def meet(x, d):
        pairs = [(2 * c + 1, 2 * ((c + d) % chips)) for c in range(chips)]
        return lax.ppermute(x, "trench", pairs + [(j, i) for i, j in pairs])

    partner = meet(own, 0)
    matrix = shape(16 * (len(FIELDS) + 1), 8 * levels, dtype=jnp.bfloat16)
    w_eta, w_flow, cel, coef, factor, hot, places, hot_next, places_next, own, eta, flow = pl.pallas_call(
        prepare_kernel,
        out_shape=(
            matrix,
            matrix,
            shape(rows, across),
            shape(8 * STEPS, across),
            shape(band_weight.shape[0], across),
            shape(across, 6 * slots * (chips - 1), dtype=jnp.bfloat16),
            shape(8, 6 * slots * (chips - 1), dtype=jnp.int32),
            shape(across, 6 * slots, dtype=jnp.bfloat16),
            shape(8, 6 * slots, dtype=jnp.int32),
            shape(*own.shape),
            shape(*adjoint_eta.shape),
            shape(*adjoint_flow.shape),
        ),
        in_specs=[spec(pltpu.HBM)] * 10,
        out_specs=(spec(VMEM),) * 12,
        scratch_shapes=[
            VMEM((rows, across), jnp.int32),
            SMEM(speed_table.shape, jnp.float32),
            VMEM((1, levels), jnp.float32),
            VMEM((1, levels), jnp.float32),
            VMEM((1, band_weight.shape[0]), jnp.float32),
            VMEM(sensor_cell.shape, jnp.int32),
            SMEM(sensor_count.shape, jnp.int32),
            pltpu.SemaphoreType.DMA((10,)),
        ],
        compiler_params=params,
        cost_estimate=pl.CostEstimate(flops=10**7, bytes_accessed=4 * 10**6, transcendentals=0),
        name="prepare",
    )(
        *[
            pltpu.with_memory_space_constraint(x, pltpu.HBM)
            for x in (
                depth_class, speed_table, damping[None], profile[None], band_weight[None],
                sensor_cell, sensor_count, own, adjoint_eta, adjoint_flow,
            )
        ]
    )
    relays = pl.pallas_call(
        relay_kernel,
        out_shape=[shape(STEPS, -(-6 * slots // 128) * 128)] * (chips - 2),
        in_specs=[spec(VMEM)] * 2,
        out_specs=[spec(VMEM)] * (chips - 2),
        compiler_params=params,
        name="relay",
    )(own, partner)
    far = [meet(relay, d) for d, relay in enumerate(relays, 2)]
    fields, inner, outer = pl.pallas_call(
        contract_kernel,
        out_shape=(
            shape(len(FIELDS), rows, across),
            shape(ROWS, across),
            shape(STEPS + ROWS, across),
        ),
        in_specs=[spec(VMEM)] * 7 + [spec(pl.ANY)],
        out_specs=(spec(VMEM),) * 3,
        compiler_params=params,
        cost_estimate=pl.CostEstimate(flops=10**9, bytes_accessed=4 * 10**6, transcendentals=0),
        name="contract",
    )(eta, flow, w_eta, w_flow, cel, own, partner, relays[0])
    facing_out = meet(outer, 1)
    facing_in = meet(inner, 0)
    planes = pl.pallas_call(
        inject_kernel,
        out_shape=shape(STEPS * (rows + 2 * PAD), across),
        in_specs=[spec(VMEM)] * (4 + len(far)),
        out_specs=spec(VMEM),
        compiler_params=params,
        cost_estimate=pl.CostEstimate(flops=10**8, bytes_accessed=4 * 10**6, transcendentals=0),
        name="inject",
    )(hot, places, own, partner, *far)
    series = pl.pallas_call(
        functools.partial(advance_kernel, slots, tiles),
        out_shape=(shape(STEPS * rows // blocks, across),) * blocks,
        in_specs=[spec(VMEM)] * 8,
        out_specs=(spec(VMEM),) * blocks,
        scratch_shapes=[
            VMEM((blocks, STEPS * rows // blocks, across), jnp.float32),
            VMEM((len(HALO), tall, across), jnp.float32),
            VMEM((tall, across), jnp.float32),
        ],
        compiler_params=params,
        name="advance",
    )(fields, cel, coef, hot_next, places_next, facing_in, facing_out, planes)
    gots = swaps(series, "tblock")
    return pl.pallas_call(
        prior_kernel,
        out_shape=shape(STEPS * blocks, rows // blocks, across),
        in_specs=[spec(VMEM)] * (blocks + 1),
        out_specs=spec(pl.ANY),
        scratch_shapes=[
            VMEM((blocks, STEPS * rows // blocks, across), jnp.float32),
            VMEM((STEPS * blocks, rows // blocks, across), jnp.float32),
            pltpu.SemaphoreType.DMA((4,)),
        ],
        compiler_params=params,
        name="prior",
    )(*reversed(gots), factor)


def solution(mesh):
    in_specs = (
        P("tblock", None, "trench", None),
        P("tblock", None, "trench", None),
        P("tblock", "trench", None, None, None),
        P(),
        P(),
        P("trench", None),
        P(),
        P(),
        P(),
        P(),
    )
    out_specs = P(None, ("trench", "tblock"), None)
    return jax.shard_map(body, mesh=mesh, in_specs=in_specs, out_specs=out_specs, check_vma=False)
```

```python
import functools
import math

import jax
import jax.numpy as jnp
from jax import lax
from jax.experimental import pallas as pl
from jax.experimental.pallas import tpu as pltpu
from jax.sharding import PartitionSpec as P

VERT = 0.2
STEPS = 4
PAD = 8
VMEM = pltpu.VMEM
SMEM = pltpu.SMEM
LIMIT = 32 * 1024 * 1024

SHIFT = 1.2

FIELDS = [(4, 4), (4, 3), (4, 2), (3, 2), (4, 1), (3, 1), (2, 1), (4, 0), (3, 0), (2, 0), (1, 0)]
HALO = [4, 3, 2, 2, 1, 1, 1]
HALO_AT = [0, 4, 7, 9, 11, 12, 13]
CEL_AT = 14
CEL_HALO = 3
ROWS = 17


def split(x):
    hi = x.astype(jnp.bfloat16)
    return hi, (x - hi.astype(jnp.float32)).astype(jnp.bfloat16)


def dot(a, b, dims=((1,), (0,))):
    return lax.dot_general(a, b, (dims, ((), ())), preferred_element_type=jnp.float32)


def prepare_kernel(
    depth, table, damping, profile, band, residual, eta, flow,
    w_eta, w_flow, cel, coef, factor, own, eta_v, flow_v,
    depth_v, table_s, damping_v, profile_v, band_v, sems,
):
    rows, across = cel.shape
    levels = damping.shape[1]
    copies = [
        pltpu.make_async_copy(src, dst, sems.at[i])
        for i, (src, dst) in enumerate((
            (damping, damping_v), (profile, profile_v), (table, table_s), (depth, depth_v),
            (band, band_v), (residual, own), (eta, eta_v), (flow, flow_v),
        ))
    ]
    for copy in copies:
        copy.start()
    for copy in copies[:-2]:
        copy.wait()

    classes = depth_v[...]
    speed = jnp.zeros(classes.shape, jnp.float32)
    for c in range(table_s.shape[0]):
        speed = jnp.where(classes == c, table_s[c], speed)
    cel[...] = speed
    for j in range(factor.shape[0]):
        factor[j : j + 1, :] = jnp.broadcast_to(band_v[:, j : j + 1], (1, across))

    lane = lax.broadcasted_iota(jnp.int32, (8, 128), 1)
    sub = lax.broadcasted_iota(jnp.int32, (8, 128), 0)
    inside = lane < levels
    fill = jnp.zeros((1, 128 - levels), jnp.float32)
    keep = jnp.broadcast_to(jnp.concatenate([damping_v[...], fill], axis=1), (8, 128))
    weight = jnp.broadcast_to(jnp.concatenate([profile_v[...], fill], axis=1), (8, 128))
    u = jnp.zeros((8, 128), jnp.float32)
    v = jnp.where(sub == 0, weight * (1.0 / math.sqrt(levels)), 0.0)
    us, vs = [u], [v]
    for r in range(STEPS):
        s = u + v
        bottom = jnp.sum(jnp.where(lane == levels - 1, s, 0.0), axis=1, keepdims=True)
        coef[8 * r : 8 * r + 8, :] = jnp.broadcast_to(bottom, (8, coef.shape[1]))
        vertical = pltpu.roll(s, 1, 1) + pltpu.roll(s, 127, 1) - 2.0 * s
        u = jnp.where(inside, u + VERT * vertical - SHIFT * s + pltpu.roll(s, 1, 0), 0.0)
        v = s * keep
        us.append(u)
        vs.append(v)

    wide = w_eta.shape[1]
    spread = (
        lax.broadcasted_iota(jnp.int32, (128, wide), 1) // 8
        == lax.broadcasted_iota(jnp.int32, (128, wide), 0)
    ).astype(jnp.bfloat16)
    count_f = len(FIELDS) + 1
    diagonal = (
        lax.broadcasted_iota(jnp.int32, (8 * count_f, wide), 1) % 8
        == lax.broadcasted_iota(jnp.int32, (8 * count_f, wide), 0) % 8
    )

    def matrix(vectors):
        blocks = [jnp.broadcast_to(vectors[n][k : k + 1, :], (8, 128)) for n, k in FIELDS]
        blocks.append(jnp.zeros((8, 128), jnp.float32))
        hi, lo = split(jnp.concatenate(blocks, axis=0))
        zero = jnp.zeros((8 * count_f, wide), jnp.float32)
        hi = jnp.where(diagonal, dot(hi, spread), zero).astype(jnp.bfloat16)
        lo = jnp.where(diagonal, dot(lo, spread), zero).astype(jnp.bfloat16)
        return jnp.concatenate([hi, lo], axis=0)

    w_eta[...] = matrix(us)
    w_flow[...] = matrix(vs)

    for copy in copies[-2:]:
        copy.wait()


def contract_kernel(eta, flow, w_eta, w_flow, cel, own, partner, fields, inner, outer):
    levels, rows, across = eta.shape[1:]
    wide = w_eta.shape[1]
    half = w_eta.shape[0] // 2
    for h in range(rows // 8):
        hi, lo = split(eta[0, :, 8 * h : 8 * h + 8, :].reshape(wide, across))
        total = dot(w_eta[...], hi)
        part = dot(w_eta[0:half, :], lo)
        hi, lo = split(flow[0, :, 8 * h : 8 * h + 8, :].reshape(wide, across))
        total += dot(w_flow[...], hi)
        part += dot(w_flow[0:half, :], lo)
        part = part + total[:half] + total[half:]
        for f in range(len(FIELDS)):
            fields[f, 8 * h : 8 * h + 8, :] = part[8 * f : 8 * f + 8]

    me = lax.axis_index("trench")
    tiles = own.shape[0]
    if two_rounds(tiles):
        values = [both_rows(me ^ 3, own, partner), both_rows(me ^ 4, own, partner)]
    else:
        values = [both_rows(met(me, 1, tiles), own, partner)]
    outer[0:STEPS, :] = widen(values, across)

    def edge(out, at, last):
        for f, width in enumerate(HALO):
            start = rows - width if last else 0
            out[at + HALO_AT[f] : at + HALO_AT[f] + width, :] = fields[f, start : start + width, :]
        start = rows - CEL_HALO if last else 0
        out[at + CEL_AT : at + CEL_AT + CEL_HALO, :] = cel[start : start + CEL_HALO, :]

    @pl.when(me % 2 == 0)
    def _():
        edge(inner, 0, True)
        edge(outer, STEPS, False)

    @pl.when(me % 2 == 1)
    def _():
        edge(inner, 0, False)
        edge(outer, STEPS, True)


def met(me, d, tiles):
    odd = me % 2
    chip = (me // 2 + jnp.where(odd == 1, d, tiles // 2 - d)) % (tiles // 2)
    return jnp.where(d == 0, me, 2 * chip + 1 - odd)


def two_rounds(tiles):
    return tiles == 8


def sources(me, tiles):
    if two_rounds(tiles):
        return [me, me ^ 1, me ^ 3, me ^ 2], [me ^ 7, me ^ 6, me ^ 4, me ^ 5]
    early = [0] + list(range(2, tiles // 2))
    return [met(me, d, tiles) ^ core for d in early for core in range(2)], [met(me, 1, tiles) ^ core for core in range(2)]


def widen(values, lanes):
    fill = lanes - sum(value.shape[1] for value in values)
    return jnp.concatenate(values + [jnp.zeros((STEPS, fill), jnp.float32)], axis=1)


def residual_rows(owner, own):
    tiles = own.shape[0]
    return jnp.concatenate([own[jnp.clip(owner + d - 1, 0, tiles - 1)] for d in range(3)], axis=1)


def both_rows(owner, own, partner):
    return jnp.concatenate([residual_rows(owner, own), residual_rows(owner, partner)], axis=1)


def relay_kernel(own, partner, *outs):
    me = lax.axis_index("trench")
    for d, out in enumerate(outs, 2):
        out[...] = widen([both_rows(met(me, d, own.shape[0]), own, partner)], out.shape[1])


def second_kernel(own, partner, outer, first, after, out):
    per = 6 * own.shape[2]
    rows = both_rows(lax.axis_index("trench") ^ 7, own, partner)
    out[0:STEPS, :] = widen([rows, first[0:STEPS, per : 2 * per]], out.shape[1])
    out[STEPS:, :] = outer[STEPS:, :]


def sensors_kernel(rows, cells, count, hot_early, places_early, hot_late, places_late):
    me = lax.axis_index("trench")
    tiles, _, slots = cells.shape
    across = hot_early.shape[0]
    slot = lax.broadcasted_iota(jnp.int32, (1, slots), 1)
    bits = across.bit_length() - 1

    def list_slots(listed_sources, hot, places):
        listed = []
        for source in listed_sources:
            for d in range(3):
                owner = me + d - 1
                inside = (owner >= 0) & (owner < tiles)
                owner = jnp.clip(owner, 0, tiles - 1)
                live = jnp.where(inside, count[source, owner], 0)
                listed.append(jnp.where(slot < live, cells[source, pl.ds(owner, 1), :], -1))
        listed = jnp.concatenate(listed, axis=1)
        tile = (lax.broadcasted_iota(jnp.int32, listed.shape, 1) // slots) % 3
        at = jnp.where(listed < 0, -1, (listed >> bits) + (rows * (tile - 1) + PAD))
        places[...] = jnp.broadcast_to(at, places.shape)
        columns = listed & (across - 1)
        hot[...] = jnp.where(lax.broadcasted_iota(jnp.int32, hot.shape, 0) == columns, 1.0, 0.0).astype(jnp.bfloat16)

    early, late = sources(me, tiles)
    list_slots(early, hot_early, places_early)
    list_slots(late, hot_late, places_late)


def planes_of(values, hot, places, tall):
    here = lax.broadcasted_iota(jnp.int32, (tall, values.shape[1]), 0) == places[0:1, :]
    left = jnp.concatenate([jnp.where(here, values[t : t + 1, :], 0.0) for t in range(STEPS)], axis=0)
    both = dot(jnp.concatenate(split(left), axis=0), hot[...], ((1,), (1,)))
    return both[: STEPS * tall] + both[STEPS * tall :]


def inject_kernel(hot, places, own, partner, *refs):
    far, planes = refs[:-1], refs[-1]
    per = 6 * own.shape[2]
    values = [both_rows(lax.axis_index("trench"), own, partner)] + [got[0:STEPS, 0:per] for got in far]
    planes[...] = planes_of(jnp.concatenate(values, axis=1), hot, places, planes.shape[0] // STEPS)


def advance_kernel(tiles, fields, cel, coef, hot, places, facing_in, first, second, planes, *refs):
    outs, (stage, ext, cel_ext) = refs[:-3], refs[-3:]
    blocks = len(outs)
    me = lax.axis_index("trench")
    rows, across = cel.shape
    tall = rows + 2 * PAD
    part = rows // blocks
    odd = me % 2 == 1
    facing = me // 2 + jnp.where(odd, 1, -1)
    inner = facing_in[...]
    arrived = jnp.where((me // 2 + me) % 2 == 1, first[STEPS:, :], second[STEPS:, :])
    outer = jnp.where((facing >= 0) & (facing < tiles // 2), arrived, 0.0)
    before = jnp.where(odd, inner, outer)
    after = jnp.where(odd, outer, inner)

    all_planes = planes[...] + planes_of(second[0:STEPS, 0 : hot.shape[1]], hot, places, tall)
    inject = [all_planes[tall * t : tall * t + tall] for t in range(STEPS)]

    def extend(store, own, at, width):
        store(0, PAD, jnp.zeros((PAD, across), jnp.float32))
        store(PAD + rows, tall, jnp.zeros((PAD, across), jnp.float32))
        store(PAD, PAD + rows, own)
        store(PAD - width, PAD, before[at : at + width])
        store(PAD + rows, PAD + rows + width, after[at : at + width])

    for f, width in enumerate(HALO):
        def store(a, b, value, f=f):
            ext[f, a:b, :] = value
        extend(store, fields[f], HALO_AT[f], width)

    def store_cel(a, b, value):
        cel_ext[a:b, :] = value
    extend(store_cel, cel[...], CEL_AT, CEL_HALO)

    lane = lax.broadcasted_iota(jnp.int32, (tall, across), 1)
    first = lane == 0
    last = lane == across - 1
    speed = cel_ext[...]

    def horizontal(z):
        around = pltpu.roll(z, 1, 0) + pltpu.roll(z, tall - 1, 0)
        around += jnp.where(first, 0.0, pltpu.roll(z, 1, 1))
        around += jnp.where(last, 0.0, pltpu.roll(z, across - 1, 1))
        return speed * (around - 4.0 * z) + SHIFT * z

    def injected(n, k, a, b):
        total = None
        for tau in range(1, n - k + 1):
            r = n - tau
            term = coef[8 * r + k : 8 * r + k + 1, :] * inject[STEPS - tau][a:b]
            total = term if total is None else total + term
        return total

    base = horizontal(ext[0])
    for n in range(1, STEPS + 1):
        z = base
        for k in range(n - 1, 0, -1):
            z = horizontal(z + ext[FIELDS.index((n, k))] + injected(n, k, 0, tall))
        own = z[PAD : PAD + rows] + fields[FIELDS.index((n, 0))] + injected(n, 0, PAD, PAD + rows)
        t = STEPS - n
        for b in range(blocks):
            stage[b, part * t : part * t + part, :] = own[part * b : part * b + part]
    block = lax.axis_index("tblock")
    for r, out in enumerate(outs):
        out[...] = stage[block ^ r]


def prior_kernel(*refs):
    gots, (weight, out, whole, done, sems) = refs[:-5], refs[-5:]
    block = lax.axis_index("tblock")
    for r, got in enumerate(reversed(gots)):
        whole[block ^ r] = got[...]
    part = out.shape[1]
    length = out.shape[0]
    width = weight.shape[0]
    factor = [weight[j : j + 1, :] for j in range(width)]
    copies = []

    def finish(p):
        if (p + 1) % (length // 4) == 0:
            cut = pl.ds(p + 1 - length // 4, length // 4)
            copies.append(pltpu.make_async_copy(done.at[cut], out.at[cut], sems.at[len(copies)]))
            copies[-1].start()

    if 2 * part != 8:
        series = [whole[i // STEPS, part * (i % STEPS) : part * (i % STEPS) + part, :] for i in range(length)]
        for k in range(length):
            done[k] = sum(factor[j] * series[k + j] for j in range(min(width, length - k)))
            finish(k)
        for copy in copies:
            copy.wait()
        return
    pairs = length // 2
    even = [whole[p // 2, 8 * (p % 2) : 8 * (p % 2) + 8, :] for p in range(pairs)]
    half = lax.broadcasted_iota(jnp.int32, even[0].shape, 0) < part
    turned = [pltpu.roll(x, part, 0) for x in even] + [jnp.zeros(even[0].shape, jnp.float32)]
    odd = [jnp.where(half, turned[p], turned[p + 1]) for p in range(pairs)]
    for p in range(pairs):
        total = None
        for j in range(width):
            if p + j // 2 < pairs:
                term = factor[j] * (odd if j % 2 else even)[p + j // 2]
                total = term if total is None else total + term
        done[2 * p] = total[:part]
        done[2 * p + 1] = total[part:]
        finish(2 * p + 1)
    for copy in copies:
        copy.wait()


def shape(*dims, dtype=jnp.float32):
    return jax.ShapeDtypeStruct(dims, dtype)


def spec(space):
    return pl.BlockSpec(memory_space=space)


def body(
    adjoint_eta,
    adjoint_flow,
    residual,
    sensor_cell,
    sensor_count,
    depth_class,
    speed_table,
    damping,
    profile,
    band_weight,
):
    tiles = lax.axis_size("trench")
    blocks = lax.axis_size("tblock")
    levels, rows, across = adjoint_eta.shape[1:]
    tall = rows + 2 * PAD
    params = pltpu.CompilerParams(vmem_limit_bytes=LIMIT)

    def swaps(parts, axis):
        devices = lax.axis_size(axis)
        moved = {r: lax.ppermute(parts[r], axis, [(i, i ^ r) for i in range(devices)]) for r in range(devices - 1, 0, -1)}
        return [parts[0]] + [moved[r] for r in range(1, devices)]

    own = residual[0, 0]
    slots = own.shape[2]
    chips = tiles // 2

    def meet(x, d):
        pairs = [(2 * c + 1, 2 * ((c + d) % chips)) for c in range(chips)]
        return lax.ppermute(x, "trench", pairs + [(j, i) for i, j in pairs])

    partner = meet(own, 0)
    matrix = shape(16 * (len(FIELDS) + 1), 8 * levels, dtype=jnp.bfloat16)
    w_eta, w_flow, cel, coef, factor, own, eta, flow = pl.pallas_call(
        prepare_kernel,
        out_shape=(
            matrix,
            matrix,
            shape(rows, across),
            shape(8 * STEPS, across),
            shape(band_weight.shape[0], across),
            shape(*own.shape),
            shape(*adjoint_eta.shape),
            shape(*adjoint_flow.shape),
        ),
        in_specs=[spec(pltpu.HBM)] * 8,
        out_specs=(spec(VMEM),) * 8,
        scratch_shapes=[
            VMEM((rows, across), jnp.int32),
            SMEM(speed_table.shape, jnp.float32),
            VMEM((1, levels), jnp.float32),
            VMEM((1, levels), jnp.float32),
            VMEM((1, band_weight.shape[0]), jnp.float32),
            pltpu.SemaphoreType.DMA((8,)),
        ],
        compiler_params=params,
        cost_estimate=pl.CostEstimate(flops=10**7, bytes_accessed=4 * 10**6, transcendentals=0),
        name="prepare",
    )(
        *[
            pltpu.with_memory_space_constraint(x, pltpu.HBM)
            for x in (
                depth_class, speed_table, damping[None], profile[None], band_weight[None],
                own, adjoint_eta, adjoint_flow,
            )
        ]
    )
    fields, inner, outer = pl.pallas_call(
        contract_kernel,
        out_shape=(
            shape(len(FIELDS), rows, across),
            shape(ROWS, across),
            shape(STEPS + ROWS, across),
        ),
        in_specs=[spec(VMEM)] * 7,
        out_specs=(spec(VMEM),) * 3,
        compiler_params=params,
        cost_estimate=pl.CostEstimate(flops=10**9, bytes_accessed=4 * 10**6, transcendentals=0),
        name="contract",
    )(eta, flow, w_eta, w_flow, cel, own, partner)
    late = 4 if two_rounds(tiles) else 2

    def slot_shapes(count):
        return shape(across, 3 * slots * count, dtype=jnp.bfloat16), shape(8, 3 * slots * count, dtype=jnp.int32)

    hot, places, hot_late, places_late = pl.pallas_call(
        functools.partial(sensors_kernel, rows),
        out_shape=slot_shapes(tiles - late) + slot_shapes(late),
        in_specs=[spec(VMEM), spec(SMEM)],
        out_specs=(spec(VMEM),) * 4,
        compiler_params=params,
        cost_estimate=pl.CostEstimate(flops=10**6, bytes_accessed=2 * 10**6, transcendentals=0),
        name="sensors",
    )(sensor_cell, sensor_count)
    facing_in = meet(inner, 0)
    if two_rounds(tiles):
        def swap(x, r):
            return lax.ppermute(x, "trench", [(i, i ^ r) for i in range(tiles)])

        first = swap(outer, 3)
        second = swap(
            pl.pallas_call(
                second_kernel,
                out_shape=shape(*outer.shape),
                in_specs=[spec(VMEM)] * 4 + [spec(pl.ANY)],
                out_specs=spec(VMEM),
                compiler_params=params,
                name="second",
            )(own, partner, outer, first, places_late),
            7,
        )
        far = [first]
    else:
        relays = pl.pallas_call(
            relay_kernel,
            out_shape=[shape(STEPS, -(-6 * slots // 128) * 128)] * (chips - 2),
            in_specs=[spec(VMEM)] * 2,
            out_specs=[spec(VMEM)] * (chips - 2),
            compiler_params=params,
            name="relay",
        )(own, partner)
        far = [meet(relay, d) for d, relay in enumerate(relays, 2)]
        first = second = meet(outer, 1)

    planes = pl.pallas_call(
        inject_kernel,
        out_shape=shape(STEPS * (rows + 2 * PAD), across),
        in_specs=[spec(VMEM)] * (4 + len(far)),
        out_specs=spec(VMEM),
        compiler_params=params,
        cost_estimate=pl.CostEstimate(flops=10**8, bytes_accessed=4 * 10**6, transcendentals=0),
        name="inject",
    )(hot, places, own, partner, *far)
    series = pl.pallas_call(
        functools.partial(advance_kernel, tiles),
        out_shape=(shape(STEPS * rows // blocks, across),) * blocks,
        in_specs=[spec(VMEM)] * 9,
        out_specs=(spec(VMEM),) * blocks,
        scratch_shapes=[
            VMEM((blocks, STEPS * rows // blocks, across), jnp.float32),
            VMEM((len(HALO), tall, across), jnp.float32),
            VMEM((tall, across), jnp.float32),
        ],
        compiler_params=params,
        name="advance",
    )(fields, cel, coef, hot_late, places_late, facing_in, first, second, planes)
    gots = swaps(series, "tblock")
    return pl.pallas_call(
        prior_kernel,
        out_shape=shape(STEPS * blocks, rows // blocks, across),
        in_specs=[spec(VMEM)] * (blocks + 1),
        out_specs=spec(pl.ANY),
        scratch_shapes=[
            VMEM((blocks, STEPS * rows // blocks, across), jnp.float32),
            VMEM((STEPS * blocks, rows // blocks, across), jnp.float32),
            pltpu.SemaphoreType.DMA((4,)),
        ],
        compiler_params=params,
        name="prior",
    )(*reversed(gots), factor)


def solution(mesh):
    in_specs = (
        P("tblock", None, "trench", None),
        P("tblock", None, "trench", None),
        P("tblock", "trench", None, None, None),
        P(),
        P(),
        P("trench", None),
        P(),
        P(),
        P(),
        P(),
    )
    out_specs = P(None, ("trench", "tblock"), None)
    return jax.shard_map(body, mesh=mesh, in_specs=in_specs, out_specs=out_specs, check_vma=False)
```

```python
import functools
import math

import jax
import jax.numpy as jnp
from jax import lax
from jax.experimental import pallas as pl
from jax.experimental.pallas import tpu as pltpu
from jax.sharding import PartitionSpec as P

VERT = 0.2
STEPS = 4
PAD = 8
VMEM = pltpu.VMEM
SMEM = pltpu.SMEM
LIMIT = 32 * 1024 * 1024

SHIFT = 1.2

FIELDS = [(4, 4), (4, 3), (4, 2), (3, 2), (4, 1), (3, 1), (2, 1), (4, 0), (3, 0), (2, 0), (1, 0)]
HALO = [4, 3, 2, 2, 1, 1, 1]
HALO_AT = [0, 4, 7, 9, 11, 12, 13]
CEL_AT = 14
CEL_HALO = 3
ROWS = 17


def split(x):
    hi = x.astype(jnp.bfloat16)
    return hi, (x - hi.astype(jnp.float32)).astype(jnp.bfloat16)


def dot(a, b, dims=((1,), (0,))):
    return lax.dot_general(a, b, (dims, ((), ())), preferred_element_type=jnp.float32)


def prepare_kernel(
    depth, table, damping, profile, band, residual, eta, flow,
    w_eta, w_flow, cel, coef, factor, own, eta_v, flow_v,
    depth_v, table_s, damping_v, profile_v, band_v, sems,
):
    rows, across = cel.shape
    levels = damping.shape[1]
    copies = [
        pltpu.make_async_copy(src, dst, sems.at[i])
        for i, (src, dst) in enumerate((
            (damping, damping_v), (profile, profile_v), (table, table_s), (depth, depth_v),
            (band, band_v), (residual, own), (eta, eta_v), (flow, flow_v),
        ))
    ]
    for copy in copies:
        copy.start()
    for copy in copies[:-2]:
        copy.wait()

    classes = depth_v[...]
    speed = jnp.zeros(classes.shape, jnp.float32)
    for c in range(table_s.shape[0]):
        speed = jnp.where(classes == c, table_s[c], speed)
    cel[...] = speed
    for j in range(factor.shape[0]):
        factor[j : j + 1, :] = jnp.broadcast_to(band_v[:, j : j + 1], (1, across))

    lane = lax.broadcasted_iota(jnp.int32, (8, 128), 1)
    sub = lax.broadcasted_iota(jnp.int32, (8, 128), 0)
    inside = lane < levels
    fill = jnp.zeros((1, 128 - levels), jnp.float32)
    keep = jnp.broadcast_to(jnp.concatenate([damping_v[...], fill], axis=1), (8, 128))
    weight = jnp.broadcast_to(jnp.concatenate([profile_v[...], fill], axis=1), (8, 128))
    u = jnp.zeros((8, 128), jnp.float32)
    v = jnp.where(sub == 0, weight * (1.0 / math.sqrt(levels)), 0.0)
    us, vs = [u], [v]
    for r in range(STEPS):
        s = u + v
        bottom = jnp.sum(jnp.where(lane == levels - 1, s, 0.0), axis=1, keepdims=True)
        coef[8 * r : 8 * r + 8, :] = jnp.broadcast_to(bottom, (8, coef.shape[1]))
        vertical = pltpu.roll(s, 1, 1) + pltpu.roll(s, 127, 1) - 2.0 * s
        u = jnp.where(inside, u + VERT * vertical - SHIFT * s + pltpu.roll(s, 1, 0), 0.0)
        v = s * keep
        us.append(u)
        vs.append(v)

    wide = w_eta.shape[1]
    spread = (
        lax.broadcasted_iota(jnp.int32, (128, wide), 1) // 8
        == lax.broadcasted_iota(jnp.int32, (128, wide), 0)
    ).astype(jnp.bfloat16)
    count_f = len(FIELDS) + 1
    diagonal = (
        lax.broadcasted_iota(jnp.int32, (8 * count_f, wide), 1) % 8
        == lax.broadcasted_iota(jnp.int32, (8 * count_f, wide), 0) % 8
    )

    def matrix(vectors):
        blocks = [jnp.broadcast_to(vectors[n][k : k + 1, :], (8, 128)) for n, k in FIELDS]
        blocks.append(jnp.zeros((8, 128), jnp.float32))
        hi, lo = split(jnp.concatenate(blocks, axis=0))
        zero = jnp.zeros((8 * count_f, wide), jnp.float32)
        hi = jnp.where(diagonal, dot(hi, spread), zero).astype(jnp.bfloat16)
        lo = jnp.where(diagonal, dot(lo, spread), zero).astype(jnp.bfloat16)
        return jnp.concatenate([hi, lo], axis=0)

    w_eta[...] = matrix(us)
    w_flow[...] = matrix(vs)

    for copy in copies[-2:]:
        copy.wait()


def contract_kernel(eta, flow, w_eta, w_flow, cel, own, partner, fields, inner, outer, *relays):
    levels, rows, across = eta.shape[1:]
    wide = w_eta.shape[1]
    half = w_eta.shape[0] // 2
    for h in range(rows // 8):
        hi, lo = split(eta[0, :, 8 * h : 8 * h + 8, :].reshape(wide, across))
        total = dot(w_eta[...], hi)
        part = dot(w_eta[0:half, :], lo)
        hi, lo = split(flow[0, :, 8 * h : 8 * h + 8, :].reshape(wide, across))
        total += dot(w_flow[...], hi)
        part += dot(w_flow[0:half, :], lo)
        part = part + total[:half] + total[half:]
        for f in range(len(FIELDS)):
            fields[f, 8 * h : 8 * h + 8, :] = part[8 * f : 8 * f + 8]

    me = lax.axis_index("trench")
    tiles = own.shape[0]
    for d in range(1, len(relays) + 2):
        target = met(me, d, tiles)
        values = [both_rows(target, own, partner)]
        if d <= passed_on(tiles):
            values.append(both_rows(target ^ 1, own, partner))
        out = relays[d - 2] if d > 1 else outer
        out[0:STEPS, :] = widen(values, out.shape[1])

    def edge(out, at, last):
        for f, width in enumerate(HALO):
            start = rows - width if last else 0
            out[at + HALO_AT[f] : at + HALO_AT[f] + width, :] = fields[f, start : start + width, :]
        start = rows - CEL_HALO if last else 0
        out[at + CEL_AT : at + CEL_AT + CEL_HALO, :] = cel[start : start + CEL_HALO, :]

    @pl.when(me % 2 == 0)
    def _():
        edge(inner, 0, True)
        edge(outer, STEPS, False)

    @pl.when(me % 2 == 1)
    def _():
        edge(inner, 0, False)
        edge(outer, STEPS, True)


def met(me, d, tiles):
    odd = me % 2
    chip = (me // 2 + jnp.where(odd == 1, d, tiles // 2 - d)) % (tiles // 2)
    return jnp.where(d == 0, me, 2 * chip + 1 - odd)


def direct(tiles):
    return tiles // 4


def passed_on(tiles):
    return tiles // 2 - 1 - direct(tiles)


def sources(me, tiles):
    near = [met(me, d, tiles) ^ core for d in range(direct(tiles) + 1) for core in range(2)]
    far = [met(me ^ 1, d, tiles) ^ core for d in range(1, passed_on(tiles) + 1) for core in range(2)]
    return near, far


def packed(q):
    return STEPS * (q // 2), 256 * (q % 2)


def widen(values, lanes):
    fill = lanes - sum(value.shape[1] for value in values)
    if fill:
        values = values + [jnp.zeros((STEPS, fill), jnp.float32)]
    return jnp.concatenate(values, axis=1)


def residual_rows(owner, own):
    tiles = own.shape[0]
    return jnp.concatenate([own[jnp.clip(owner + d - 1, 0, tiles - 1)] for d in range(3)], axis=1)


def both_rows(owner, own, partner):
    return jnp.concatenate([residual_rows(owner, own), residual_rows(owner, partner)], axis=1)


def pass_kernel(slots, count, inner, after, *refs):
    gots, out = refs[:-1], refs[-1]
    per = 6 * slots
    top = out.shape[0] - ROWS
    out[0:top, :] = jnp.zeros((top, out.shape[1]), jnp.float32)
    for q in range(count):
        row, lane = packed(q)
        out[row : row + STEPS, lane : lane + 256] = widen([gots[q][0:STEPS, per : 2 * per]], 256)
    out[top:, :] = inner[...]


def sensors_kernel(rows, cells, count, hot_early, places_early, hot_late, places_late):
    me = lax.axis_index("trench")
    tiles, _, slots = cells.shape
    across = hot_early.shape[0]
    slot = lax.broadcasted_iota(jnp.int32, (1, slots), 1)
    bits = across.bit_length() - 1

    def list_slots(listed_sources, hot, places):
        listed = []
        for source in listed_sources:
            for d in range(3):
                owner = me + d - 1
                inside = (owner >= 0) & (owner < tiles)
                owner = jnp.clip(owner, 0, tiles - 1)
                live = jnp.where(inside, count[source, owner], 0)
                listed.append(jnp.where(slot < live, cells[source, pl.ds(owner, 1), :], -1))
        listed = jnp.concatenate(listed, axis=1)
        tile = (lax.broadcasted_iota(jnp.int32, listed.shape, 1) // slots) % 3
        at = jnp.where(listed < 0, -1, (listed >> bits) + (rows * (tile - 1) + PAD))
        places[...] = jnp.broadcast_to(at, places.shape)
        columns = listed & (across - 1)
        hot[...] = jnp.where(lax.broadcasted_iota(jnp.int32, hot.shape, 0) == columns, 1.0, 0.0).astype(jnp.bfloat16)

    early, late = sources(me, tiles)
    list_slots(early, hot_early, places_early)
    list_slots(late, hot_late, places_late)


def planes_of(values, hot, places, tall):
    here = lax.broadcasted_iota(jnp.int32, (tall, values.shape[1]), 0) == places[0:1, :]
    left = jnp.concatenate([jnp.where(here, values[t : t + 1, :], 0.0) for t in range(STEPS)], axis=0)
    both = dot(jnp.concatenate(split(left), axis=0), hot[...], ((1,), (1,)))
    return both[: STEPS * tall] + both[STEPS * tall :]


def inject_kernel(hot, places, own, partner, *refs):
    gots, planes = refs[:-1], refs[-1]
    per = 6 * own.shape[2]
    values = [both_rows(lax.axis_index("trench"), own, partner)] + [got[0:STEPS, 0:per] for got in gots]
    planes[...] = planes_of(jnp.concatenate(values, axis=1), hot, places, planes.shape[0] // STEPS)


def advance_kernel(tiles, fields, cel, coef, hot, places, facing_in, facing_out, planes, *refs):
    outs, (stage, ext, cel_ext) = refs[:-3], refs[-3:]
    blocks = len(outs)
    me = lax.axis_index("trench")
    rows, across = cel.shape
    tall = rows + 2 * PAD
    part = rows // blocks
    odd = me % 2 == 1
    facing = me // 2 + jnp.where(odd, 1, -1)
    top = facing_in.shape[0] - ROWS
    inner = facing_in[top:, :]
    outer = jnp.where((facing >= 0) & (facing < tiles // 2), facing_out[STEPS:, :], 0.0)
    before = jnp.where(odd, inner, outer)
    after = jnp.where(odd, outer, inner)

    count = passed_on(tiles)
    per = hot.shape[1] // count
    late = [facing_in[row : row + STEPS, at : at + per] for row, at in map(packed, range(count))]
    all_planes = planes[...] + planes_of(jnp.concatenate(late, axis=1), hot, places, tall)
    inject = [all_planes[tall * t : tall * t + tall] for t in range(STEPS)]

    def extend(store, own, at, width):
        store(0, PAD, jnp.zeros((PAD, across), jnp.float32))
        store(PAD + rows, tall, jnp.zeros((PAD, across), jnp.float32))
        store(PAD, PAD + rows, own)
        store(PAD - width, PAD, before[at : at + width])
        store(PAD + rows, PAD + rows + width, after[at : at + width])

    for f, width in enumerate(HALO):
        def store(a, b, value, f=f):
            ext[f, a:b, :] = value
        extend(store, fields[f], HALO_AT[f], width)

    def store_cel(a, b, value):
        cel_ext[a:b, :] = value
    extend(store_cel, cel[...], CEL_AT, CEL_HALO)

    lane = lax.broadcasted_iota(jnp.int32, (tall, across), 1)
    first = lane == 0
    last = lane == across - 1
    speed = cel_ext[...]

    def horizontal(z):
        around = pltpu.roll(z, 1, 0) + pltpu.roll(z, tall - 1, 0)
        around += jnp.where(first, 0.0, pltpu.roll(z, 1, 1))
        around += jnp.where(last, 0.0, pltpu.roll(z, across - 1, 1))
        return speed * (around - 4.0 * z) + SHIFT * z

    def injected(n, k, a, b):
        total = None
        for tau in range(1, n - k + 1):
            r = n - tau
            term = coef[8 * r + k : 8 * r + k + 1, :] * inject[STEPS - tau][a:b]
            total = term if total is None else total + term
        return total

    base = horizontal(ext[0])
    for n in range(1, STEPS + 1):
        z = base
        for k in range(n - 1, 0, -1):
            z = horizontal(z + ext[FIELDS.index((n, k))] + injected(n, k, 0, tall))
        own = z[PAD : PAD + rows] + fields[FIELDS.index((n, 0))] + injected(n, 0, PAD, PAD + rows)
        t = STEPS - n
        for b in range(blocks):
            stage[b, part * t : part * t + part, :] = own[part * b : part * b + part]
    block = lax.axis_index("tblock")
    for r, out in enumerate(outs):
        out[...] = stage[block ^ r]


def prior_kernel(*refs):
    gots, (weight, out, whole, done, sems) = refs[:-5], refs[-5:]
    block = lax.axis_index("tblock")
    for r, got in enumerate(reversed(gots)):
        whole[block ^ r] = got[...]
    part = out.shape[1]
    length = out.shape[0]
    width = weight.shape[0]
    factor = [weight[j : j + 1, :] for j in range(width)]
    copies = []

    def finish(p):
        if (p + 1) % (length // 4) == 0:
            cut = pl.ds(p + 1 - length // 4, length // 4)
            copies.append(pltpu.make_async_copy(done.at[cut], out.at[cut], sems.at[len(copies)]))
            copies[-1].start()

    if 2 * part != 8:
        series = [whole[i // STEPS, part * (i % STEPS) : part * (i % STEPS) + part, :] for i in range(length)]
        for k in range(length):
            done[k] = sum(factor[j] * series[k + j] for j in range(min(width, length - k)))
            finish(k)
        for copy in copies:
            copy.wait()
        return
    pairs = length // 2
    even = [whole[p // 2, 8 * (p % 2) : 8 * (p % 2) + 8, :] for p in range(pairs)]
    half = lax.broadcasted_iota(jnp.int32, even[0].shape, 0) < part
    turned = [pltpu.roll(x, part, 0) for x in even] + [jnp.zeros(even[0].shape, jnp.float32)]
    odd = [jnp.where(half, turned[p], turned[p + 1]) for p in range(pairs)]
    for p in range(pairs):
        total = None
        for j in range(width):
            if p + j // 2 < pairs:
                term = factor[j] * (odd if j % 2 else even)[p + j // 2]
                total = term if total is None else total + term
        done[2 * p] = total[:part]
        done[2 * p + 1] = total[part:]
        finish(2 * p + 1)
    for copy in copies:
        copy.wait()


def shape(*dims, dtype=jnp.float32):
    return jax.ShapeDtypeStruct(dims, dtype)


def spec(space):
    return pl.BlockSpec(memory_space=space)


def body(
    adjoint_eta,
    adjoint_flow,
    residual,
    sensor_cell,
    sensor_count,
    depth_class,
    speed_table,
    damping,
    profile,
    band_weight,
):
    tiles = lax.axis_size("trench")
    blocks = lax.axis_size("tblock")
    levels, rows, across = adjoint_eta.shape[1:]
    tall = rows + 2 * PAD
    params = pltpu.CompilerParams(vmem_limit_bytes=LIMIT)

    def swaps(parts, axis):
        devices = lax.axis_size(axis)
        moved = {r: lax.ppermute(parts[r], axis, [(i, i ^ r) for i in range(devices)]) for r in range(devices - 1, 0, -1)}
        return [parts[0]] + [moved[r] for r in range(1, devices)]

    own = residual[0, 0]
    slots = own.shape[2]
    chips = tiles // 2

    def meet(x, d):
        pairs = [(2 * c + 1, 2 * ((c + d) % chips)) for c in range(chips)]
        return lax.ppermute(x, "trench", pairs + [(j, i) for i, j in pairs])

    partner = meet(own, 0)
    matrix = shape(16 * (len(FIELDS) + 1), 8 * levels, dtype=jnp.bfloat16)
    w_eta, w_flow, cel, coef, factor, own, eta, flow = pl.pallas_call(
        prepare_kernel,
        out_shape=(
            matrix,
            matrix,
            shape(rows, across),
            shape(8 * STEPS, across),
            shape(band_weight.shape[0], across),
            shape(*own.shape),
            shape(*adjoint_eta.shape),
            shape(*adjoint_flow.shape),
        ),
        in_specs=[spec(pltpu.HBM)] * 8,
        out_specs=(spec(VMEM),) * 8,
        scratch_shapes=[
            VMEM((rows, across), jnp.int32),
            SMEM(speed_table.shape, jnp.float32),
            VMEM((1, levels), jnp.float32),
            VMEM((1, levels), jnp.float32),
            VMEM((1, band_weight.shape[0]), jnp.float32),
            pltpu.SemaphoreType.DMA((8,)),
        ],
        compiler_params=params,
        cost_estimate=pl.CostEstimate(flops=10**7, bytes_accessed=4 * 10**6, transcendentals=0),
        name="prepare",
    )(
        *[
            pltpu.with_memory_space_constraint(x, pltpu.HBM)
            for x in (
                depth_class, speed_table, damping[None], profile[None], band_weight[None],
                own, adjoint_eta, adjoint_flow,
            )
        ]
    )
    fields, inner, outer, *relays = pl.pallas_call(
        contract_kernel,
        out_shape=(
            shape(len(FIELDS), rows, across),
            shape(ROWS, across),
            shape(STEPS + ROWS, across),
        ) + tuple(
            shape(STEPS, 6 * slots * (2 if d <= passed_on(tiles) else 1)) for d in range(2, direct(tiles) + 1)
        ),
        in_specs=[spec(VMEM)] * 7,
        out_specs=(spec(VMEM),) * (2 + direct(tiles)),
        compiler_params=params,
        cost_estimate=pl.CostEstimate(flops=10**9, bytes_accessed=4 * 10**6, transcendentals=0),
        name="contract",
    )(eta, flow, w_eta, w_flow, cel, own, partner)
    facing_out = meet(outer, 1)
    gots = [facing_out] + [meet(relay, d) for d, relay in enumerate(relays, 2)]
    late = 2 * passed_on(tiles)

    def slot_shapes(count):
        return shape(across, 3 * slots * count, dtype=jnp.bfloat16), shape(8, 3 * slots * count, dtype=jnp.int32)

    hot, places, hot_late, places_late = pl.pallas_call(
        functools.partial(sensors_kernel, rows),
        out_shape=slot_shapes(tiles - late) + slot_shapes(late),
        in_specs=[spec(VMEM), spec(SMEM)],
        out_specs=(spec(VMEM),) * 4,
        compiler_params=params,
        cost_estimate=pl.CostEstimate(flops=10**6, bytes_accessed=2 * 10**6, transcendentals=0),
        name="sensors",
    )(sensor_cell, sensor_count)
    facing_in = meet(
        pl.pallas_call(
            functools.partial(pass_kernel, slots, passed_on(tiles)),
            out_shape=shape(STEPS * -(-passed_on(tiles) // 2) + ROWS, across),
            in_specs=[spec(VMEM), spec(pl.ANY)] + [spec(VMEM)] * len(gots),
            out_specs=spec(VMEM),
            compiler_params=params,
            name="pass",
        )(inner, places_late, *gots),
        0,
    )
    planes = pl.pallas_call(
        inject_kernel,
        out_shape=shape(STEPS * (rows + 2 * PAD), across),
        in_specs=[spec(VMEM)] * (4 + len(gots)),
        out_specs=spec(VMEM),
        compiler_params=params,
        cost_estimate=pl.CostEstimate(flops=10**8, bytes_accessed=4 * 10**6, transcendentals=0),
        name="inject",
    )(hot, places, own, partner, *gots)
    series = pl.pallas_call(
        functools.partial(advance_kernel, tiles),
        out_shape=(shape(STEPS * rows // blocks, across),) * blocks,
        in_specs=[spec(VMEM)] * 8,
        out_specs=(spec(VMEM),) * blocks,
        scratch_shapes=[
            VMEM((blocks, STEPS * rows // blocks, across), jnp.float32),
            VMEM((len(HALO), tall, across), jnp.float32),
            VMEM((tall, across), jnp.float32),
        ],
        compiler_params=params,
        name="advance",
    )(fields, cel, coef, hot_late, places_late, facing_in, facing_out, planes)
    gots = swaps(series, "tblock")
    return pl.pallas_call(
        prior_kernel,
        out_shape=shape(STEPS * blocks, rows // blocks, across),
        in_specs=[spec(VMEM)] * (blocks + 1),
        out_specs=spec(pl.ANY),
        scratch_shapes=[
            VMEM((blocks, STEPS * rows // blocks, across), jnp.float32),
            VMEM((STEPS * blocks, rows // blocks, across), jnp.float32),
            pltpu.SemaphoreType.DMA((4,)),
        ],
        compiler_params=params,
        name="prior",
    )(*reversed(gots), factor)


def solution(mesh):
    in_specs = (
        P("tblock", None, "trench", None),
        P("tblock", None, "trench", None),
        P("tblock", "trench", None, None, None),
        P(),
        P(),
        P("trench", None),
        P(),
        P(),
        P(),
        P(),
    )
    out_specs = P(None, ("trench", "tblock"), None)
    return jax.shard_map(body, mesh=mesh, in_specs=in_specs, out_specs=out_specs, check_vma=False)
```

```python
import functools
import math

import jax
import jax.numpy as jnp
from jax import lax
from jax.experimental import pallas as pl
from jax.experimental.pallas import tpu as pltpu
from jax.sharding import PartitionSpec as P

VERT = 0.2
STEPS = 4
PAD = 8
VMEM = pltpu.VMEM
SMEM = pltpu.SMEM
LIMIT = 32 * 1024 * 1024

SHIFT = 1.2

FIELDS = [(4, 4), (4, 3), (4, 2), (3, 2), (4, 1), (3, 1), (2, 1), (4, 0), (3, 0), (2, 0), (1, 0)]
TRACED = [(4, 4), (4, 3), (3, 2), (2, 1), (4, 2), (3, 1), (4, 1)]
CEL_AT = len(TRACED)
CEL_HALO = 3
ROWS = CEL_AT + CEL_HALO


def beside(z):
    across = z.shape[1]
    lane = lax.broadcasted_iota(jnp.int32, z.shape, 1)
    left = jnp.where(lane == 0, 0.0, pltpu.roll(z, 1, 1))
    return left + jnp.where(lane == across - 1, 0.0, pltpu.roll(z, across - 1, 1))


def split(x):
    hi = x.astype(jnp.bfloat16)
    return hi, (x - hi.astype(jnp.float32)).astype(jnp.bfloat16)


def dot(a, b, dims=((1,), (0,))):
    return lax.dot_general(a, b, (dims, ((), ())), preferred_element_type=jnp.float32)


def prepare_kernel(
    depth, table, damping, profile, band, residual, eta, flow,
    w_eta, w_flow, cel, coef, factor, own, eta_v, flow_v,
    depth_v, table_s, damping_v, profile_v, band_v, sems,
):
    rows, across = cel.shape
    levels = damping.shape[1]
    copies = [
        pltpu.make_async_copy(src, dst, sems.at[i])
        for i, (src, dst) in enumerate((
            (damping, damping_v), (profile, profile_v), (table, table_s), (depth, depth_v),
            (band, band_v), (residual, own), (eta, eta_v), (flow, flow_v),
        ))
    ]
    for copy in copies:
        copy.start()
    for copy in copies[:-2]:
        copy.wait()

    classes = depth_v[...]
    speed = jnp.zeros(classes.shape, jnp.float32)
    for c in range(table_s.shape[0]):
        speed = jnp.where(classes == c, table_s[c], speed)
    cel[...] = speed
    for j in range(factor.shape[0]):
        factor[j : j + 1, :] = jnp.broadcast_to(band_v[:, j : j + 1], (1, across))

    lane = lax.broadcasted_iota(jnp.int32, (8, 128), 1)
    sub = lax.broadcasted_iota(jnp.int32, (8, 128), 0)
    inside = lane < levels
    fill = jnp.zeros((1, 128 - levels), jnp.float32)
    keep = jnp.broadcast_to(jnp.concatenate([damping_v[...], fill], axis=1), (8, 128))
    weight = jnp.broadcast_to(jnp.concatenate([profile_v[...], fill], axis=1), (8, 128))
    u = jnp.zeros((8, 128), jnp.float32)
    v = jnp.where(sub == 0, weight * (1.0 / math.sqrt(levels)), 0.0)
    us, vs = [u], [v]
    for r in range(STEPS):
        s = u + v
        bottom = jnp.sum(jnp.where(lane == levels - 1, s, 0.0), axis=1, keepdims=True)
        coef[8 * r : 8 * r + 8, :] = jnp.broadcast_to(bottom, (8, coef.shape[1]))
        vertical = pltpu.roll(s, 1, 1) + pltpu.roll(s, 127, 1) - 2.0 * s
        u = jnp.where(inside, u + VERT * vertical - SHIFT * s + pltpu.roll(s, 1, 0), 0.0)
        v = s * keep
        us.append(u)
        vs.append(v)

    wide = w_eta.shape[1]
    spread = (
        lax.broadcasted_iota(jnp.int32, (128, wide), 1) // 8
        == lax.broadcasted_iota(jnp.int32, (128, wide), 0)
    ).astype(jnp.bfloat16)
    count_f = len(FIELDS) + 1
    diagonal = (
        lax.broadcasted_iota(jnp.int32, (8 * count_f, wide), 1) % 8
        == lax.broadcasted_iota(jnp.int32, (8 * count_f, wide), 0) % 8
    )

    def matrix(vectors):
        blocks = [jnp.broadcast_to(vectors[n][k : k + 1, :], (8, 128)) for n, k in FIELDS]
        blocks.append(jnp.zeros((8, 128), jnp.float32))
        hi, lo = split(jnp.concatenate(blocks, axis=0))
        zero = jnp.zeros((8 * count_f, wide), jnp.float32)
        hi = jnp.where(diagonal, dot(hi, spread), zero).astype(jnp.bfloat16)
        lo = jnp.where(diagonal, dot(lo, spread), zero).astype(jnp.bfloat16)
        return jnp.concatenate([hi, lo], axis=0)

    w_eta[...] = matrix(us)
    w_flow[...] = matrix(vs)

    for copy in copies[-2:]:
        copy.wait()


def contract_kernel(eta, flow, w_eta, w_flow, cel, own, partner, fields, inner, outer, *relays):
    levels, rows, across = eta.shape[1:]
    wide = w_eta.shape[1]
    half = w_eta.shape[0] // 2
    for h in range(rows // 8):
        hi, lo = split(eta[0, :, 8 * h : 8 * h + 8, :].reshape(wide, across))
        total = dot(w_eta[...], hi)
        part = dot(w_eta[0:half, :], lo)
        hi, lo = split(flow[0, :, 8 * h : 8 * h + 8, :].reshape(wide, across))
        total += dot(w_flow[...], hi)
        part += dot(w_flow[0:half, :], lo)
        part = part + total[:half] + total[half:]
        for f in range(len(FIELDS)):
            fields[f, 8 * h : 8 * h + 8, :] = part[8 * f : 8 * f + 8]

    me = lax.axis_index("trench")
    tiles = own.shape[0]
    for d in range(1, len(relays) + 2):
        target = met(me, d, tiles)
        values = [both_rows(target, own, partner)]
        if d <= passed_on(tiles):
            values.append(both_rows(target ^ 1, own, partner))
        out = relays[d - 2] if d > 1 else outer
        out[0:STEPS, :] = widen(values, out.shape[1])

    speed = cel[...]
    row = lax.broadcasted_iota(jnp.int32, (rows, across), 0)

    def horizontal(z):
        around = jnp.where(row == 0, 0.0, pltpu.roll(z, 1, 0)) + jnp.where(row == rows - 1, 0.0, pltpu.roll(z, rows - 1, 0))
        return speed * (around + beside(z) - 4.0 * z) + SHIFT * z

    operand = {(STEPS, STEPS): fields[0]}
    base = horizontal(fields[0])
    for n in range(2, STEPS + 1):
        z = base
        for k in range(n - 1, 0, -1):
            operand[n, k] = z + fields[FIELDS.index((n, k))]
            if k > 1:
                z = horizontal(operand[n, k])

    def edge(out, at, last):
        for f, key in enumerate(TRACED):
            out[at + f : at + f + 1, :] = operand[key][rows - 1 : rows] if last else operand[key][0:1]
        start = rows - CEL_HALO if last else 0
        out[at + CEL_AT : at + CEL_AT + CEL_HALO, :] = cel[start : start + CEL_HALO, :]

    @pl.when(me % 2 == 0)
    def _():
        edge(inner, 0, True)
        edge(outer, STEPS, False)

    @pl.when(me % 2 == 1)
    def _():
        edge(inner, 0, False)
        edge(outer, STEPS, True)


def met(me, d, tiles):
    odd = me % 2
    chip = (me // 2 + jnp.where(odd == 1, d, tiles // 2 - d)) % (tiles // 2)
    return jnp.where(d == 0, me, 2 * chip + 1 - odd)


def direct(tiles):
    return tiles // 4


def passed_on(tiles):
    return tiles // 2 - 1 - direct(tiles)


def sources(me, tiles):
    near = [met(me, d, tiles) ^ core for d in range(direct(tiles) + 1) for core in range(2)]
    far = [met(me ^ 1, d, tiles) ^ core for d in range(1, passed_on(tiles) + 1) for core in range(2)]
    return near, far


def packed(q):
    return STEPS * (q // 2), 256 * (q % 2)


def widen(values, lanes):
    fill = lanes - sum(value.shape[1] for value in values)
    if fill:
        values = values + [jnp.zeros((STEPS, fill), jnp.float32)]
    return jnp.concatenate(values, axis=1)


def residual_rows(owner, own):
    tiles = own.shape[0]
    return jnp.concatenate([own[jnp.clip(owner + d - 1, 0, tiles - 1)] for d in range(3)], axis=1)


def both_rows(owner, own, partner):
    return jnp.concatenate([residual_rows(owner, own), residual_rows(owner, partner)], axis=1)


def pass_kernel(slots, count, inner, after, *refs):
    gots, out = refs[:-1], refs[-1]
    per = 6 * slots
    top = out.shape[0] - ROWS
    out[0:top, :] = jnp.zeros((top, out.shape[1]), jnp.float32)
    for q in range(count):
        row, lane = packed(q)
        out[row : row + STEPS, lane : lane + 256] = widen([gots[q][0:STEPS, per : 2 * per]], 256)
    out[top:, :] = inner[...]


def sensors_kernel(rows, cells, count, hot_early, places_early, hot_late, places_late):
    me = lax.axis_index("trench")
    tiles, _, slots = cells.shape
    across = hot_early.shape[0]
    slot = lax.broadcasted_iota(jnp.int32, (1, slots), 1)
    bits = across.bit_length() - 1

    def list_slots(listed_sources, hot, places):
        listed = []
        for source in listed_sources:
            for d in range(3):
                owner = me + d - 1
                inside = (owner >= 0) & (owner < tiles)
                owner = jnp.clip(owner, 0, tiles - 1)
                live = jnp.where(inside, count[source, owner], 0)
                listed.append(jnp.where(slot < live, cells[source, pl.ds(owner, 1), :], -1))
        listed = jnp.concatenate(listed, axis=1)
        tile = (lax.broadcasted_iota(jnp.int32, listed.shape, 1) // slots) % 3
        at = jnp.where(listed < 0, -1, (listed >> bits) + (rows * (tile - 1) + PAD))
        places[...] = jnp.broadcast_to(at, places.shape)
        columns = listed & (across - 1)
        hot[...] = jnp.where(lax.broadcasted_iota(jnp.int32, hot.shape, 0) == columns, 1.0, 0.0).astype(jnp.bfloat16)

    early, late = sources(me, tiles)
    list_slots(early, hot_early, places_early)
    list_slots(late, hot_late, places_late)


def planes_of(values, hot, places, tall):
    here = lax.broadcasted_iota(jnp.int32, (tall, values.shape[1]), 0) == places[0:1, :]
    left = jnp.concatenate([jnp.where(here, values[t : t + 1, :], 0.0) for t in range(STEPS)], axis=0)
    both = dot(jnp.concatenate(split(left), axis=0), hot[...], ((1,), (1,)))
    return both[: STEPS * tall] + both[STEPS * tall :]


def inject_kernel(hot, places, own, partner, *refs):
    gots, planes = refs[:-1], refs[-1]
    per = 6 * own.shape[2]
    values = [both_rows(lax.axis_index("trench"), own, partner)] + [got[0:STEPS, 0:per] for got in gots]
    planes[...] = planes_of(jnp.concatenate(values, axis=1), hot, places, planes.shape[0] // STEPS)


def advance_kernel(tiles, fields, cel, coef, hot, places, facing_in, facing_out, planes, *refs):
    outs, (stage, cel_ext) = refs[:-2], refs[-2:]
    blocks = len(outs)
    me = lax.axis_index("trench")
    rows, across = cel.shape
    tall = rows + 2 * PAD
    part = rows // blocks
    odd = me % 2 == 1
    facing = me // 2 + jnp.where(odd, 1, -1)
    top = facing_in.shape[0] - ROWS
    inner = facing_in[top:, :]
    outer = jnp.where((facing >= 0) & (facing < tiles // 2), facing_out[STEPS:, :], 0.0)
    before = jnp.where(odd, inner, outer)
    after = jnp.where(odd, outer, inner)

    count = passed_on(tiles)
    per = hot.shape[1] // count
    late = [facing_in[row : row + STEPS, at : at + per] for row, at in map(packed, range(count))]
    all_planes = planes[...] + planes_of(jnp.concatenate(late, axis=1), hot, places, tall)
    inject = [all_planes[tall * t : tall * t + tall] for t in range(STEPS)]

    cel_ext[...] = jnp.zeros((tall, across), jnp.float32)
    cel_ext[PAD - CEL_HALO : PAD, :] = before[CEL_AT:]
    cel_ext[PAD : PAD + rows, :] = cel[...]
    cel_ext[PAD + rows : PAD + rows + CEL_HALO, :] = after[CEL_AT:]


    row = lax.broadcasted_iota(jnp.int32, (tall, across), 0)
    speed = cel_ext[...]
    margin = jnp.zeros((PAD, across), jnp.float32)

    def own(n, k):
        return jnp.concatenate([margin, fields[FIELDS.index((n, k))], margin], axis=0)

    def horizontal(z, n, k):
        at = TRACED.index((n, k))
        facing = jnp.where(row == PAD + rows - 1, after[at : at + 1], 0.0)
        facing = jnp.where(row == PAD, before[at : at + 1], facing)
        around = pltpu.roll(z, 1, 0) + pltpu.roll(z, tall - 1, 0) + facing + beside(z)
        return speed * (around - 4.0 * z) + SHIFT * z

    def injected(n, k, a, b):
        total = None
        for tau in range(1, n - k + 1):
            r = n - tau
            term = coef[8 * r + k : 8 * r + k + 1, :] * inject[STEPS - tau][a:b]
            total = term if total is None else total + term
        return total

    base = horizontal(own(STEPS, STEPS), STEPS, STEPS)
    for n in range(1, STEPS + 1):
        z = base
        for k in range(n - 1, 0, -1):
            z = horizontal(z + own(n, k) + injected(n, k, 0, tall), n, k)
        series = z[PAD : PAD + rows] + fields[FIELDS.index((n, 0))] + injected(n, 0, PAD, PAD + rows)
        t = STEPS - n
        for b in range(blocks):
            stage[b, part * t : part * t + part, :] = series[part * b : part * b + part]
    block = lax.axis_index("tblock")
    for r, out in enumerate(outs):
        out[...] = stage[block ^ r]


def prior_kernel(*refs):
    gots, (weight, out, whole, done, sems) = refs[:-5], refs[-5:]
    block = lax.axis_index("tblock")
    for r, got in enumerate(reversed(gots)):
        whole[block ^ r] = got[...]
    part = out.shape[1]
    length = out.shape[0]
    width = weight.shape[0]
    factor = [weight[j : j + 1, :] for j in range(width)]
    copies = []

    def finish(p):
        if (p + 1) % (length // 4) == 0:
            cut = pl.ds(p + 1 - length // 4, length // 4)
            copies.append(pltpu.make_async_copy(done.at[cut], out.at[cut], sems.at[len(copies)]))
            copies[-1].start()

    if 2 * part != 8:
        series = [whole[i // STEPS, part * (i % STEPS) : part * (i % STEPS) + part, :] for i in range(length)]
        for k in range(length):
            done[k] = sum(factor[j] * series[k + j] for j in range(min(width, length - k)))
            finish(k)
        for copy in copies:
            copy.wait()
        return
    pairs = length // 2
    even = [whole[p // 2, 8 * (p % 2) : 8 * (p % 2) + 8, :] for p in range(pairs)]
    half = lax.broadcasted_iota(jnp.int32, even[0].shape, 0) < part
    turned = [pltpu.roll(x, part, 0) for x in even] + [jnp.zeros(even[0].shape, jnp.float32)]
    odd = [jnp.where(half, turned[p], turned[p + 1]) for p in range(pairs)]
    for p in range(pairs):
        total = None
        for j in range(width):
            if p + j // 2 < pairs:
                term = factor[j] * (odd if j % 2 else even)[p + j // 2]
                total = term if total is None else total + term
        done[2 * p] = total[:part]
        done[2 * p + 1] = total[part:]
        finish(2 * p + 1)
    for copy in copies:
        copy.wait()


def shape(*dims, dtype=jnp.float32):
    return jax.ShapeDtypeStruct(dims, dtype)


def spec(space):
    return pl.BlockSpec(memory_space=space)


def body(
    adjoint_eta,
    adjoint_flow,
    residual,
    sensor_cell,
    sensor_count,
    depth_class,
    speed_table,
    damping,
    profile,
    band_weight,
):
    tiles = lax.axis_size("trench")
    blocks = lax.axis_size("tblock")
    levels, rows, across = adjoint_eta.shape[1:]
    tall = rows + 2 * PAD
    params = pltpu.CompilerParams(vmem_limit_bytes=LIMIT)

    def swaps(parts, axis):
        devices = lax.axis_size(axis)
        moved = {r: lax.ppermute(parts[r], axis, [(i, i ^ r) for i in range(devices)]) for r in range(devices - 1, 0, -1)}
        return [parts[0]] + [moved[r] for r in range(1, devices)]

    own = residual[0, 0]
    slots = own.shape[2]
    chips = tiles // 2

    def meet(x, d):
        pairs = [(2 * c + 1, 2 * ((c + d) % chips)) for c in range(chips)]
        return lax.ppermute(x, "trench", pairs + [(j, i) for i, j in pairs])

    partner = meet(own, 0)
    matrix = shape(16 * (len(FIELDS) + 1), 8 * levels, dtype=jnp.bfloat16)
    w_eta, w_flow, cel, coef, factor, own, eta, flow = pl.pallas_call(
        prepare_kernel,
        out_shape=(
            matrix,
            matrix,
            shape(rows, across),
            shape(8 * STEPS, across),
            shape(band_weight.shape[0], across),
            shape(*own.shape),
            shape(*adjoint_eta.shape),
            shape(*adjoint_flow.shape),
        ),
        in_specs=[spec(pltpu.HBM)] * 8,
        out_specs=(spec(VMEM),) * 8,
        scratch_shapes=[
            VMEM((rows, across), jnp.int32),
            SMEM(speed_table.shape, jnp.float32),
            VMEM((1, levels), jnp.float32),
            VMEM((1, levels), jnp.float32),
            VMEM((1, band_weight.shape[0]), jnp.float32),
            pltpu.SemaphoreType.DMA((8,)),
        ],
        compiler_params=params,
        cost_estimate=pl.CostEstimate(flops=10**7, bytes_accessed=4 * 10**6, transcendentals=0),
        name="prepare",
    )(
        *[
            pltpu.with_memory_space_constraint(x, pltpu.HBM)
            for x in (
                depth_class, speed_table, damping[None], profile[None], band_weight[None],
                own, adjoint_eta, adjoint_flow,
            )
        ]
    )
    fields, inner, outer, *relays = pl.pallas_call(
        contract_kernel,
        out_shape=(
            shape(len(FIELDS), rows, across),
            shape(ROWS, across),
            shape(STEPS + ROWS, across),
        ) + tuple(
            shape(STEPS, 6 * slots * (2 if d <= passed_on(tiles) else 1)) for d in range(2, direct(tiles) + 1)
        ),
        in_specs=[spec(VMEM)] * 7,
        out_specs=(spec(VMEM),) * (2 + direct(tiles)),
        compiler_params=params,
        cost_estimate=pl.CostEstimate(flops=10**9, bytes_accessed=4 * 10**6, transcendentals=0),
        name="contract",
    )(eta, flow, w_eta, w_flow, cel, own, partner)
    facing_out = meet(outer, 1)
    gots = [facing_out] + [meet(relay, d) for d, relay in enumerate(relays, 2)]
    late = 2 * passed_on(tiles)

    def slot_shapes(count):
        return shape(across, 3 * slots * count, dtype=jnp.bfloat16), shape(8, 3 * slots * count, dtype=jnp.int32)

    hot, places, hot_late, places_late = pl.pallas_call(
        functools.partial(sensors_kernel, rows),
        out_shape=slot_shapes(tiles - late) + slot_shapes(late),
        in_specs=[spec(VMEM), spec(SMEM)],
        out_specs=(spec(VMEM),) * 4,
        compiler_params=params,
        cost_estimate=pl.CostEstimate(flops=10**6, bytes_accessed=2 * 10**6, transcendentals=0),
        name="sensors",
    )(sensor_cell, sensor_count)
    facing_in = meet(
        pl.pallas_call(
            functools.partial(pass_kernel, slots, passed_on(tiles)),
            out_shape=shape(STEPS * -(-passed_on(tiles) // 2) + ROWS, across),
            in_specs=[spec(VMEM), spec(pl.ANY)] + [spec(VMEM)] * len(gots),
            out_specs=spec(VMEM),
            compiler_params=params,
            name="pass",
        )(inner, places_late, *gots),
        0,
    )
    planes = pl.pallas_call(
        inject_kernel,
        out_shape=shape(STEPS * (rows + 2 * PAD), across),
        in_specs=[spec(VMEM)] * (4 + len(gots)),
        out_specs=spec(VMEM),
        compiler_params=params,
        cost_estimate=pl.CostEstimate(flops=10**8, bytes_accessed=4 * 10**6, transcendentals=0),
        name="inject",
    )(hot, places, own, partner, *gots)
    series = pl.pallas_call(
        functools.partial(advance_kernel, tiles),
        out_shape=(shape(STEPS * rows // blocks, across),) * blocks,
        in_specs=[spec(VMEM)] * 8,
        out_specs=(spec(VMEM),) * blocks,
        scratch_shapes=[
            VMEM((blocks, STEPS * rows // blocks, across), jnp.float32),
            VMEM((tall, across), jnp.float32),
        ],
        compiler_params=params,
        name="advance",
    )(fields, cel, coef, hot_late, places_late, facing_in, facing_out, planes)
    gots = swaps(series, "tblock")
    return pl.pallas_call(
        prior_kernel,
        out_shape=shape(STEPS * blocks, rows // blocks, across),
        in_specs=[spec(VMEM)] * (blocks + 1),
        out_specs=spec(pl.ANY),
        scratch_shapes=[
            VMEM((blocks, STEPS * rows // blocks, across), jnp.float32),
            VMEM((STEPS * blocks, rows // blocks, across), jnp.float32),
            pltpu.SemaphoreType.DMA((4,)),
        ],
        compiler_params=params,
        name="prior",
    )(*reversed(gots), factor)


def solution(mesh):
    in_specs = (
        P("tblock", None, "trench", None),
        P("tblock", None, "trench", None),
        P("tblock", "trench", None, None, None),
        P(),
        P(),
        P("trench", None),
        P(),
        P(),
        P(),
        P(),
    )
    out_specs = P(None, ("trench", "tblock"), None)
    return jax.shard_map(body, mesh=mesh, in_specs=in_specs, out_specs=out_specs, check_vma=False)
```

```python
import functools
import math

import jax
import jax.numpy as jnp
from jax import lax
from jax.experimental import pallas as pl
from jax.experimental.pallas import tpu as pltpu
from jax.sharding import PartitionSpec as P

VERT = 0.2
STEPS = 4
PAD = 8
VMEM = pltpu.VMEM
SMEM = pltpu.SMEM
LIMIT = 32 * 1024 * 1024

SHIFT = 1.2

FIELDS = [(4, 4), (4, 3), (4, 2), (3, 2), (4, 1), (3, 1), (2, 1), (4, 0), (3, 0), (2, 0), (1, 0)]
HALO = [4, 3, 2, 2, 1, 1, 1]
HALO_AT = [0, 4, 7, 9, 11, 12, 13]
CEL_AT = 14
CEL_HALO = 3
ROWS = 17


def split(x):
    hi = x.astype(jnp.bfloat16)
    return hi, (x - hi.astype(jnp.float32)).astype(jnp.bfloat16)


def dot(a, b, dims=((1,), (0,))):
    return lax.dot_general(a, b, (dims, ((), ())), preferred_element_type=jnp.float32)


def prepare_kernel(
    depth, table, damping, profile, band, residual, eta, flow,
    w_eta, w_flow, cel, coef, factor, own, eta_v, flow_v,
    depth_v, table_s, damping_v, profile_v, band_v, sems,
):
    rows, across = cel.shape
    levels = damping.shape[1]
    copies = [
        pltpu.make_async_copy(src, dst, sems.at[i])
        for i, (src, dst) in enumerate((
            (damping, damping_v), (profile, profile_v), (table, table_s), (depth, depth_v),
            (band, band_v), (residual, own), (eta, eta_v), (flow, flow_v),
        ))
    ]
    for copy in copies:
        copy.start()
    for copy in copies[:-2]:
        copy.wait()

    classes = depth_v[...]
    speed = jnp.zeros(classes.shape, jnp.float32)
    for c in range(table_s.shape[0]):
        speed = jnp.where(classes == c, table_s[c], speed)
    cel[...] = speed
    for j in range(factor.shape[0]):
        factor[j : j + 1, :] = jnp.broadcast_to(band_v[:, j : j + 1], (1, across))

    lane = lax.broadcasted_iota(jnp.int32, (8, 128), 1)
    sub = lax.broadcasted_iota(jnp.int32, (8, 128), 0)
    inside = lane < levels
    fill = jnp.zeros((1, 128 - levels), jnp.float32)
    keep = jnp.broadcast_to(jnp.concatenate([damping_v[...], fill], axis=1), (8, 128))
    weight = jnp.broadcast_to(jnp.concatenate([profile_v[...], fill], axis=1), (8, 128))
    u = jnp.zeros((8, 128), jnp.float32)
    v = jnp.where(sub == 0, weight * (1.0 / math.sqrt(levels)), 0.0)
    us, vs = [u], [v]
    for r in range(STEPS):
        s = u + v
        bottom = jnp.sum(jnp.where(lane == levels - 1, s, 0.0), axis=1, keepdims=True)
        coef[8 * r : 8 * r + 8, :] = jnp.broadcast_to(bottom, (8, coef.shape[1]))
        vertical = pltpu.roll(s, 1, 1) + pltpu.roll(s, 127, 1) - 2.0 * s
        u = jnp.where(inside, u + VERT * vertical - SHIFT * s + pltpu.roll(s, 1, 0), 0.0)
        v = s * keep
        us.append(u)
        vs.append(v)

    wide = w_eta.shape[1]
    spread = (
        lax.broadcasted_iota(jnp.int32, (128, wide), 1) // 8
        == lax.broadcasted_iota(jnp.int32, (128, wide), 0)
    ).astype(jnp.bfloat16)
    count_f = len(FIELDS) + 1
    diagonal = (
        lax.broadcasted_iota(jnp.int32, (8 * count_f, wide), 1) % 8
        == lax.broadcasted_iota(jnp.int32, (8 * count_f, wide), 0) % 8
    )

    def matrix(vectors):
        blocks = [jnp.broadcast_to(vectors[n][k : k + 1, :], (8, 128)) for n, k in FIELDS]
        blocks.append(jnp.zeros((8, 128), jnp.float32))
        hi, lo = split(jnp.concatenate(blocks, axis=0))
        zero = jnp.zeros((8 * count_f, wide), jnp.float32)
        hi = jnp.where(diagonal, dot(hi, spread), zero).astype(jnp.bfloat16)
        lo = jnp.where(diagonal, dot(lo, spread), zero).astype(jnp.bfloat16)
        return jnp.concatenate([hi, lo], axis=0)

    w_eta[...] = matrix(us)
    w_flow[...] = matrix(vs)

    for copy in copies[-2:]:
        copy.wait()


def contract_kernel(eta, flow, w_eta, w_flow, cel, own, partner, fields, inner, outer, *relays):
    levels, rows, across = eta.shape[1:]
    wide = w_eta.shape[1]
    half = w_eta.shape[0] // 2
    for h in range(rows // 8):
        hi, lo = split(eta[0, :, 8 * h : 8 * h + 8, :].reshape(wide, across))
        total = dot(w_eta[...], hi)
        part = dot(w_eta[0:half, :], lo)
        hi, lo = split(flow[0, :, 8 * h : 8 * h + 8, :].reshape(wide, across))
        total += dot(w_flow[...], hi)
        part += dot(w_flow[0:half, :], lo)
        part = part + total[:half] + total[half:]
        for f in range(len(FIELDS)):
            fields[f, 8 * h : 8 * h + 8, :] = part[8 * f : 8 * f + 8]

    me = lax.axis_index("trench")
    tiles = own.shape[0]
    for d, out in enumerate((outer, *relays), 1):
        out[0:STEPS, :] = widen([both_rows(met(me, d, tiles), own, partner)], out.shape[1])

    def edge(out, at, last):
        for f, width in enumerate(HALO):
            start = rows - width if last else 0
            out[at + HALO_AT[f] : at + HALO_AT[f] + width, :] = fields[f, start : start + width, :]
        start = rows - CEL_HALO if last else 0
        out[at + CEL_AT : at + CEL_AT + CEL_HALO, :] = cel[start : start + CEL_HALO, :]

    @pl.when(me % 2 == 0)
    def _():
        edge(inner, 0, True)
        edge(outer, STEPS, False)

    @pl.when(me % 2 == 1)
    def _():
        edge(inner, 0, False)
        edge(outer, STEPS, True)


def met(me, d, tiles):
    odd = me % 2
    chip = (me // 2 + jnp.where(odd == 1, d, tiles // 2 - d)) % (tiles // 2)
    return jnp.where(d == 0, me, 2 * chip + 1 - odd)


def sources(me, tiles):
    listed = [met(me, d, tiles) ^ core for d in range(tiles // 2) for core in range(2)]
    return listed[:-2], listed[-2:]


def widen(values, lanes):
    fill = lanes - sum(value.shape[1] for value in values)
    if fill:
        values = values + [jnp.zeros((STEPS, fill), jnp.float32)]
    return jnp.concatenate(values, axis=1)


def residual_rows(owner, own):
    tiles = own.shape[0]
    return jnp.concatenate([own[jnp.clip(owner + d - 1, 0, tiles - 1)] for d in range(3)], axis=1)


def both_rows(owner, own, partner):
    return jnp.concatenate([residual_rows(owner, own), residual_rows(owner, partner)], axis=1)


def sensors_kernel(rows, cells, count, hot_early, places_early, hot_late, places_late):
    me = lax.axis_index("trench")
    tiles, _, slots = cells.shape
    across = hot_early.shape[0]
    slot = lax.broadcasted_iota(jnp.int32, (1, slots), 1)
    bits = across.bit_length() - 1

    def list_slots(listed_sources, hot, places):
        listed = []
        for source in listed_sources:
            for d in range(3):
                owner = me + d - 1
                inside = (owner >= 0) & (owner < tiles)
                owner = jnp.clip(owner, 0, tiles - 1)
                live = jnp.where(inside, count[source, owner], 0)
                listed.append(jnp.where(slot < live, cells[source, pl.ds(owner, 1), :], -1))
        listed = jnp.concatenate(listed, axis=1)
        tile = (lax.broadcasted_iota(jnp.int32, listed.shape, 1) // slots) % 3
        at = jnp.where(listed < 0, -1, (listed >> bits) + (rows * (tile - 1) + PAD))
        places[...] = jnp.broadcast_to(at, places.shape)
        columns = listed & (across - 1)
        hot[...] = jnp.where(lax.broadcasted_iota(jnp.int32, hot.shape, 0) == columns, 1.0, 0.0).astype(jnp.bfloat16)

    early, late = sources(me, tiles)
    list_slots(early, hot_early, places_early)
    list_slots(late, hot_late, places_late)


def planes_of(values, hot, places, tall):
    here = lax.broadcasted_iota(jnp.int32, (tall, values.shape[1]), 0) == places[0:1, :]
    left = jnp.concatenate([jnp.where(here, values[t : t + 1, :], 0.0) for t in range(STEPS)], axis=0)
    both = dot(jnp.concatenate(split(left), axis=0), hot[...], ((1,), (1,)))
    return both[: STEPS * tall] + both[STEPS * tall :]


def inject_kernel(hot, places, own, partner, *refs):
    gots, planes = refs[:-1], refs[-1]
    per = 6 * own.shape[2]
    values = [both_rows(lax.axis_index("trench"), own, partner)] + [got[0:STEPS, 0:per] for got in gots]
    planes[...] = planes_of(jnp.concatenate(values, axis=1), hot, places, planes.shape[0] // STEPS)


def advance_kernel(tiles, fields, cel, coef, hot, places, facing_in, facing_out, last, planes, *refs):
    outs, (stage, ext, cel_ext) = refs[:-3], refs[-3:]
    blocks = len(outs)
    me = lax.axis_index("trench")
    rows, across = cel.shape
    tall = rows + 2 * PAD
    part = rows // blocks
    odd = me % 2 == 1
    facing = me // 2 + jnp.where(odd, 1, -1)
    inner = facing_in[...]
    outer = jnp.where((facing >= 0) & (facing < tiles // 2), facing_out[STEPS:, :], 0.0)
    before = jnp.where(odd, inner, outer)
    after = jnp.where(odd, outer, inner)

    all_planes = planes[...] + planes_of(last[0:STEPS, 0 : hot.shape[1]], hot, places, tall)
    inject = [all_planes[tall * t : tall * t + tall] for t in range(STEPS)]

    def extend(store, own, at, width):
        store(0, PAD, jnp.zeros((PAD, across), jnp.float32))
        store(PAD + rows, tall, jnp.zeros((PAD, across), jnp.float32))
        store(PAD, PAD + rows, own)
        store(PAD - width, PAD, before[at : at + width])
        store(PAD + rows, PAD + rows + width, after[at : at + width])

    for f, width in enumerate(HALO):
        def store(a, b, value, f=f):
            ext[f, a:b, :] = value
        extend(store, fields[f], HALO_AT[f], width)

    def store_cel(a, b, value):
        cel_ext[a:b, :] = value
    extend(store_cel, cel[...], CEL_AT, CEL_HALO)

    lane = lax.broadcasted_iota(jnp.int32, (tall, across), 1)
    first = lane == 0
    last = lane == across - 1
    speed = cel_ext[...]

    def horizontal(z):
        around = pltpu.roll(z, 1, 0) + pltpu.roll(z, tall - 1, 0)
        around += jnp.where(first, 0.0, pltpu.roll(z, 1, 1))
        around += jnp.where(last, 0.0, pltpu.roll(z, across - 1, 1))
        return speed * (around - 4.0 * z) + SHIFT * z

    def injected(n, k, a, b):
        total = None
        for tau in range(1, n - k + 1):
            r = n - tau
            term = coef[8 * r + k : 8 * r + k + 1, :] * inject[STEPS - tau][a:b]
            total = term if total is None else total + term
        return total

    base = horizontal(ext[0])
    for n in range(1, STEPS + 1):
        z = base
        for k in range(n - 1, 0, -1):
            z = horizontal(z + ext[FIELDS.index((n, k))] + injected(n, k, 0, tall))
        own = z[PAD : PAD + rows] + fields[FIELDS.index((n, 0))] + injected(n, 0, PAD, PAD + rows)
        t = STEPS - n
        for b in range(blocks):
            stage[b, part * t : part * t + part, :] = own[part * b : part * b + part]
    block = lax.axis_index("tblock")
    for r, out in enumerate(outs):
        out[...] = stage[block ^ r]


def prior_kernel(*refs):
    gots, (weight, out, whole, done, sems) = refs[:-5], refs[-5:]
    block = lax.axis_index("tblock")
    for r, got in enumerate(reversed(gots)):
        whole[block ^ r] = got[...]
    part = out.shape[1]
    length = out.shape[0]
    width = weight.shape[0]
    factor = [weight[j : j + 1, :] for j in range(width)]
    copies = []

    def finish(p):
        if (p + 1) % (length // 4) == 0:
            cut = pl.ds(p + 1 - length // 4, length // 4)
            copies.append(pltpu.make_async_copy(done.at[cut], out.at[cut], sems.at[len(copies)]))
            copies[-1].start()

    if 2 * part != 8:
        series = [whole[i // STEPS, part * (i % STEPS) : part * (i % STEPS) + part, :] for i in range(length)]
        for k in range(length):
            done[k] = sum(factor[j] * series[k + j] for j in range(min(width, length - k)))
            finish(k)
        for copy in copies:
            copy.wait()
        return
    pairs = length // 2
    even = [whole[p // 2, 8 * (p % 2) : 8 * (p % 2) + 8, :] for p in range(pairs)]
    half = lax.broadcasted_iota(jnp.int32, even[0].shape, 0) < part
    turned = [pltpu.roll(x, part, 0) for x in even] + [jnp.zeros(even[0].shape, jnp.float32)]
    odd = [jnp.where(half, turned[p], turned[p + 1]) for p in range(pairs)]
    for p in range(pairs):
        total = None
        for j in range(width):
            if p + j // 2 < pairs:
                term = factor[j] * (odd if j % 2 else even)[p + j // 2]
                total = term if total is None else total + term
        done[2 * p] = total[:part]
        done[2 * p + 1] = total[part:]
        finish(2 * p + 1)
    for copy in copies:
        copy.wait()


def shape(*dims, dtype=jnp.float32):
    return jax.ShapeDtypeStruct(dims, dtype)


def spec(space):
    return pl.BlockSpec(memory_space=space)


def body(
    adjoint_eta,
    adjoint_flow,
    residual,
    sensor_cell,
    sensor_count,
    depth_class,
    speed_table,
    damping,
    profile,
    band_weight,
):
    tiles = lax.axis_size("trench")
    blocks = lax.axis_size("tblock")
    levels, rows, across = adjoint_eta.shape[1:]
    tall = rows + 2 * PAD
    params = pltpu.CompilerParams(vmem_limit_bytes=LIMIT)

    def swaps(parts, axis):
        devices = lax.axis_size(axis)
        moved = {r: lax.ppermute(parts[r], axis, [(i, i ^ r) for i in range(devices)]) for r in range(devices - 1, 0, -1)}
        return [parts[0]] + [moved[r] for r in range(1, devices)]

    own = residual[0, 0]
    slots = own.shape[2]
    chips = tiles // 2

    def meet(x, d):
        pairs = [(2 * c + 1, 2 * ((c + d) % chips)) for c in range(chips)]
        return lax.ppermute(x, "trench", pairs + [(j, i) for i, j in pairs])

    partner = meet(own, 0)
    matrix = shape(16 * (len(FIELDS) + 1), 8 * levels, dtype=jnp.bfloat16)
    w_eta, w_flow, cel, coef, factor, own, eta, flow = pl.pallas_call(
        prepare_kernel,
        out_shape=(
            matrix,
            matrix,
            shape(rows, across),
            shape(8 * STEPS, across),
            shape(band_weight.shape[0], across),
            shape(*own.shape),
            shape(*adjoint_eta.shape),
            shape(*adjoint_flow.shape),
        ),
        in_specs=[spec(pltpu.HBM)] * 8,
        out_specs=(spec(VMEM),) * 8,
        scratch_shapes=[
            VMEM((rows, across), jnp.int32),
            SMEM(speed_table.shape, jnp.float32),
            VMEM((1, levels), jnp.float32),
            VMEM((1, levels), jnp.float32),
            VMEM((1, band_weight.shape[0]), jnp.float32),
            pltpu.SemaphoreType.DMA((8,)),
        ],
        compiler_params=params,
        cost_estimate=pl.CostEstimate(flops=10**7, bytes_accessed=4 * 10**6, transcendentals=0),
        name="prepare",
    )(
        *[
            pltpu.with_memory_space_constraint(x, pltpu.HBM)
            for x in (
                depth_class, speed_table, damping[None], profile[None], band_weight[None],
                own, adjoint_eta, adjoint_flow,
            )
        ]
    )
    fields, inner, outer, *relays = pl.pallas_call(
        contract_kernel,
        out_shape=(
            shape(len(FIELDS), rows, across),
            shape(ROWS, across),
            shape(STEPS + ROWS, across),
        ) + (shape(STEPS, 6 * slots),) * (chips - 2),
        in_specs=[spec(VMEM)] * 7,
        out_specs=(spec(VMEM),) * (1 + chips),
        compiler_params=params,
        cost_estimate=pl.CostEstimate(flops=10**9, bytes_accessed=4 * 10**6, transcendentals=0),
        name="contract",
    )(eta, flow, w_eta, w_flow, cel, own, partner)
    facing_out = meet(outer, 1)
    gots = [facing_out] + [meet(relay, d) for d, relay in enumerate(relays, 2)]
    facing_in = meet(inner, 0)

    def slot_shapes(count):
        return shape(across, 3 * slots * count, dtype=jnp.bfloat16), shape(8, 3 * slots * count, dtype=jnp.int32)

    hot, places, hot_late, places_late = pl.pallas_call(
        functools.partial(sensors_kernel, rows),
        out_shape=slot_shapes(tiles - 2) + slot_shapes(2),
        in_specs=[spec(VMEM), spec(SMEM)],
        out_specs=(spec(VMEM),) * 4,
        compiler_params=params,
        cost_estimate=pl.CostEstimate(flops=10**6, bytes_accessed=2 * 10**6, transcendentals=0),
        name="sensors",
    )(sensor_cell, sensor_count)
    planes = pl.pallas_call(
        inject_kernel,
        out_shape=shape(STEPS * (rows + 2 * PAD), across),
        in_specs=[spec(VMEM)] * (3 + len(gots)),
        out_specs=spec(VMEM),
        compiler_params=params,
        cost_estimate=pl.CostEstimate(flops=1000, bytes_accessed=1000, transcendentals=0),
        name="inject",
    )(hot, places, own, partner, *gots[:-1])
    series = pl.pallas_call(
        functools.partial(advance_kernel, tiles),
        out_shape=(shape(STEPS * rows // blocks, across),) * blocks,
        in_specs=[spec(VMEM)] * 9,
        out_specs=(spec(VMEM),) * blocks,
        scratch_shapes=[
            VMEM((blocks, STEPS * rows // blocks, across), jnp.float32),
            VMEM((len(HALO), tall, across), jnp.float32),
            VMEM((tall, across), jnp.float32),
        ],
        compiler_params=params,
        name="advance",
    )(fields, cel, coef, hot_late, places_late, facing_in, facing_out, gots[-1], planes)
    gots = swaps(series, "tblock")
    return pl.pallas_call(
        prior_kernel,
        out_shape=shape(STEPS * blocks, rows // blocks, across),
        in_specs=[spec(VMEM)] * (blocks + 1),
        out_specs=spec(pl.ANY),
        scratch_shapes=[
            VMEM((blocks, STEPS * rows // blocks, across), jnp.float32),
            VMEM((STEPS * blocks, rows // blocks, across), jnp.float32),
            pltpu.SemaphoreType.DMA((4,)),
        ],
        compiler_params=params,
        name="prior",
    )(*reversed(gots), factor)


def solution(mesh):
    in_specs = (
        P("tblock", None, "trench", None),
        P("tblock", None, "trench", None),
        P("tblock", "trench", None, None, None),
        P(),
        P(),
        P("trench", None),
        P(),
        P(),
        P(),
        P(),
    )
    out_specs = P(None, ("trench", "tblock"), None)
    return jax.shard_map(body, mesh=mesh, in_specs=in_specs, out_specs=out_specs, check_vma=False)
```

```python
import functools
import math

import jax
import jax.numpy as jnp
from jax import lax
from jax.experimental import pallas as pl
from jax.experimental.pallas import tpu as pltpu
from jax.sharding import PartitionSpec as P

VERT = 0.2
STEPS = 4
PAD = 8
VMEM = pltpu.VMEM
SMEM = pltpu.SMEM
LIMIT = 32 * 1024 * 1024

SHIFT = 1.2

FIELDS = [(4, 4), (4, 3), (4, 2), (3, 2), (4, 1), (3, 1), (2, 1), (4, 0), (3, 0), (2, 0), (1, 0)]
HALO = [4, 3, 2, 2, 1, 1, 1]
HALO_AT = [0, 4, 7, 9, 11, 12, 13]
CEL_AT = 14
CEL_HALO = 3
ROWS = 17


def split(x):
    hi = x.astype(jnp.bfloat16)
    return hi, (x - hi.astype(jnp.float32)).astype(jnp.bfloat16)


def dot(a, b, dims=((1,), (0,))):
    return lax.dot_general(a, b, (dims, ((), ())), preferred_element_type=jnp.float32)


def prepare_kernel(
    depth, table, damping, profile, band, cells, count, residual, eta, flow,
    w_eta, w_flow, cel, coef, factor, hot_early, places_early, hot_late, places_late, own, eta_v, flow_v,
    depth_v, table_s, damping_v, profile_v, band_v, cells_v, count_s, sems,
):
    rows, across = cel.shape
    levels = damping.shape[1]
    copies = [
        pltpu.make_async_copy(src, dst, sems.at[i])
        for i, (src, dst) in enumerate((
            (damping, damping_v), (profile, profile_v), (table, table_s), (depth, depth_v),
            (band, band_v), (cells, cells_v), (count, count_s), (residual, own), (eta, eta_v), (flow, flow_v),
        ))
    ]
    for copy in copies:
        copy.start()
    for copy in copies[:-2]:
        copy.wait()

    classes = depth_v[...]
    speed = jnp.zeros(classes.shape, jnp.float32)
    for c in range(table_s.shape[0]):
        speed = jnp.where(classes == c, table_s[c], speed)
    cel[...] = speed
    for j in range(factor.shape[0]):
        factor[j : j + 1, :] = jnp.broadcast_to(band_v[:, j : j + 1], (1, across))

    lane = lax.broadcasted_iota(jnp.int32, (8, 128), 1)
    sub = lax.broadcasted_iota(jnp.int32, (8, 128), 0)
    inside = lane < levels
    fill = jnp.zeros((1, 128 - levels), jnp.float32)
    keep = jnp.broadcast_to(jnp.concatenate([damping_v[...], fill], axis=1), (8, 128))
    weight = jnp.broadcast_to(jnp.concatenate([profile_v[...], fill], axis=1), (8, 128))
    u = jnp.zeros((8, 128), jnp.float32)
    v = jnp.where(sub == 0, weight * (1.0 / math.sqrt(levels)), 0.0)
    us, vs = [u], [v]
    for r in range(STEPS):
        s = u + v
        bottom = jnp.sum(jnp.where(lane == levels - 1, s, 0.0), axis=1, keepdims=True)
        coef[8 * r : 8 * r + 8, :] = jnp.broadcast_to(bottom, (8, coef.shape[1]))
        vertical = pltpu.roll(s, 1, 1) + pltpu.roll(s, 127, 1) - 2.0 * s
        u = jnp.where(inside, u + VERT * vertical - SHIFT * s + pltpu.roll(s, 1, 0), 0.0)
        v = s * keep
        us.append(u)
        vs.append(v)

    wide = w_eta.shape[1]
    spread = (
        lax.broadcasted_iota(jnp.int32, (128, wide), 1) // 8
        == lax.broadcasted_iota(jnp.int32, (128, wide), 0)
    ).astype(jnp.bfloat16)
    count_f = len(FIELDS) + 1
    diagonal = (
        lax.broadcasted_iota(jnp.int32, (8 * count_f, wide), 1) % 8
        == lax.broadcasted_iota(jnp.int32, (8 * count_f, wide), 0) % 8
    )

    def matrix(vectors):
        blocks = [jnp.broadcast_to(vectors[n][k : k + 1, :], (8, 128)) for n, k in FIELDS]
        blocks.append(jnp.zeros((8, 128), jnp.float32))
        hi, lo = split(jnp.concatenate(blocks, axis=0))
        zero = jnp.zeros((8 * count_f, wide), jnp.float32)
        hi = jnp.where(diagonal, dot(hi, spread), zero).astype(jnp.bfloat16)
        lo = jnp.where(diagonal, dot(lo, spread), zero).astype(jnp.bfloat16)
        return jnp.concatenate([hi, lo], axis=0)

    w_eta[...] = matrix(us)
    w_flow[...] = matrix(vs)

    list_sensors(rows, cells_v, count_s, hot_early, places_early, hot_late, places_late)
    for copy in copies[-2:]:
        copy.wait()


def contract_kernel(eta, flow, w_eta, w_flow, cel, own, partner, fields, inner, outer, *relays):
    levels, rows, across = eta.shape[1:]
    wide = w_eta.shape[1]
    half = w_eta.shape[0] // 2
    for h in range(rows // 8):
        hi, lo = split(eta[0, :, 8 * h : 8 * h + 8, :].reshape(wide, across))
        total = dot(w_eta[...], hi)
        part = dot(w_eta[0:half, :], lo)
        hi, lo = split(flow[0, :, 8 * h : 8 * h + 8, :].reshape(wide, across))
        total += dot(w_flow[...], hi)
        part += dot(w_flow[0:half, :], lo)
        part = part + total[:half] + total[half:]
        for f in range(len(FIELDS)):
            fields[f, 8 * h : 8 * h + 8, :] = part[8 * f : 8 * f + 8]

    me = lax.axis_index("trench")
    tiles = own.shape[0]
    for d, out in enumerate((outer, *relays), 1):
        out[0:STEPS, :] = widen([both_rows(met(me, d, tiles), own, partner)], out.shape[1])

    def edge(out, at, last):
        for f, width in enumerate(HALO):
            start = rows - width if last else 0
            out[at + HALO_AT[f] : at + HALO_AT[f] + width, :] = fields[f, start : start + width, :]
        start = rows - CEL_HALO if last else 0
        out[at + CEL_AT : at + CEL_AT + CEL_HALO, :] = cel[start : start + CEL_HALO, :]

    @pl.when(me % 2 == 0)
    def _():
        edge(inner, 0, True)
        edge(outer, STEPS, False)

    @pl.when(me % 2 == 1)
    def _():
        edge(inner, 0, False)
        edge(outer, STEPS, True)


def met(me, d, tiles):
    odd = me % 2
    chip = (me // 2 + jnp.where(odd == 1, d, tiles // 2 - d)) % (tiles // 2)
    return jnp.where(d == 0, me, 2 * chip + 1 - odd)


def sources(me, tiles):
    def at(distances):
        return [met(me, d, tiles) ^ core for d in distances for core in range(2)]

    half = tiles // 4
    return at(d for d in range(tiles // 2) if d != half), at([half])


def widen(values, lanes):
    fill = lanes - sum(value.shape[1] for value in values)
    if fill:
        values = values + [jnp.zeros((STEPS, fill), jnp.float32)]
    return jnp.concatenate(values, axis=1)


def residual_rows(owner, own):
    tiles = own.shape[0]
    return jnp.concatenate([own[jnp.clip(owner + d - 1, 0, tiles - 1)] for d in range(3)], axis=1)


def both_rows(owner, own, partner):
    return jnp.concatenate([residual_rows(owner, own), residual_rows(owner, partner)], axis=1)


def list_sensors(rows, cells, count, hot_early, places_early, hot_late, places_late):
    me = lax.axis_index("trench")
    tiles, _, slots = cells.shape
    across = hot_early.shape[0]
    slot = lax.broadcasted_iota(jnp.int32, (1, slots), 1)
    bits = across.bit_length() - 1

    def list_slots(listed_sources, hot, places):
        listed = []
        for source in listed_sources:
            for d in range(3):
                owner = me + d - 1
                inside = (owner >= 0) & (owner < tiles)
                owner = jnp.clip(owner, 0, tiles - 1)
                live = jnp.where(inside, count[source, owner], 0)
                listed.append(jnp.where(slot < live, cells[source, pl.ds(owner, 1), :], -1))
        listed = jnp.concatenate(listed, axis=1)
        tile = (lax.broadcasted_iota(jnp.int32, listed.shape, 1) // slots) % 3
        at = jnp.where(listed < 0, -1, (listed >> bits) + (rows * (tile - 1) + PAD))
        places[...] = jnp.broadcast_to(at, places.shape)
        columns = listed & (across - 1)
        hot[...] = jnp.where(lax.broadcasted_iota(jnp.int32, hot.shape, 0) == columns, 1.0, 0.0).astype(jnp.bfloat16)

    early, late = sources(me, tiles)
    list_slots(early, hot_early, places_early)
    list_slots(late, hot_late, places_late)


def planes_of(values, hot, places, tall):
    here = lax.broadcasted_iota(jnp.int32, (tall, values.shape[1]), 0) == places[0:1, :]
    left = jnp.concatenate([jnp.where(here, values[t : t + 1, :], 0.0) for t in range(STEPS)], axis=0)
    both = dot(jnp.concatenate(split(left), axis=0), hot[...], ((1,), (1,)))
    return both[: STEPS * tall] + both[STEPS * tall :]


def inject_kernel(hot, places, own, partner, *refs):
    gots, planes = refs[:-1], refs[-1]
    per = 6 * own.shape[2]
    values = [both_rows(lax.axis_index("trench"), own, partner)] + [got[0:STEPS, 0:per] for got in gots]
    planes[...] = planes_of(jnp.concatenate(values, axis=1), hot, places, planes.shape[0] // STEPS)


def advance_kernel(tiles, fields, cel, coef, hot, places, facing_in, facing_out, last, planes, *refs):
    outs, (stage, ext, cel_ext) = refs[:-3], refs[-3:]
    blocks = len(outs)
    me = lax.axis_index("trench")
    rows, across = cel.shape
    tall = rows + 2 * PAD
    part = rows // blocks
    odd = me % 2 == 1
    facing = me // 2 + jnp.where(odd, 1, -1)
    inner = facing_in[...]
    outer = jnp.where((facing >= 0) & (facing < tiles // 2), facing_out[STEPS:, :], 0.0)
    before = jnp.where(odd, inner, outer)
    after = jnp.where(odd, outer, inner)

    all_planes = planes[...] + planes_of(last[0:STEPS, 0 : hot.shape[1]], hot, places, tall)
    inject = [all_planes[tall * t : tall * t + tall] for t in range(STEPS)]

    def extend(store, own, at, width):
        store(0, PAD, jnp.zeros((PAD, across), jnp.float32))
        store(PAD + rows, tall, jnp.zeros((PAD, across), jnp.float32))
        store(PAD, PAD + rows, own)
        store(PAD - width, PAD, before[at : at + width])
        store(PAD + rows, PAD + rows + width, after[at : at + width])

    for f, width in enumerate(HALO):
        def store(a, b, value, f=f):
            ext[f, a:b, :] = value
        extend(store, fields[f], HALO_AT[f], width)

    def store_cel(a, b, value):
        cel_ext[a:b, :] = value
    extend(store_cel, cel[...], CEL_AT, CEL_HALO)

    lane = lax.broadcasted_iota(jnp.int32, (tall, across), 1)
    first = lane == 0
    last = lane == across - 1
    speed = cel_ext[...]

    def horizontal(z):
        around = pltpu.roll(z, 1, 0) + pltpu.roll(z, tall - 1, 0)
        around += jnp.where(first, 0.0, pltpu.roll(z, 1, 1))
        around += jnp.where(last, 0.0, pltpu.roll(z, across - 1, 1))
        return speed * (around - 4.0 * z) + SHIFT * z

    def injected(n, k, a, b):
        total = None
        for tau in range(1, n - k + 1):
            r = n - tau
            term = coef[8 * r + k : 8 * r + k + 1, :] * inject[STEPS - tau][a:b]
            total = term if total is None else total + term
        return total

    base = horizontal(ext[0])
    for n in range(1, STEPS + 1):
        z = base
        for k in range(n - 1, 0, -1):
            z = horizontal(z + ext[FIELDS.index((n, k))] + injected(n, k, 0, tall))
        own = z[PAD : PAD + rows] + fields[FIELDS.index((n, 0))] + injected(n, 0, PAD, PAD + rows)
        t = STEPS - n
        for b in range(blocks):
            stage[b, part * t : part * t + part, :] = own[part * b : part * b + part]
    block = lax.axis_index("tblock")
    for r, out in enumerate(outs):
        out[...] = stage[block ^ r]


def prior_kernel(*refs):
    gots, (weight, out, whole, done, sems) = refs[:-5], refs[-5:]
    block = lax.axis_index("tblock")
    for r, got in enumerate(reversed(gots)):
        whole[block ^ r] = got[...]
    part = out.shape[1]
    length = out.shape[0]
    width = weight.shape[0]
    factor = [weight[j : j + 1, :] for j in range(width)]
    copies = []

    def finish(p):
        if (p + 1) % (length // 4) == 0:
            cut = pl.ds(p + 1 - length // 4, length // 4)
            copies.append(pltpu.make_async_copy(done.at[cut], out.at[cut], sems.at[len(copies)]))
            copies[-1].start()

    if 2 * part != 8:
        series = [whole[i // STEPS, part * (i % STEPS) : part * (i % STEPS) + part, :] for i in range(length)]
        for k in range(length):
            done[k] = sum(factor[j] * series[k + j] for j in range(min(width, length - k)))
            finish(k)
        for copy in copies:
            copy.wait()
        return
    pairs = length // 2
    even = [whole[p // 2, 8 * (p % 2) : 8 * (p % 2) + 8, :] for p in range(pairs)]
    half = lax.broadcasted_iota(jnp.int32, even[0].shape, 0) < part
    turned = [pltpu.roll(x, part, 0) for x in even] + [jnp.zeros(even[0].shape, jnp.float32)]
    odd = [jnp.where(half, turned[p], turned[p + 1]) for p in range(pairs)]
    for p in range(pairs):
        total = None
        for j in range(width):
            if p + j // 2 < pairs:
                term = factor[j] * (odd if j % 2 else even)[p + j // 2]
                total = term if total is None else total + term
        done[2 * p] = total[:part]
        done[2 * p + 1] = total[part:]
        finish(2 * p + 1)
    for copy in copies:
        copy.wait()


def shape(*dims, dtype=jnp.float32):
    return jax.ShapeDtypeStruct(dims, dtype)


def spec(space):
    return pl.BlockSpec(memory_space=space)


def body(
    adjoint_eta,
    adjoint_flow,
    residual,
    sensor_cell,
    sensor_count,
    depth_class,
    speed_table,
    damping,
    profile,
    band_weight,
):
    tiles = lax.axis_size("trench")
    blocks = lax.axis_size("tblock")
    levels, rows, across = adjoint_eta.shape[1:]
    tall = rows + 2 * PAD
    params = pltpu.CompilerParams(vmem_limit_bytes=LIMIT)

    def swaps(parts, axis):
        devices = lax.axis_size(axis)
        moved = {r: lax.ppermute(parts[r], axis, [(i, i ^ r) for i in range(devices)]) for r in range(devices - 1, 0, -1)}
        return [parts[0]] + [moved[r] for r in range(1, devices)]

    own = residual[0, 0]
    slots = own.shape[2]
    chips = tiles // 2

    def meet(x, d):
        pairs = [(2 * c + 1, 2 * ((c + d) % chips)) for c in range(chips)]
        return lax.ppermute(x, "trench", pairs + [(j, i) for i, j in pairs])

    partner = meet(own, 0)
    def slot_shapes(count):
        return shape(across, 3 * slots * count, dtype=jnp.bfloat16), shape(8, 3 * slots * count, dtype=jnp.int32)

    matrix = shape(16 * (len(FIELDS) + 1), 8 * levels, dtype=jnp.bfloat16)
    w_eta, w_flow, cel, coef, factor, hot, places, hot_late, places_late, own, eta, flow = pl.pallas_call(
        prepare_kernel,
        out_shape=(
            matrix,
            matrix,
            shape(rows, across),
            shape(8 * STEPS, across),
            shape(band_weight.shape[0], across),
            *slot_shapes(tiles - 2),
            *slot_shapes(2),
            shape(*own.shape),
            shape(*adjoint_eta.shape),
            shape(*adjoint_flow.shape),
        ),
        in_specs=[spec(pltpu.HBM)] * 10,
        out_specs=(spec(VMEM),) * 12,
        scratch_shapes=[
            VMEM((rows, across), jnp.int32),
            SMEM(speed_table.shape, jnp.float32),
            VMEM((1, levels), jnp.float32),
            VMEM((1, levels), jnp.float32),
            VMEM((1, band_weight.shape[0]), jnp.float32),
            VMEM(sensor_cell.shape, jnp.int32),
            SMEM(sensor_count.shape, jnp.int32),
            pltpu.SemaphoreType.DMA((10,)),
        ],
        compiler_params=params,
        cost_estimate=pl.CostEstimate(flops=10**7, bytes_accessed=4 * 10**6, transcendentals=0),
        name="prepare",
    )(
        *[
            pltpu.with_memory_space_constraint(x, pltpu.HBM)
            for x in (
                depth_class, speed_table, damping[None], profile[None], band_weight[None],
                sensor_cell, sensor_count, own, adjoint_eta, adjoint_flow,
            )
        ]
    )
    fields, inner, outer, *relays = pl.pallas_call(
        contract_kernel,
        out_shape=(
            shape(len(FIELDS), rows, across),
            shape(ROWS, across),
            shape(STEPS + ROWS, across),
        ) + (shape(STEPS, 6 * slots),) * (chips - 2),
        in_specs=[spec(VMEM)] * 7,
        out_specs=(spec(VMEM),) * (1 + chips),
        compiler_params=params,
        cost_estimate=pl.CostEstimate(flops=10**9, bytes_accessed=4 * 10**6, transcendentals=0),
        name="contract",
    )(eta, flow, w_eta, w_flow, cel, own, partner)
    facing_out = meet(outer, 1)
    gots = {d: meet(relay, d) for d, relay in enumerate(relays, 2)}
    last = gots.pop(chips // 2)
    gots = [facing_out, *gots.values()]
    facing_in = meet(inner, 0)

    planes = pl.pallas_call(
        inject_kernel,
        out_shape=shape(STEPS * (rows + 2 * PAD), across),
        in_specs=[spec(VMEM)] * (4 + len(gots)),
        out_specs=spec(VMEM),
        compiler_params=params,
        cost_estimate=pl.CostEstimate(flops=1000, bytes_accessed=1000, transcendentals=0),
        name="inject",
    )(hot, places, own, partner, *gots)
    series = pl.pallas_call(
        functools.partial(advance_kernel, tiles),
        out_shape=(shape(STEPS * rows // blocks, across),) * blocks,
        in_specs=[spec(VMEM)] * 9,
        out_specs=(spec(VMEM),) * blocks,
        scratch_shapes=[
            VMEM((blocks, STEPS * rows // blocks, across), jnp.float32),
            VMEM((len(HALO), tall, across), jnp.float32),
            VMEM((tall, across), jnp.float32),
        ],
        compiler_params=params,
        name="advance",
    )(fields, cel, coef, hot_late, places_late, facing_in, facing_out, last, planes)
    gots = swaps(series, "tblock")
    return pl.pallas_call(
        prior_kernel,
        out_shape=shape(STEPS * blocks, rows // blocks, across),
        in_specs=[spec(VMEM)] * (blocks + 1),
        out_specs=spec(pl.ANY),
        scratch_shapes=[
            VMEM((blocks, STEPS * rows // blocks, across), jnp.float32),
            VMEM((STEPS * blocks, rows // blocks, across), jnp.float32),
            pltpu.SemaphoreType.DMA((4,)),
        ],
        compiler_params=params,
        name="prior",
    )(*reversed(gots), factor)


def solution(mesh):
    in_specs = (
        P("tblock", None, "trench", None),
        P("tblock", None, "trench", None),
        P("tblock", "trench", None, None, None),
        P(),
        P(),
        P("trench", None),
        P(),
        P(),
        P(),
        P(),
    )
    out_specs = P(None, ("trench", "tblock"), None)
    return jax.shard_map(body, mesh=mesh, in_specs=in_specs, out_specs=out_specs, check_vma=False)
```

```python
import functools
import math

import jax
import jax.numpy as jnp
from jax import lax
from jax.experimental import pallas as pl
from jax.experimental.pallas import tpu as pltpu
from jax.sharding import PartitionSpec as P

VERT = 0.2
STEPS = 4
PAD = 8
VMEM = pltpu.VMEM
SMEM = pltpu.SMEM
LIMIT = 32 * 1024 * 1024

SHIFT = 1.2

FIELDS = [(4, 4), (4, 3), (4, 2), (3, 2), (4, 1), (3, 1), (2, 1), (4, 0), (3, 0), (2, 0), (1, 0)]
HALO = [4, 3, 2, 2, 1, 1, 1]
HALO_AT = [0, 4, 7, 9, 11, 12, 13]
CEL_AT = 14
CEL_HALO = 3
ROWS = 17


def split(x):
    hi = x.astype(jnp.bfloat16)
    return hi, (x - hi.astype(jnp.float32)).astype(jnp.bfloat16)


def dot(a, b, dims=((1,), (0,))):
    return lax.dot_general(a, b, (dims, ((), ())), preferred_element_type=jnp.float32)


def prepare_kernel(
    depth, table, damping, profile, band, cells, count, residual, eta, flow,
    w_eta, w_flow, cel, coef, factor, hot_early, places_early, hot_late, places_late, own, eta_v, flow_v,
    depth_v, table_s, damping_v, profile_v, band_v, cells_v, count_s, sems,
):
    rows, across = cel.shape
    levels = damping.shape[1]
    copies = [
        pltpu.make_async_copy(src, dst, sems.at[i])
        for i, (src, dst) in enumerate((
            (damping, damping_v), (profile, profile_v), (table, table_s), (depth, depth_v),
            (band, band_v), (cells, cells_v), (count, count_s), (residual, own), (eta, eta_v), (flow, flow_v),
        ))
    ]
    for copy in copies:
        copy.start()
    for copy in copies[:-2]:
        copy.wait()

    classes = depth_v[...]
    speed = jnp.zeros(classes.shape, jnp.float32)
    for c in range(table_s.shape[0]):
        speed = jnp.where(classes == c, table_s[c], speed)
    cel[...] = speed
    for j in range(factor.shape[0]):
        factor[j : j + 1, :] = jnp.broadcast_to(band_v[:, j : j + 1], (1, across))

    lane = lax.broadcasted_iota(jnp.int32, (8, 128), 1)
    sub = lax.broadcasted_iota(jnp.int32, (8, 128), 0)
    inside = lane < levels
    fill = jnp.zeros((1, 128 - levels), jnp.float32)
    keep = jnp.broadcast_to(jnp.concatenate([damping_v[...], fill], axis=1), (8, 128))
    weight = jnp.broadcast_to(jnp.concatenate([profile_v[...], fill], axis=1), (8, 128))
    u = jnp.zeros((8, 128), jnp.float32)
    v = jnp.where(sub == 0, weight * (1.0 / math.sqrt(levels)), 0.0)
    us, vs = [u], [v]
    for r in range(STEPS):
        s = u + v
        bottom = jnp.sum(jnp.where(lane == levels - 1, s, 0.0), axis=1, keepdims=True)
        coef[8 * r : 8 * r + 8, :] = jnp.broadcast_to(bottom, (8, coef.shape[1]))
        vertical = pltpu.roll(s, 1, 1) + pltpu.roll(s, 127, 1) - 2.0 * s
        u = jnp.where(inside, u + VERT * vertical - SHIFT * s + pltpu.roll(s, 1, 0), 0.0)
        v = s * keep
        us.append(u)
        vs.append(v)

    wide = w_eta.shape[1]
    spread = (
        lax.broadcasted_iota(jnp.int32, (128, wide), 1) // 8
        == lax.broadcasted_iota(jnp.int32, (128, wide), 0)
    ).astype(jnp.bfloat16)
    count_f = len(FIELDS) + 1
    diagonal = (
        lax.broadcasted_iota(jnp.int32, (8 * count_f, wide), 1) % 8
        == lax.broadcasted_iota(jnp.int32, (8 * count_f, wide), 0) % 8
    )

    def matrix(vectors):
        blocks = [jnp.broadcast_to(vectors[n][k : k + 1, :], (8, 128)) for n, k in FIELDS]
        blocks.append(jnp.zeros((8, 128), jnp.float32))
        hi, lo = split(jnp.concatenate(blocks, axis=0))
        zero = jnp.zeros((8 * count_f, wide), jnp.float32)
        hi = jnp.where(diagonal, dot(hi, spread), zero).astype(jnp.bfloat16)
        lo = jnp.where(diagonal, dot(lo, spread), zero).astype(jnp.bfloat16)
        return jnp.concatenate([hi, lo], axis=0)

    w_eta[...] = matrix(us)
    w_flow[...] = matrix(vs)

    list_sensors(rows, cells_v, count_s, hot_early, places_early, hot_late, places_late)
    for copy in copies[-2:]:
        copy.wait()


def contract_kernel(eta, flow, w_eta, w_flow, cel, own, partner, fields, inner, outer, *relays):
    levels, rows, across = eta.shape[1:]
    wide = w_eta.shape[1]
    half = w_eta.shape[0] // 2
    for h in range(rows // 8):
        hi, lo = split(eta[0, :, 8 * h : 8 * h + 8, :].reshape(wide, across))
        total = dot(w_eta[...], hi)
        part = dot(w_eta[0:half, :], lo)
        hi, lo = split(flow[0, :, 8 * h : 8 * h + 8, :].reshape(wide, across))
        total += dot(w_flow[...], hi)
        part += dot(w_flow[0:half, :], lo)
        part = part + total[:half] + total[half:]
        for f in range(len(FIELDS)):
            fields[f, 8 * h : 8 * h + 8, :] = part[8 * f : 8 * f + 8]

    me = lax.axis_index("trench")
    tiles = own.shape[0]
    for d, out in enumerate((outer, *relays), 1):
        out[0:STEPS, :] = widen([both_rows(met(me, d, tiles), own, partner)], out.shape[1])

    def edge(out, at, last):
        for f, width in enumerate(HALO):
            start = rows - width if last else 0
            out[at + HALO_AT[f] : at + HALO_AT[f] + width, :] = fields[f, start : start + width, :]
        start = rows - CEL_HALO if last else 0
        out[at + CEL_AT : at + CEL_AT + CEL_HALO, :] = cel[start : start + CEL_HALO, :]

    @pl.when(me % 2 == 0)
    def _():
        edge(inner, 0, True)
        edge(outer, STEPS, False)

    @pl.when(me % 2 == 1)
    def _():
        edge(inner, 0, False)
        edge(outer, STEPS, True)


def met(me, d, tiles):
    odd = me % 2
    chip = (me // 2 + jnp.where(odd == 1, d, tiles // 2 - d)) % (tiles // 2)
    return jnp.where(d == 0, me, 2 * chip + 1 - odd)


def sources(me, tiles):
    def at(distances):
        return [met(me, d, tiles) ^ core for d in distances for core in range(2)]

    half = tiles // 4
    return at(d for d in range(tiles // 2) if d not in (half, 1)), at((half, 1))


def widen(values, lanes):
    fill = lanes - sum(value.shape[1] for value in values)
    if fill:
        values = values + [jnp.zeros((STEPS, fill), jnp.float32)]
    return jnp.concatenate(values, axis=1)


def residual_rows(owner, own):
    tiles = own.shape[0]
    return jnp.concatenate([own[jnp.clip(owner + d - 1, 0, tiles - 1)] for d in range(3)], axis=1)


def both_rows(owner, own, partner):
    return jnp.concatenate([residual_rows(owner, own), residual_rows(owner, partner)], axis=1)


def list_sensors(rows, cells, count, hot_early, places_early, hot_late, places_late):
    me = lax.axis_index("trench")
    tiles, _, slots = cells.shape
    across = hot_early.shape[0]
    slot = lax.broadcasted_iota(jnp.int32, (1, slots), 1)
    bits = across.bit_length() - 1

    def list_slots(listed_sources, hot, places):
        listed = []
        for source in listed_sources:
            for d in range(3):
                owner = me + d - 1
                inside = (owner >= 0) & (owner < tiles)
                owner = jnp.clip(owner, 0, tiles - 1)
                live = jnp.where(inside, count[source, owner], 0)
                listed.append(jnp.where(slot < live, cells[source, pl.ds(owner, 1), :], -1))
        listed = jnp.concatenate(listed, axis=1)
        tile = (lax.broadcasted_iota(jnp.int32, listed.shape, 1) // slots) % 3
        at = jnp.where(listed < 0, -1, (listed >> bits) + (rows * (tile - 1) + PAD))
        places[...] = jnp.broadcast_to(at, places.shape)
        columns = listed & (across - 1)
        hot[...] = jnp.where(lax.broadcasted_iota(jnp.int32, hot.shape, 0) == columns, 1.0, 0.0).astype(jnp.bfloat16)

    early, late = sources(me, tiles)
    list_slots(early, hot_early, places_early)
    list_slots(late, hot_late, places_late)


def planes_of(values, hot, places, tall):
    here = lax.broadcasted_iota(jnp.int32, (tall, values.shape[1]), 0) == places[0:1, :]
    left = jnp.concatenate([jnp.where(here, values[t : t + 1, :], 0.0) for t in range(STEPS)], axis=0)
    both = dot(jnp.concatenate(split(left), axis=0), hot[...], ((1,), (1,)))
    return both[: STEPS * tall] + both[STEPS * tall :]


def inject_kernel(hot, places, own, partner, *refs):
    gots, planes = refs[:-1], refs[-1]
    per = 6 * own.shape[2]
    values = [both_rows(lax.axis_index("trench"), own, partner)] + [got[0:STEPS, 0:per] for got in gots]
    planes[...] = planes_of(jnp.concatenate(values, axis=1), hot, places, planes.shape[0] // STEPS)


def advance_kernel(tiles, fields, cel, coef, hot, places, facing_in, facing_out, last, planes, *refs):
    outs, (stage, ext, cel_ext) = refs[:-3], refs[-3:]
    blocks = len(outs)
    me = lax.axis_index("trench")
    rows, across = cel.shape
    tall = rows + 2 * PAD
    part = rows // blocks
    odd = me % 2 == 1
    facing = me // 2 + jnp.where(odd, 1, -1)
    inner = facing_in[...]
    outer = jnp.where((facing >= 0) & (facing < tiles // 2), facing_out[STEPS:, :], 0.0)
    before = jnp.where(odd, inner, outer)
    after = jnp.where(odd, outer, inner)

    per = hot.shape[1] // 2
    values = jnp.concatenate([last[:, 0:per], facing_out[0:STEPS, 0:per]], axis=1)
    all_planes = planes[...] + planes_of(values, hot, places, tall)
    inject = [all_planes[tall * t : tall * t + tall] for t in range(STEPS)]

    def extend(store, own, at, width):
        store(0, PAD, jnp.zeros((PAD, across), jnp.float32))
        store(PAD + rows, tall, jnp.zeros((PAD, across), jnp.float32))
        store(PAD, PAD + rows, own)
        store(PAD - width, PAD, before[at : at + width])
        store(PAD + rows, PAD + rows + width, after[at : at + width])

    for f, width in enumerate(HALO):
        def store(a, b, value, f=f):
            ext[f, a:b, :] = value
        extend(store, fields[f], HALO_AT[f], width)

    def store_cel(a, b, value):
        cel_ext[a:b, :] = value
    extend(store_cel, cel[...], CEL_AT, CEL_HALO)

    lane = lax.broadcasted_iota(jnp.int32, (tall, across), 1)
    first = lane == 0
    last = lane == across - 1
    speed = cel_ext[...]

    def horizontal(z):
        around = pltpu.roll(z, 1, 0) + pltpu.roll(z, tall - 1, 0)
        around += jnp.where(first, 0.0, pltpu.roll(z, 1, 1))
        around += jnp.where(last, 0.0, pltpu.roll(z, across - 1, 1))
        return speed * (around - 4.0 * z) + SHIFT * z

    def injected(n, k, a, b):
        total = None
        for tau in range(1, n - k + 1):
            r = n - tau
            term = coef[8 * r + k : 8 * r + k + 1, :] * inject[STEPS - tau][a:b]
            total = term if total is None else total + term
        return total

    base = horizontal(ext[0])
    for n in range(1, STEPS + 1):
        z = base
        for k in range(n - 1, 0, -1):
            z = horizontal(z + ext[FIELDS.index((n, k))] + injected(n, k, 0, tall))
        own = z[PAD : PAD + rows] + fields[FIELDS.index((n, 0))] + injected(n, 0, PAD, PAD + rows)
        t = STEPS - n
        for b in range(blocks):
            stage[b, part * t : part * t + part, :] = own[part * b : part * b + part]
    block = lax.axis_index("tblock")
    for r, out in enumerate(outs):
        out[...] = stage[block ^ r]


def prior_kernel(*refs):
    gots, (weight, out, whole, done, sems) = refs[:-5], refs[-5:]
    block = lax.axis_index("tblock")
    for r, got in enumerate(reversed(gots)):
        whole[block ^ r] = got[...]
    part = out.shape[1]
    length = out.shape[0]
    width = weight.shape[0]
    factor = [weight[j : j + 1, :] for j in range(width)]
    copies = []

    def finish(p):
        if (p + 1) % (length // 4) == 0:
            cut = pl.ds(p + 1 - length // 4, length // 4)
            copies.append(pltpu.make_async_copy(done.at[cut], out.at[cut], sems.at[len(copies)]))
            copies[-1].start()

    if 2 * part != 8:
        series = [whole[i // STEPS, part * (i % STEPS) : part * (i % STEPS) + part, :] for i in range(length)]
        for k in range(length):
            done[k] = sum(factor[j] * series[k + j] for j in range(min(width, length - k)))
            finish(k)
        for copy in copies:
            copy.wait()
        return
    pairs = length // 2
    even = [whole[p // 2, 8 * (p % 2) : 8 * (p % 2) + 8, :] for p in range(pairs)]
    half = lax.broadcasted_iota(jnp.int32, even[0].shape, 0) < part
    turned = [pltpu.roll(x, part, 0) for x in even] + [jnp.zeros(even[0].shape, jnp.float32)]
    odd = [jnp.where(half, turned[p], turned[p + 1]) for p in range(pairs)]
    for p in range(pairs):
        total = None
        for j in range(width):
            if p + j // 2 < pairs:
                term = factor[j] * (odd if j % 2 else even)[p + j // 2]
                total = term if total is None else total + term
        done[2 * p] = total[:part]
        done[2 * p + 1] = total[part:]
        finish(2 * p + 1)
    for copy in copies:
        copy.wait()


def shape(*dims, dtype=jnp.float32):
    return jax.ShapeDtypeStruct(dims, dtype)


def spec(space):
    return pl.BlockSpec(memory_space=space)


def body(
    adjoint_eta,
    adjoint_flow,
    residual,
    sensor_cell,
    sensor_count,
    depth_class,
    speed_table,
    damping,
    profile,
    band_weight,
):
    tiles = lax.axis_size("trench")
    blocks = lax.axis_size("tblock")
    levels, rows, across = adjoint_eta.shape[1:]
    tall = rows + 2 * PAD
    params = pltpu.CompilerParams(vmem_limit_bytes=LIMIT)

    def swaps(parts, axis):
        devices = lax.axis_size(axis)
        moved = {r: lax.ppermute(parts[r], axis, [(i, i ^ r) for i in range(devices)]) for r in range(devices - 1, 0, -1)}
        return [parts[0]] + [moved[r] for r in range(1, devices)]

    own = residual[0, 0]
    slots = own.shape[2]
    chips = tiles // 2

    def meet(x, d):
        pairs = [(2 * c + 1, 2 * ((c + d) % chips)) for c in range(chips)]
        return lax.ppermute(x, "trench", pairs + [(j, i) for i, j in pairs])

    partner = meet(own, 0)
    def slot_shapes(count):
        return shape(across, 3 * slots * count, dtype=jnp.bfloat16), shape(8, 3 * slots * count, dtype=jnp.int32)

    matrix = shape(16 * (len(FIELDS) + 1), 8 * levels, dtype=jnp.bfloat16)
    w_eta, w_flow, cel, coef, factor, hot, places, hot_late, places_late, own, eta, flow = pl.pallas_call(
        prepare_kernel,
        out_shape=(
            matrix,
            matrix,
            shape(rows, across),
            shape(8 * STEPS, across),
            shape(band_weight.shape[0], across),
            *slot_shapes(tiles - 4),
            *slot_shapes(4),
            shape(*own.shape),
            shape(*adjoint_eta.shape),
            shape(*adjoint_flow.shape),
        ),
        in_specs=[spec(pltpu.HBM)] * 10,
        out_specs=(spec(VMEM),) * 12,
        scratch_shapes=[
            VMEM((rows, across), jnp.int32),
            SMEM(speed_table.shape, jnp.float32),
            VMEM((1, levels), jnp.float32),
            VMEM((1, levels), jnp.float32),
            VMEM((1, band_weight.shape[0]), jnp.float32),
            VMEM(sensor_cell.shape, jnp.int32),
            SMEM(sensor_count.shape, jnp.int32),
            pltpu.SemaphoreType.DMA((10,)),
        ],
        compiler_params=params,
        cost_estimate=pl.CostEstimate(flops=10**7, bytes_accessed=4 * 10**6, transcendentals=0),
        name="prepare",
    )(
        *[
            pltpu.with_memory_space_constraint(x, pltpu.HBM)
            for x in (
                depth_class, speed_table, damping[None], profile[None], band_weight[None],
                sensor_cell, sensor_count, own, adjoint_eta, adjoint_flow,
            )
        ]
    )
    fields, inner, outer, *relays = pl.pallas_call(
        contract_kernel,
        out_shape=(
            shape(len(FIELDS), rows, across),
            shape(ROWS, across),
            shape(STEPS + ROWS, across),
        ) + (shape(STEPS, 6 * slots),) * (chips - 2),
        in_specs=[spec(VMEM)] * 7,
        out_specs=(spec(VMEM),) * (1 + chips),
        compiler_params=params,
        cost_estimate=pl.CostEstimate(flops=10**9, bytes_accessed=4 * 10**6, transcendentals=0),
        name="contract",
    )(eta, flow, w_eta, w_flow, cel, own, partner)
    facing_out = meet(outer, 1)
    gots = {d: meet(relay, d) for d, relay in enumerate(relays, 2)}
    last = gots.pop(chips // 2)
    gots = list(gots.values())
    facing_in = meet(inner, 0)

    planes = pl.pallas_call(
        inject_kernel,
        out_shape=shape(STEPS * (rows + 2 * PAD), across),
        in_specs=[spec(VMEM)] * (4 + len(gots)),
        out_specs=spec(VMEM),
        compiler_params=params,
        cost_estimate=pl.CostEstimate(flops=1000, bytes_accessed=1000, transcendentals=0),
        name="inject",
    )(hot, places, own, partner, *gots)
    series = pl.pallas_call(
        functools.partial(advance_kernel, tiles),
        out_shape=(shape(STEPS * rows // blocks, across),) * blocks,
        in_specs=[spec(VMEM)] * 9,
        out_specs=(spec(VMEM),) * blocks,
        scratch_shapes=[
            VMEM((blocks, STEPS * rows // blocks, across), jnp.float32),
            VMEM((len(HALO), tall, across), jnp.float32),
            VMEM((tall, across), jnp.float32),
        ],
        compiler_params=params,
        name="advance",
    )(fields, cel, coef, hot_late, places_late, facing_in, facing_out, last, planes)
    gots = swaps(series, "tblock")
    return pl.pallas_call(
        prior_kernel,
        out_shape=shape(STEPS * blocks, rows // blocks, across),
        in_specs=[spec(VMEM)] * (blocks + 1),
        out_specs=spec(pl.ANY),
        scratch_shapes=[
            VMEM((blocks, STEPS * rows // blocks, across), jnp.float32),
            VMEM((STEPS * blocks, rows // blocks, across), jnp.float32),
            pltpu.SemaphoreType.DMA((4,)),
        ],
        compiler_params=params,
        name="prior",
    )(*reversed(gots), factor)


def solution(mesh):
    in_specs = (
        P("tblock", None, "trench", None),
        P("tblock", None, "trench", None),
        P("tblock", "trench", None, None, None),
        P(),
        P(),
        P("trench", None),
        P(),
        P(),
        P(),
        P(),
    )
    out_specs = P(None, ("trench", "tblock"), None)
    return jax.shard_map(body, mesh=mesh, in_specs=in_specs, out_specs=out_specs, check_vma=False)
```

```python
import functools
import math

import jax
import jax.numpy as jnp
from jax import lax
from jax.experimental import pallas as pl
from jax.experimental.pallas import tpu as pltpu
from jax.sharding import PartitionSpec as P

VERT = 0.2
STEPS = 4
PAD = 8
VMEM = pltpu.VMEM
SMEM = pltpu.SMEM
LIMIT = 32 * 1024 * 1024

SHIFT = 1.2

FIELDS = [(4, 4), (4, 3), (4, 2), (3, 2), (4, 1), (3, 1), (2, 1), (4, 0), (3, 0), (2, 0), (1, 0)]
HALO = [4, 3, 2, 2, 1, 1, 1]
HALO_AT = [0, 4, 7, 9, 11, 12, 13]
CEL_AT = 14
CEL_HALO = 3
ROWS = 17


def split(x):
    hi = x.astype(jnp.bfloat16)
    return hi, (x - hi.astype(jnp.float32)).astype(jnp.bfloat16)


def dot(a, b, dims=((1,), (0,))):
    return lax.dot_general(a, b, (dims, ((), ())), preferred_element_type=jnp.float32)


def prepare_kernel(
    depth, table, damping, profile, band, cells, count, residual, eta, flow,
    w_eta, w_flow, cel, coef, factor, hot_early, places_early, hot_late, places_late, own, eta_v, flow_v,
    depth_v, table_s, damping_v, profile_v, band_v, cells_v, count_s, sems,
):
    rows, across = cel.shape
    levels = damping.shape[1]
    copies = [
        pltpu.make_async_copy(src, dst, sems.at[i])
        for i, (src, dst) in enumerate((
            (damping, damping_v), (profile, profile_v), (table, table_s), (depth, depth_v),
            (band, band_v), (cells, cells_v), (count, count_s), (residual, own), (eta, eta_v), (flow, flow_v),
        ))
    ]
    for copy in copies:
        copy.start()
    for copy in copies[:-2]:
        copy.wait()

    classes = depth_v[...]
    speed = jnp.zeros(classes.shape, jnp.float32)
    for c in range(table_s.shape[0]):
        speed = jnp.where(classes == c, table_s[c], speed)
    cel[...] = speed
    for j in range(factor.shape[0]):
        factor[j : j + 1, :] = jnp.broadcast_to(band_v[:, j : j + 1], (1, across))

    lane = lax.broadcasted_iota(jnp.int32, (8, 128), 1)
    sub = lax.broadcasted_iota(jnp.int32, (8, 128), 0)
    inside = lane < levels
    fill = jnp.zeros((1, 128 - levels), jnp.float32)
    keep = jnp.broadcast_to(jnp.concatenate([damping_v[...], fill], axis=1), (8, 128))
    weight = jnp.broadcast_to(jnp.concatenate([profile_v[...], fill], axis=1), (8, 128))
    u = jnp.zeros((8, 128), jnp.float32)
    v = jnp.where(sub == 0, weight * (1.0 / math.sqrt(levels)), 0.0)
    us, vs = [u], [v]
    for r in range(STEPS):
        s = u + v
        bottom = jnp.sum(jnp.where(lane == levels - 1, s, 0.0), axis=1, keepdims=True)
        coef[8 * r : 8 * r + 8, :] = jnp.broadcast_to(bottom, (8, coef.shape[1]))
        vertical = pltpu.roll(s, 1, 1) + pltpu.roll(s, 127, 1) - 2.0 * s
        u = jnp.where(inside, u + VERT * vertical - SHIFT * s + pltpu.roll(s, 1, 0), 0.0)
        v = s * keep
        us.append(u)
        vs.append(v)

    wide = w_eta.shape[1]
    spread = (
        lax.broadcasted_iota(jnp.int32, (128, wide), 1) // 8
        == lax.broadcasted_iota(jnp.int32, (128, wide), 0)
    ).astype(jnp.bfloat16)
    count_f = len(FIELDS) + 1
    diagonal = (
        lax.broadcasted_iota(jnp.int32, (8 * count_f, wide), 1) % 8
        == lax.broadcasted_iota(jnp.int32, (8 * count_f, wide), 0) % 8
    )

    def matrix(vectors):
        blocks = [jnp.broadcast_to(vectors[n][k : k + 1, :], (8, 128)) for n, k in FIELDS]
        blocks.append(jnp.zeros((8, 128), jnp.float32))
        hi, lo = split(jnp.concatenate(blocks, axis=0))
        zero = jnp.zeros((8 * count_f, wide), jnp.float32)
        hi = jnp.where(diagonal, dot(hi, spread), zero).astype(jnp.bfloat16)
        lo = jnp.where(diagonal, dot(lo, spread), zero).astype(jnp.bfloat16)
        return jnp.concatenate([hi, lo], axis=0)

    w_eta[...] = matrix(us)
    w_flow[...] = matrix(vs)

    list_sensors(rows, cells_v, count_s, hot_early, places_early, hot_late, places_late)
    for copy in copies[-2:]:
        copy.wait()


def contract_kernel(eta, flow, w_eta, w_flow, cel, own, partner, fields, inner, outer, *relays):
    levels, rows, across = eta.shape[1:]
    wide = w_eta.shape[1]
    half = w_eta.shape[0] // 2
    for h in range(rows // 8):
        hi, lo = split(eta[0, :, 8 * h : 8 * h + 8, :].reshape(wide, across))
        total = dot(w_eta[...], hi)
        part = dot(w_eta[0:half, :], lo)
        hi, lo = split(flow[0, :, 8 * h : 8 * h + 8, :].reshape(wide, across))
        total += dot(w_flow[...], hi)
        part += dot(w_flow[0:half, :], lo)
        part = part + total[:half] + total[half:]
        for f in range(len(FIELDS)):
            fields[f, 8 * h : 8 * h + 8, :] = part[8 * f : 8 * f + 8]

    me = lax.axis_index("trench")
    tiles = own.shape[0]
    for d, out in enumerate((outer, *relays), 1):
        out[0:STEPS, :] = widen([both_rows(met(me, d, tiles), own, partner)], out.shape[1])

    def edge(out, at, last):
        for f, width in enumerate(HALO):
            start = rows - width if last else 0
            out[at + HALO_AT[f] : at + HALO_AT[f] + width, :] = fields[f, start : start + width, :]
        start = rows - CEL_HALO if last else 0
        out[at + CEL_AT : at + CEL_AT + CEL_HALO, :] = cel[start : start + CEL_HALO, :]

    @pl.when(me % 2 == 0)
    def _():
        edge(inner, 0, True)
        edge(outer, STEPS, False)

    @pl.when(me % 2 == 1)
    def _():
        edge(inner, 0, False)
        edge(outer, STEPS, True)


def met(me, d, tiles):
    odd = me % 2
    chip = (me // 2 + jnp.where(odd == 1, d, tiles // 2 - d)) % (tiles // 2)
    return jnp.where(d == 0, me, 2 * chip + 1 - odd)


def sources(me, tiles):
    def at(distances):
        return [met(me, d, tiles) ^ core for d in distances for core in range(2)]

    last = tiles // 2 - 1
    return at(d for d in range(last) if d != 1), at((last, 1))


def widen(values, lanes):
    fill = lanes - sum(value.shape[1] for value in values)
    if fill:
        values = values + [jnp.zeros((STEPS, fill), jnp.float32)]
    return jnp.concatenate(values, axis=1)


def residual_rows(owner, own):
    tiles = own.shape[0]
    return jnp.concatenate([own[jnp.clip(owner + d - 1, 0, tiles - 1)] for d in range(3)], axis=1)


def both_rows(owner, own, partner):
    return jnp.concatenate([residual_rows(owner, own), residual_rows(owner, partner)], axis=1)


def list_sensors(rows, cells, count, hot_early, places_early, hot_late, places_late):
    me = lax.axis_index("trench")
    tiles, _, slots = cells.shape
    across = hot_early.shape[0]
    slot = lax.broadcasted_iota(jnp.int32, (1, slots), 1)
    bits = across.bit_length() - 1

    def list_slots(listed_sources, hot, places):
        listed = []
        for source in listed_sources:
            for d in range(3):
                owner = me + d - 1
                inside = (owner >= 0) & (owner < tiles)
                owner = jnp.clip(owner, 0, tiles - 1)
                live = jnp.where(inside, count[source, owner], 0)
                listed.append(jnp.where(slot < live, cells[source, pl.ds(owner, 1), :], -1))
        listed = jnp.concatenate(listed, axis=1)
        tile = (lax.broadcasted_iota(jnp.int32, listed.shape, 1) // slots) % 3
        at = jnp.where(listed < 0, -1, (listed >> bits) + (rows * (tile - 1) + PAD))
        places[...] = jnp.broadcast_to(at, places.shape)
        columns = listed & (across - 1)
        hot[...] = jnp.where(lax.broadcasted_iota(jnp.int32, hot.shape, 0) == columns, 1.0, 0.0).astype(jnp.bfloat16)

    early, late = sources(me, tiles)
    list_slots(early, hot_early, places_early)
    list_slots(late, hot_late, places_late)


def planes_of(values, hot, places, tall):
    here = lax.broadcasted_iota(jnp.int32, (tall, values.shape[1]), 0) == places[0:1, :]
    left = jnp.concatenate([jnp.where(here, values[t : t + 1, :], 0.0) for t in range(STEPS)], axis=0)
    both = dot(jnp.concatenate(split(left), axis=0), hot[...], ((1,), (1,)))
    return both[: STEPS * tall] + both[STEPS * tall :]


def inject_kernel(hot, places, own, partner, *refs):
    gots, planes = refs[:-1], refs[-1]
    per = 6 * own.shape[2]
    values = [both_rows(lax.axis_index("trench"), own, partner)] + [got[0:STEPS, 0:per] for got in gots]
    planes[...] = planes_of(jnp.concatenate(values, axis=1), hot, places, planes.shape[0] // STEPS)


def advance_kernel(tiles, fields, cel, coef, hot, places, facing_in, facing_out, last, planes, *refs):
    outs, (stage, ext, cel_ext) = refs[:-3], refs[-3:]
    blocks = len(outs)
    me = lax.axis_index("trench")
    rows, across = cel.shape
    tall = rows + 2 * PAD
    part = rows // blocks
    odd = me % 2 == 1
    facing = me // 2 + jnp.where(odd, 1, -1)
    inner = facing_in[...]
    outer = jnp.where((facing >= 0) & (facing < tiles // 2), facing_out[STEPS:, :], 0.0)
    before = jnp.where(odd, inner, outer)
    after = jnp.where(odd, outer, inner)

    per = hot.shape[1] // 2
    values = jnp.concatenate([last[:, 0:per], facing_out[0:STEPS, 0:per]], axis=1)
    all_planes = planes[...] + planes_of(values, hot, places, tall)
    inject = [all_planes[tall * t : tall * t + tall] for t in range(STEPS)]

    def extend(store, own, at, width):
        store(0, PAD, jnp.zeros((PAD, across), jnp.float32))
        store(PAD + rows, tall, jnp.zeros((PAD, across), jnp.float32))
        store(PAD, PAD + rows, own)
        store(PAD - width, PAD, before[at : at + width])
        store(PAD + rows, PAD + rows + width, after[at : at + width])

    for f, width in enumerate(HALO):
        def store(a, b, value, f=f):
            ext[f, a:b, :] = value
        extend(store, fields[f], HALO_AT[f], width)

    def store_cel(a, b, value):
        cel_ext[a:b, :] = value
    extend(store_cel, cel[...], CEL_AT, CEL_HALO)

    lane = lax.broadcasted_iota(jnp.int32, (tall, across), 1)
    first = lane == 0
    last = lane == across - 1
    speed = cel_ext[...]

    def horizontal(z):
        around = pltpu.roll(z, 1, 0) + pltpu.roll(z, tall - 1, 0)
        around += jnp.where(first, 0.0, pltpu.roll(z, 1, 1))
        around += jnp.where(last, 0.0, pltpu.roll(z, across - 1, 1))
        return speed * (around - 4.0 * z) + SHIFT * z

    def injected(n, k, a, b):
        total = None
        for tau in range(1, n - k + 1):
            r = n - tau
            term = coef[8 * r + k : 8 * r + k + 1, :] * inject[STEPS - tau][a:b]
            total = term if total is None else total + term
        return total

    base = horizontal(ext[0])
    for n in range(1, STEPS + 1):
        z = base
        for k in range(n - 1, 0, -1):
            z = horizontal(z + ext[FIELDS.index((n, k))] + injected(n, k, 0, tall))
        own = z[PAD : PAD + rows] + fields[FIELDS.index((n, 0))] + injected(n, 0, PAD, PAD + rows)
        t = STEPS - n
        for b in range(blocks):
            stage[b, part * t : part * t + part, :] = own[part * b : part * b + part]
    block = lax.axis_index("tblock")
    for r, out in enumerate(outs):
        out[...] = stage[block ^ r]


def prior_kernel(*refs):
    gots, (weight, out, whole, done, sems) = refs[:-5], refs[-5:]
    block = lax.axis_index("tblock")
    for r, got in enumerate(reversed(gots)):
        whole[block ^ r] = got[...]
    part = out.shape[1]
    length = out.shape[0]
    width = weight.shape[0]
    factor = [weight[j : j + 1, :] for j in range(width)]
    copies = []

    def finish(p):
        if (p + 1) % (length // 4) == 0:
            cut = pl.ds(p + 1 - length // 4, length // 4)
            copies.append(pltpu.make_async_copy(done.at[cut], out.at[cut], sems.at[len(copies)]))
            copies[-1].start()

    if 2 * part != 8:
        series = [whole[i // STEPS, part * (i % STEPS) : part * (i % STEPS) + part, :] for i in range(length)]
        for k in range(length):
            done[k] = sum(factor[j] * series[k + j] for j in range(min(width, length - k)))
            finish(k)
        for copy in copies:
            copy.wait()
        return
    pairs = length // 2
    even = [whole[p // 2, 8 * (p % 2) : 8 * (p % 2) + 8, :] for p in range(pairs)]
    half = lax.broadcasted_iota(jnp.int32, even[0].shape, 0) < part
    turned = [pltpu.roll(x, part, 0) for x in even] + [jnp.zeros(even[0].shape, jnp.float32)]
    odd = [jnp.where(half, turned[p], turned[p + 1]) for p in range(pairs)]
    for p in range(pairs):
        total = None
        for j in range(width):
            if p + j // 2 < pairs:
                term = factor[j] * (odd if j % 2 else even)[p + j // 2]
                total = term if total is None else total + term
        done[2 * p] = total[:part]
        done[2 * p + 1] = total[part:]
        finish(2 * p + 1)
    for copy in copies:
        copy.wait()


def shape(*dims, dtype=jnp.float32):
    return jax.ShapeDtypeStruct(dims, dtype)


def spec(space):
    return pl.BlockSpec(memory_space=space)


def body(
    adjoint_eta,
    adjoint_flow,
    residual,
    sensor_cell,
    sensor_count,
    depth_class,
    speed_table,
    damping,
    profile,
    band_weight,
):
    tiles = lax.axis_size("trench")
    blocks = lax.axis_size("tblock")
    levels, rows, across = adjoint_eta.shape[1:]
    tall = rows + 2 * PAD
    params = pltpu.CompilerParams(vmem_limit_bytes=LIMIT)

    def swaps(parts, axis):
        devices = lax.axis_size(axis)
        moved = {r: lax.ppermute(parts[r], axis, [(i, i ^ r) for i in range(devices)]) for r in range(devices - 1, 0, -1)}
        return [parts[0]] + [moved[r] for r in range(1, devices)]

    own = residual[0, 0]
    slots = own.shape[2]
    chips = tiles // 2

    def meet(x, d):
        pairs = [(2 * c + 1, 2 * ((c + d) % chips)) for c in range(chips)]
        return lax.ppermute(x, "trench", pairs + [(j, i) for i, j in pairs])

    partner = meet(own, 0)
    def slot_shapes(count):
        return shape(across, 3 * slots * count, dtype=jnp.bfloat16), shape(8, 3 * slots * count, dtype=jnp.int32)

    matrix = shape(16 * (len(FIELDS) + 1), 8 * levels, dtype=jnp.bfloat16)
    w_eta, w_flow, cel, coef, factor, hot, places, hot_late, places_late, own, eta, flow = pl.pallas_call(
        prepare_kernel,
        out_shape=(
            matrix,
            matrix,
            shape(rows, across),
            shape(8 * STEPS, across),
            shape(band_weight.shape[0], across),
            *slot_shapes(tiles - 4),
            *slot_shapes(4),
            shape(*own.shape),
            shape(*adjoint_eta.shape),
            shape(*adjoint_flow.shape),
        ),
        in_specs=[spec(pltpu.HBM)] * 10,
        out_specs=(spec(VMEM),) * 12,
        scratch_shapes=[
            VMEM((rows, across), jnp.int32),
            SMEM(speed_table.shape, jnp.float32),
            VMEM((1, levels), jnp.float32),
            VMEM((1, levels), jnp.float32),
            VMEM((1, band_weight.shape[0]), jnp.float32),
            VMEM(sensor_cell.shape, jnp.int32),
            SMEM(sensor_count.shape, jnp.int32),
            pltpu.SemaphoreType.DMA((10,)),
        ],
        compiler_params=params,
        cost_estimate=pl.CostEstimate(flops=10**7, bytes_accessed=4 * 10**6, transcendentals=0),
        name="prepare",
    )(
        *[
            pltpu.with_memory_space_constraint(x, pltpu.HBM)
            for x in (
                depth_class, speed_table, damping[None], profile[None], band_weight[None],
                sensor_cell, sensor_count, own, adjoint_eta, adjoint_flow,
            )
        ]
    )
    fields, inner, outer, *relays = pl.pallas_call(
        contract_kernel,
        out_shape=(
            shape(len(FIELDS), rows, across),
            shape(ROWS, across),
            shape(STEPS + ROWS, across),
        ) + (shape(STEPS, 6 * slots),) * (chips - 2),
        in_specs=[spec(VMEM)] * 7,
        out_specs=(spec(VMEM),) * (1 + chips),
        compiler_params=params,
        cost_estimate=pl.CostEstimate(flops=10**9, bytes_accessed=4 * 10**6, transcendentals=0),
        name="contract",
    )(eta, flow, w_eta, w_flow, cel, own, partner)
    facing_out = meet(outer, 1)
    *gots, last = [meet(relay, d) for d, relay in enumerate(relays, 2)]
    facing_in = meet(inner, 0)

    planes = pl.pallas_call(
        inject_kernel,
        out_shape=shape(STEPS * (rows + 2 * PAD), across),
        in_specs=[spec(VMEM)] * (4 + len(gots)),
        out_specs=spec(VMEM),
        compiler_params=params,
        cost_estimate=pl.CostEstimate(flops=1000, bytes_accessed=1000, transcendentals=0),
        name="inject",
    )(hot, places, own, partner, *gots)
    series = pl.pallas_call(
        functools.partial(advance_kernel, tiles),
        out_shape=(shape(STEPS * rows // blocks, across),) * blocks,
        in_specs=[spec(VMEM)] * 9,
        out_specs=(spec(VMEM),) * blocks,
        scratch_shapes=[
            VMEM((blocks, STEPS * rows // blocks, across), jnp.float32),
            VMEM((len(HALO), tall, across), jnp.float32),
            VMEM((tall, across), jnp.float32),
        ],
        compiler_params=params,
        name="advance",
    )(fields, cel, coef, hot_late, places_late, facing_in, facing_out, last, planes)
    gots = swaps(series, "tblock")
    return pl.pallas_call(
        prior_kernel,
        out_shape=shape(STEPS * blocks, rows // blocks, across),
        in_specs=[spec(VMEM)] * (blocks + 1),
        out_specs=spec(pl.ANY),
        scratch_shapes=[
            VMEM((blocks, STEPS * rows // blocks, across), jnp.float32),
            VMEM((STEPS * blocks, rows // blocks, across), jnp.float32),
            pltpu.SemaphoreType.DMA((4,)),
        ],
        compiler_params=params,
        name="prior",
    )(*reversed(gots), factor)


def solution(mesh):
    in_specs = (
        P("tblock", None, "trench", None),
        P("tblock", None, "trench", None),
        P("tblock", "trench", None, None, None),
        P(),
        P(),
        P("trench", None),
        P(),
        P(),
        P(),
        P(),
    )
    out_specs = P(None, ("trench", "tblock"), None)
    return jax.shard_map(body, mesh=mesh, in_specs=in_specs, out_specs=out_specs, check_vma=False)
```

```python
import functools
import math

import jax
import jax.numpy as jnp
from jax import lax
from jax.experimental import pallas as pl
from jax.experimental.pallas import tpu as pltpu
from jax.sharding import PartitionSpec as P

VERT = 0.2
STEPS = 4
PAD = 8
CUTS = 5
VMEM = pltpu.VMEM
SMEM = pltpu.SMEM
LIMIT = 32 * 1024 * 1024

SHIFT = 1.2

FIELDS = [(4, 4), (4, 3), (4, 2), (3, 2), (4, 1), (3, 1), (2, 1), (4, 0), (3, 0), (2, 0), (1, 0)]
HALO = [4, 3, 2, 2, 1, 1, 1]
HALO_AT = [0, 4, 7, 9, 11, 12, 13]
CEL_AT = 14
CEL_HALO = 3
ROWS = 17


def split(x):
    hi = x.astype(jnp.bfloat16)
    return hi, (x - hi.astype(jnp.float32)).astype(jnp.bfloat16)


def dot(a, b, dims=((1,), (0,))):
    return lax.dot_general(a, b, (dims, ((), ())), preferred_element_type=jnp.float32)


def prepare_kernel(
    depth, table, damping, profile, band, residual, eta, flow,
    w_eta, w_flow, cel, coef, factor, own, eta_v, flow_v,
    depth_v, table_s, damping_v, profile_v, band_v, sems,
):
    rows, across = cel.shape
    levels = damping.shape[1]
    copies = [
        pltpu.make_async_copy(src, dst, sems.at[i])
        for i, (src, dst) in enumerate((
            (damping, damping_v), (profile, profile_v), (table, table_s), (depth, depth_v),
            (band, band_v), (residual, own),
        ))
    ]
    for copy in copies:
        copy.start()
    step = -(-eta.shape[1] // CUTS)
    large = []
    for i in range(CUTS):
        for j, (src, dst) in enumerate(((eta, eta_v), (flow, flow_v))):
            cut = pl.ds(step * i, min(step, eta.shape[1] - step * i))
            large.append(pltpu.make_async_copy(src.at[:, cut], dst.at[:, cut], sems.at[len(copies) + 2 * i + j]))
            large[-1].start()
    for copy in copies:
        copy.wait()

    classes = depth_v[...]
    speed = jnp.zeros(classes.shape, jnp.float32)
    for c in range(table_s.shape[0]):
        speed = jnp.where(classes == c, table_s[c], speed)
    cel[...] = speed
    for j in range(factor.shape[0]):
        factor[j : j + 1, :] = jnp.broadcast_to(band_v[:, j : j + 1], (1, across))

    lane = lax.broadcasted_iota(jnp.int32, (8, 128), 1)
    sub = lax.broadcasted_iota(jnp.int32, (8, 128), 0)
    inside = lane < levels
    fill = jnp.zeros((1, 128 - levels), jnp.float32)
    keep = jnp.broadcast_to(jnp.concatenate([damping_v[...], fill], axis=1), (8, 128))
    weight = jnp.broadcast_to(jnp.concatenate([profile_v[...], fill], axis=1), (8, 128))
    u = jnp.zeros((8, 128), jnp.float32)
    v = jnp.where(sub == 0, weight * (1.0 / math.sqrt(levels)), 0.0)
    us, vs = [u], [v]
    for r in range(STEPS):
        s = u + v
        bottom = jnp.sum(jnp.where(lane == levels - 1, s, 0.0), axis=1, keepdims=True)
        coef[8 * r : 8 * r + 8, :] = jnp.broadcast_to(bottom, (8, coef.shape[1]))
        vertical = pltpu.roll(s, 1, 1) + pltpu.roll(s, 127, 1) - 2.0 * s
        u = jnp.where(inside, u + VERT * vertical - SHIFT * s + pltpu.roll(s, 1, 0), 0.0)
        v = s * keep
        us.append(u)
        vs.append(v)

    wide = w_eta.shape[1]
    spread = (
        lax.broadcasted_iota(jnp.int32, (128, wide), 1) // 8
        == lax.broadcasted_iota(jnp.int32, (128, wide), 0)
    ).astype(jnp.bfloat16)
    count_f = len(FIELDS) + 1
    diagonal = (
        lax.broadcasted_iota(jnp.int32, (8 * count_f, wide), 1) % 8
        == lax.broadcasted_iota(jnp.int32, (8 * count_f, wide), 0) % 8
    )

    def matrix(vectors):
        blocks = [jnp.broadcast_to(vectors[n][k : k + 1, :], (8, 128)) for n, k in FIELDS]
        blocks.append(jnp.zeros((8, 128), jnp.float32))
        hi, lo = split(jnp.concatenate(blocks, axis=0))
        zero = jnp.zeros((8 * count_f, wide), jnp.float32)
        hi = jnp.where(diagonal, dot(hi, spread), zero).astype(jnp.bfloat16)
        lo = jnp.where(diagonal, dot(lo, spread), zero).astype(jnp.bfloat16)
        return jnp.concatenate([hi, lo], axis=0)

    w_eta[...] = matrix(us)
    w_flow[...] = matrix(vs)

    for copy in large:
        copy.wait()


def contract_kernel(eta, flow, w_eta, w_flow, cel, own, partner, fields, inner, outer, *relays):
    levels, rows, across = eta.shape[1:]
    wide = w_eta.shape[1]
    half = w_eta.shape[0] // 2
    for h in range(rows // 8):
        hi, lo = split(eta[0, :, 8 * h : 8 * h + 8, :].reshape(wide, across))
        total = dot(w_eta[...], hi)
        part = dot(w_eta[0:half, :], lo)
        hi, lo = split(flow[0, :, 8 * h : 8 * h + 8, :].reshape(wide, across))
        total += dot(w_flow[...], hi)
        part += dot(w_flow[0:half, :], lo)
        part = part + total[:half] + total[half:]
        for f in range(len(FIELDS)):
            fields[f, 8 * h : 8 * h + 8, :] = part[8 * f : 8 * f + 8]

    me = lax.axis_index("trench")
    tiles = own.shape[0]
    for d, out in enumerate((outer, *relays), 1):
        out[0:STEPS, :] = widen([both_rows(met(me, d, tiles), own, partner)], out.shape[1])

    def edge(out, at, last):
        for f, width in enumerate(HALO):
            start = rows - width if last else 0
            out[at + HALO_AT[f] : at + HALO_AT[f] + width, :] = fields[f, start : start + width, :]
        start = rows - CEL_HALO if last else 0
        out[at + CEL_AT : at + CEL_AT + CEL_HALO, :] = cel[start : start + CEL_HALO, :]

    @pl.when(me % 2 == 0)
    def _():
        edge(inner, 0, True)
        edge(outer, STEPS, False)

    @pl.when(me % 2 == 1)
    def _():
        edge(inner, 0, False)
        edge(outer, STEPS, True)


def met(me, d, tiles):
    odd = me % 2
    chip = (me // 2 + jnp.where(odd == 1, d, tiles // 2 - d)) % (tiles // 2)
    return jnp.where(d == 0, me, 2 * chip + 1 - odd)


def sources(me, tiles):
    listed = [met(me, d, tiles) ^ core for d in range(tiles // 2) for core in range(2)]
    return listed[:-2], listed[-2:]


def widen(values, lanes):
    fill = lanes - sum(value.shape[1] for value in values)
    if fill:
        values = values + [jnp.zeros((STEPS, fill), jnp.float32)]
    return jnp.concatenate(values, axis=1)


def residual_rows(owner, own):
    tiles = own.shape[0]
    return jnp.concatenate([own[jnp.clip(owner + d - 1, 0, tiles - 1)] for d in range(3)], axis=1)


def both_rows(owner, own, partner):
    return jnp.concatenate([residual_rows(owner, own), residual_rows(owner, partner)], axis=1)


def sensors_kernel(rows, cells, count, hot_early, places_early, hot_late, places_late):
    me = lax.axis_index("trench")
    tiles, _, slots = cells.shape
    across = hot_early.shape[0]
    slot = lax.broadcasted_iota(jnp.int32, (1, slots), 1)
    bits = across.bit_length() - 1

    def list_slots(listed_sources, hot, places):
        listed = []
        for source in listed_sources:
            for d in range(3):
                owner = me + d - 1
                inside = (owner >= 0) & (owner < tiles)
                owner = jnp.clip(owner, 0, tiles - 1)
                live = jnp.where(inside, count[source, owner], 0)
                listed.append(jnp.where(slot < live, cells[source, pl.ds(owner, 1), :], -1))
        listed = jnp.concatenate(listed, axis=1)
        tile = (lax.broadcasted_iota(jnp.int32, listed.shape, 1) // slots) % 3
        at = jnp.where(listed < 0, -1, (listed >> bits) + (rows * (tile - 1) + PAD))
        places[...] = jnp.broadcast_to(at, places.shape)
        columns = listed & (across - 1)
        hot[...] = jnp.where(lax.broadcasted_iota(jnp.int32, hot.shape, 0) == columns, 1.0, 0.0).astype(jnp.bfloat16)

    early, late = sources(me, tiles)
    list_slots(early, hot_early, places_early)
    list_slots(late, hot_late, places_late)


def planes_of(values, hot, places, tall):
    here = lax.broadcasted_iota(jnp.int32, (tall, values.shape[1]), 0) == places[0:1, :]
    left = jnp.concatenate([jnp.where(here, values[t : t + 1, :], 0.0) for t in range(STEPS)], axis=0)
    both = dot(jnp.concatenate(split(left), axis=0), hot[...], ((1,), (1,)))
    return both[: STEPS * tall] + both[STEPS * tall :]


def inject_kernel(hot, places, own, partner, *refs):
    gots, planes = refs[:-1], refs[-1]
    per = 6 * own.shape[2]
    values = [both_rows(lax.axis_index("trench"), own, partner)] + [got[0:STEPS, 0:per] for got in gots]
    planes[...] = planes_of(jnp.concatenate(values, axis=1), hot, places, planes.shape[0] // STEPS)


def advance_kernel(tiles, fields, cel, coef, hot, places, facing_in, facing_out, last, planes, *refs):
    outs, (stage, ext, cel_ext) = refs[:-3], refs[-3:]
    blocks = len(outs)
    me = lax.axis_index("trench")
    rows, across = cel.shape
    tall = rows + 2 * PAD
    part = rows // blocks
    odd = me % 2 == 1
    facing = me // 2 + jnp.where(odd, 1, -1)
    inner = facing_in[...]
    outer = jnp.where((facing >= 0) & (facing < tiles // 2), facing_out[STEPS:, :], 0.0)
    before = jnp.where(odd, inner, outer)
    after = jnp.where(odd, outer, inner)

    all_planes = planes[...] + planes_of(last[0:STEPS, 0 : hot.shape[1]], hot, places, tall)
    inject = [all_planes[tall * t : tall * t + tall] for t in range(STEPS)]

    def extend(store, own, at, width):
        store(0, PAD, jnp.zeros((PAD, across), jnp.float32))
        store(PAD + rows, tall, jnp.zeros((PAD, across), jnp.float32))
        store(PAD, PAD + rows, own)
        store(PAD - width, PAD, before[at : at + width])
        store(PAD + rows, PAD + rows + width, after[at : at + width])

    for f, width in enumerate(HALO):
        def store(a, b, value, f=f):
            ext[f, a:b, :] = value
        extend(store, fields[f], HALO_AT[f], width)

    def store_cel(a, b, value):
        cel_ext[a:b, :] = value
    extend(store_cel, cel[...], CEL_AT, CEL_HALO)

    lane = lax.broadcasted_iota(jnp.int32, (tall, across), 1)
    first = lane == 0
    last = lane == across - 1
    speed = cel_ext[...]

    def horizontal(z):
        around = pltpu.roll(z, 1, 0) + pltpu.roll(z, tall - 1, 0)
        around += jnp.where(first, 0.0, pltpu.roll(z, 1, 1))
        around += jnp.where(last, 0.0, pltpu.roll(z, across - 1, 1))
        return speed * (around - 4.0 * z) + SHIFT * z

    def injected(n, k, a, b):
        total = None
        for tau in range(1, n - k + 1):
            r = n - tau
            term = coef[8 * r + k : 8 * r + k + 1, :] * inject[STEPS - tau][a:b]
            total = term if total is None else total + term
        return total

    base = horizontal(ext[0])
    for n in range(1, STEPS + 1):
        z = base
        for k in range(n - 1, 0, -1):
            z = horizontal(z + ext[FIELDS.index((n, k))] + injected(n, k, 0, tall))
        own = z[PAD : PAD + rows] + fields[FIELDS.index((n, 0))] + injected(n, 0, PAD, PAD + rows)
        t = STEPS - n
        for b in range(blocks):
            stage[b, part * t : part * t + part, :] = own[part * b : part * b + part]
    block = lax.axis_index("tblock")
    for r, out in enumerate(outs):
        out[...] = stage[block ^ r]


def prior_kernel(*refs):
    gots, (weight, out, whole, done, sems) = refs[:-5], refs[-5:]
    block = lax.axis_index("tblock")
    for r, got in enumerate(reversed(gots)):
        whole[block ^ r] = got[...]
    part = out.shape[1]
    length = out.shape[0]
    width = weight.shape[0]
    factor = [weight[j : j + 1, :] for j in range(width)]
    copies = []

    def finish(p):
        if (p + 1) % (length // 4) == 0:
            cut = pl.ds(p + 1 - length // 4, length // 4)
            copies.append(pltpu.make_async_copy(done.at[cut], out.at[cut], sems.at[len(copies)]))
            copies[-1].start()

    if 2 * part != 8:
        series = [whole[i // STEPS, part * (i % STEPS) : part * (i % STEPS) + part, :] for i in range(length)]
        for k in range(length):
            done[k] = sum(factor[j] * series[k + j] for j in range(min(width, length - k)))
            finish(k)
        for copy in copies:
            copy.wait()
        return
    pairs = length // 2
    even = [whole[p // 2, 8 * (p % 2) : 8 * (p % 2) + 8, :] for p in range(pairs)]
    half = lax.broadcasted_iota(jnp.int32, even[0].shape, 0) < part
    turned = [pltpu.roll(x, part, 0) for x in even] + [jnp.zeros(even[0].shape, jnp.float32)]
    odd = [jnp.where(half, turned[p], turned[p + 1]) for p in range(pairs)]
    for p in range(pairs):
        total = None
        for j in range(width):
            if p + j // 2 < pairs:
                term = factor[j] * (odd if j % 2 else even)[p + j // 2]
                total = term if total is None else total + term
        done[2 * p] = total[:part]
        done[2 * p + 1] = total[part:]
        finish(2 * p + 1)
    for copy in copies:
        copy.wait()


def shape(*dims, dtype=jnp.float32):
    return jax.ShapeDtypeStruct(dims, dtype)


def spec(space):
    return pl.BlockSpec(memory_space=space)


def body(
    adjoint_eta,
    adjoint_flow,
    residual,
    sensor_cell,
    sensor_count,
    depth_class,
    speed_table,
    damping,
    profile,
    band_weight,
):
    tiles = lax.axis_size("trench")
    blocks = lax.axis_size("tblock")
    levels, rows, across = adjoint_eta.shape[1:]
    tall = rows + 2 * PAD
    params = pltpu.CompilerParams(vmem_limit_bytes=LIMIT)

    def swaps(parts, axis):
        devices = lax.axis_size(axis)
        moved = {r: lax.ppermute(parts[r], axis, [(i, i ^ r) for i in range(devices)]) for r in range(devices - 1, 0, -1)}
        return [parts[0]] + [moved[r] for r in range(1, devices)]

    own = residual[0, 0]
    slots = own.shape[2]
    chips = tiles // 2

    def meet(x, d):
        pairs = [(2 * c + 1, 2 * ((c + d) % chips)) for c in range(chips)]
        return lax.ppermute(x, "trench", pairs + [(j, i) for i, j in pairs])

    partner = meet(own, 0)
    matrix = shape(16 * (len(FIELDS) + 1), 8 * levels, dtype=jnp.bfloat16)
    w_eta, w_flow, cel, coef, factor, own, eta, flow = pl.pallas_call(
        prepare_kernel,
        out_shape=(
            matrix,
            matrix,
            shape(rows, across),
            shape(8 * STEPS, across),
            shape(band_weight.shape[0], across),
            shape(*own.shape),
            shape(*adjoint_eta.shape),
            shape(*adjoint_flow.shape),
        ),
        in_specs=[spec(pltpu.HBM)] * 8,
        out_specs=(spec(VMEM),) * 8,
        scratch_shapes=[
            VMEM((rows, across), jnp.int32),
            SMEM(speed_table.shape, jnp.float32),
            VMEM((1, levels), jnp.float32),
            VMEM((1, levels), jnp.float32),
            VMEM((1, band_weight.shape[0]), jnp.float32),
            pltpu.SemaphoreType.DMA((6 + 2 * CUTS,)),
        ],
        compiler_params=params,
        cost_estimate=pl.CostEstimate(flops=10**7, bytes_accessed=4 * 10**6, transcendentals=0),
        name="prepare",
    )(
        *[
            pltpu.with_memory_space_constraint(x, pltpu.HBM)
            for x in (
                depth_class, speed_table, damping[None], profile[None], band_weight[None],
                own, adjoint_eta, adjoint_flow,
            )
        ]
    )
    fields, inner, outer, *relays = pl.pallas_call(
        contract_kernel,
        out_shape=(
            shape(len(FIELDS), rows, across),
            shape(ROWS, across),
            shape(STEPS + ROWS, across),
        ) + (shape(STEPS, 6 * slots),) * (chips - 2),
        in_specs=[spec(VMEM)] * 7,
        out_specs=(spec(VMEM),) * (1 + chips),
        compiler_params=params,
        cost_estimate=pl.CostEstimate(flops=10**9, bytes_accessed=4 * 10**6, transcendentals=0),
        name="contract",
    )(eta, flow, w_eta, w_flow, cel, own, partner)
    facing_out = meet(outer, 1)
    gots = [facing_out] + [meet(relay, d) for d, relay in enumerate(relays, 2)]
    facing_in = meet(inner, 0)

    def slot_shapes(count):
        return shape(across, 3 * slots * count, dtype=jnp.bfloat16), shape(8, 3 * slots * count, dtype=jnp.int32)

    hot, places, hot_late, places_late = pl.pallas_call(
        functools.partial(sensors_kernel, rows),
        out_shape=slot_shapes(tiles - 2) + slot_shapes(2),
        in_specs=[spec(VMEM), spec(SMEM)],
        out_specs=(spec(VMEM),) * 4,
        compiler_params=params,
        cost_estimate=pl.CostEstimate(flops=10**6, bytes_accessed=2 * 10**6, transcendentals=0),
        name="sensors",
    )(sensor_cell, sensor_count)
    planes = pl.pallas_call(
        inject_kernel,
        out_shape=shape(STEPS * (rows + 2 * PAD), across),
        in_specs=[spec(VMEM)] * (3 + len(gots)),
        out_specs=spec(VMEM),
        compiler_params=params,
        cost_estimate=pl.CostEstimate(flops=1000, bytes_accessed=1000, transcendentals=0),
        name="inject",
    )(hot, places, own, partner, *gots[:-1])
    series = pl.pallas_call(
        functools.partial(advance_kernel, tiles),
        out_shape=(shape(STEPS * rows // blocks, across),) * blocks,
        in_specs=[spec(VMEM)] * 9,
        out_specs=(spec(VMEM),) * blocks,
        scratch_shapes=[
            VMEM((blocks, STEPS * rows // blocks, across), jnp.float32),
            VMEM((len(HALO), tall, across), jnp.float32),
            VMEM((tall, across), jnp.float32),
        ],
        compiler_params=params,
        name="advance",
    )(fields, cel, coef, hot_late, places_late, facing_in, facing_out, gots[-1], planes)
    gots = swaps(series, "tblock")
    return pl.pallas_call(
        prior_kernel,
        out_shape=shape(STEPS * blocks, rows // blocks, across),
        in_specs=[spec(VMEM)] * (blocks + 1),
        out_specs=spec(pl.ANY),
        scratch_shapes=[
            VMEM((blocks, STEPS * rows // blocks, across), jnp.float32),
            VMEM((STEPS * blocks, rows // blocks, across), jnp.float32),
            pltpu.SemaphoreType.DMA((4,)),
        ],
        compiler_params=params,
        name="prior",
    )(*reversed(gots), factor)


def solution(mesh):
    in_specs = (
        P("tblock", None, "trench", None),
        P("tblock", None, "trench", None),
        P("tblock", "trench", None, None, None),
        P(),
        P(),
        P("trench", None),
        P(),
        P(),
        P(),
        P(),
    )
    out_specs = P(None, ("trench", "tblock"), None)
    return jax.shard_map(body, mesh=mesh, in_specs=in_specs, out_specs=out_specs, check_vma=False)
```

```python
import functools
import math

import jax
import jax.numpy as jnp
from jax import lax
from jax.experimental import pallas as pl
from jax.experimental.pallas import tpu as pltpu
from jax.sharding import PartitionSpec as P

VERT = 0.2
STEPS = 4
PAD = 8
VMEM = pltpu.VMEM
SMEM = pltpu.SMEM
LIMIT = 32 * 1024 * 1024

SHIFT = 1.2

FIELDS = [(4, 4), (4, 3), (4, 2), (3, 2), (4, 1), (3, 1), (2, 1), (4, 0), (3, 0), (2, 0), (1, 0)]
HALO = [4, 3, 2, 2, 1, 1, 1]
HALO_AT = [0, 4, 7, 9, 11, 12, 13]
CEL_AT = 14
CEL_HALO = 3
ROWS = 17


def split(x):
    hi = x.astype(jnp.bfloat16)
    return hi, (x - hi.astype(jnp.float32)).astype(jnp.bfloat16)


def dot(a, b, dims=((1,), (0,))):
    return lax.dot_general(a, b, (dims, ((), ())), preferred_element_type=jnp.float32)


def prepare_kernel(
    depth, table, damping, profile, band, residual, eta, flow,
    w_eta, w_flow, cel, coef, factor, own, eta_v, flow_v,
    depth_v, table_s, damping_v, profile_v, band_v, sems,
):
    rows, across = cel.shape
    levels = damping.shape[1]
    copies = [
        pltpu.make_async_copy(src, dst, sems.at[i])
        for i, (src, dst) in enumerate((
            (damping, damping_v), (profile, profile_v), (table, table_s), (depth, depth_v),
            (band, band_v), (residual, own), (eta, eta_v), (flow, flow_v),
        ))
    ]
    for copy in copies[:2] + copies[-2:] + copies[2:-2]:
        copy.start()
    for copy in copies[:-2]:
        copy.wait()

    classes = depth_v[...]
    speed = jnp.zeros(classes.shape, jnp.float32)
    for c in range(table_s.shape[0]):
        speed = jnp.where(classes == c, table_s[c], speed)
    cel[...] = speed
    for j in range(factor.shape[0]):
        factor[j : j + 1, :] = jnp.broadcast_to(band_v[:, j : j + 1], (1, across))

    lane = lax.broadcasted_iota(jnp.int32, (8, 128), 1)
    sub = lax.broadcasted_iota(jnp.int32, (8, 128), 0)
    inside = lane < levels
    fill = jnp.zeros((1, 128 - levels), jnp.float32)
    keep = jnp.broadcast_to(jnp.concatenate([damping_v[...], fill], axis=1), (8, 128))
    weight = jnp.broadcast_to(jnp.concatenate([profile_v[...], fill], axis=1), (8, 128))
    u = jnp.zeros((8, 128), jnp.float32)
    v = jnp.where(sub == 0, weight * (1.0 / math.sqrt(levels)), 0.0)
    us, vs = [u], [v]
    for r in range(STEPS):
        s = u + v
        bottom = jnp.sum(jnp.where(lane == levels - 1, s, 0.0), axis=1, keepdims=True)
        coef[8 * r : 8 * r + 8, :] = jnp.broadcast_to(bottom, (8, coef.shape[1]))
        vertical = pltpu.roll(s, 1, 1) + pltpu.roll(s, 127, 1) - 2.0 * s
        u = jnp.where(inside, u + VERT * vertical - SHIFT * s + pltpu.roll(s, 1, 0), 0.0)
        v = s * keep
        us.append(u)
        vs.append(v)

    wide = w_eta.shape[1]
    spread = (
        lax.broadcasted_iota(jnp.int32, (128, wide), 1) // 8
        == lax.broadcasted_iota(jnp.int32, (128, wide), 0)
    ).astype(jnp.bfloat16)
    count_f = len(FIELDS) + 1
    diagonal = (
        lax.broadcasted_iota(jnp.int32, (8 * count_f, wide), 1) % 8
        == lax.broadcasted_iota(jnp.int32, (8 * count_f, wide), 0) % 8
    )

    def matrix(vectors):
        blocks = [jnp.broadcast_to(vectors[n][k : k + 1, :], (8, 128)) for n, k in FIELDS]
        blocks.append(jnp.zeros((8, 128), jnp.float32))
        hi, lo = split(jnp.concatenate(blocks, axis=0))
        zero = jnp.zeros((8 * count_f, wide), jnp.float32)
        hi = jnp.where(diagonal, dot(hi, spread), zero).astype(jnp.bfloat16)
        lo = jnp.where(diagonal, dot(lo, spread), zero).astype(jnp.bfloat16)
        return jnp.concatenate([hi, lo], axis=0)

    w_eta[...] = matrix(us)
    w_flow[...] = matrix(vs)

    for copy in copies[-2:]:
        copy.wait()


def contract_kernel(eta, flow, w_eta, w_flow, cel, own, partner, fields, inner, outer, *relays):
    levels, rows, across = eta.shape[1:]
    wide = w_eta.shape[1]
    half = w_eta.shape[0] // 2
    for h in range(rows // 8):
        hi, lo = split(eta[0, :, 8 * h : 8 * h + 8, :].reshape(wide, across))
        total = dot(w_eta[...], hi)
        part = dot(w_eta[0:half, :], lo)
        hi, lo = split(flow[0, :, 8 * h : 8 * h + 8, :].reshape(wide, across))
        total += dot(w_flow[...], hi)
        part += dot(w_flow[0:half, :], lo)
        part = part + total[:half] + total[half:]
        for f in range(len(FIELDS)):
            fields[f, 8 * h : 8 * h + 8, :] = part[8 * f : 8 * f + 8]

    me = lax.axis_index("trench")
    tiles = own.shape[0]
    for d, out in enumerate((outer, *relays), 1):
        out[0:STEPS, :] = widen([both_rows(met(me, d, tiles), own, partner)], out.shape[1])

    def edge(out, at, last):
        for f, width in enumerate(HALO):
            start = rows - width if last else 0
            out[at + HALO_AT[f] : at + HALO_AT[f] + width, :] = fields[f, start : start + width, :]
        start = rows - CEL_HALO if last else 0
        out[at + CEL_AT : at + CEL_AT + CEL_HALO, :] = cel[start : start + CEL_HALO, :]

    @pl.when(me % 2 == 0)
    def _():
        edge(inner, 0, True)
        edge(outer, STEPS, False)

    @pl.when(me % 2 == 1)
    def _():
        edge(inner, 0, False)
        edge(outer, STEPS, True)


def met(me, d, tiles):
    odd = me % 2
    chip = (me // 2 + jnp.where(odd == 1, d, tiles // 2 - d)) % (tiles // 2)
    return jnp.where(d == 0, me, 2 * chip + 1 - odd)


def sources(me, tiles):
    listed = [met(me, d, tiles) ^ core for d in range(tiles // 2) for core in range(2)]
    return listed[:-2], listed[-2:]


def widen(values, lanes):
    fill = lanes - sum(value.shape[1] for value in values)
    if fill:
        values = values + [jnp.zeros((STEPS, fill), jnp.float32)]
    return jnp.concatenate(values, axis=1)


def residual_rows(owner, own):
    tiles = own.shape[0]
    return jnp.concatenate([own[jnp.clip(owner + d - 1, 0, tiles - 1)] for d in range(3)], axis=1)


def both_rows(owner, own, partner):
    return jnp.concatenate([residual_rows(owner, own), residual_rows(owner, partner)], axis=1)


def sensors_kernel(rows, cells, count, hot_early, places_early, hot_late, places_late):
    me = lax.axis_index("trench")
    tiles, _, slots = cells.shape
    across = hot_early.shape[0]
    slot = lax.broadcasted_iota(jnp.int32, (1, slots), 1)
    bits = across.bit_length() - 1

    def list_slots(listed_sources, hot, places):
        listed = []
        for source in listed_sources:
            for d in range(3):
                owner = me + d - 1
                inside = (owner >= 0) & (owner < tiles)
                owner = jnp.clip(owner, 0, tiles - 1)
                live = jnp.where(inside, count[source, owner], 0)
                listed.append(jnp.where(slot < live, cells[source, pl.ds(owner, 1), :], -1))
        listed = jnp.concatenate(listed, axis=1)
        tile = (lax.broadcasted_iota(jnp.int32, listed.shape, 1) // slots) % 3
        at = jnp.where(listed < 0, -1, (listed >> bits) + (rows * (tile - 1) + PAD))
        places[...] = jnp.broadcast_to(at, places.shape)
        columns = listed & (across - 1)
        hot[...] = jnp.where(lax.broadcasted_iota(jnp.int32, hot.shape, 0) == columns, 1.0, 0.0).astype(jnp.bfloat16)

    early, late = sources(me, tiles)
    list_slots(early, hot_early, places_early)
    list_slots(late, hot_late, places_late)


def planes_of(values, hot, places, tall):
    here = lax.broadcasted_iota(jnp.int32, (tall, values.shape[1]), 0) == places[0:1, :]
    left = jnp.concatenate([jnp.where(here, values[t : t + 1, :], 0.0) for t in range(STEPS)], axis=0)
    both = dot(jnp.concatenate(split(left), axis=0), hot[...], ((1,), (1,)))
    return both[: STEPS * tall] + both[STEPS * tall :]


def inject_kernel(hot, places, own, partner, *refs):
    gots, planes = refs[:-1], refs[-1]
    per = 6 * own.shape[2]
    values = [both_rows(lax.axis_index("trench"), own, partner)] + [got[0:STEPS, 0:per] for got in gots]
    planes[...] = planes_of(jnp.concatenate(values, axis=1), hot, places, planes.shape[0] // STEPS)


def advance_kernel(tiles, fields, cel, coef, hot, places, facing_in, facing_out, last, planes, *refs):
    outs, (stage, ext, cel_ext) = refs[:-3], refs[-3:]
    blocks = len(outs)
    me = lax.axis_index("trench")
    rows, across = cel.shape
    tall = rows + 2 * PAD
    part = rows // blocks
    odd = me % 2 == 1
    facing = me // 2 + jnp.where(odd, 1, -1)
    inner = facing_in[...]
    outer = jnp.where((facing >= 0) & (facing < tiles // 2), facing_out[STEPS:, :], 0.0)
    before = jnp.where(odd, inner, outer)
    after = jnp.where(odd, outer, inner)

    all_planes = planes[...] + planes_of(last[0:STEPS, 0 : hot.shape[1]], hot, places, tall)
    inject = [all_planes[tall * t : tall * t + tall] for t in range(STEPS)]

    def extend(store, own, at, width):
        store(0, PAD, jnp.zeros((PAD, across), jnp.float32))
        store(PAD + rows, tall, jnp.zeros((PAD, across), jnp.float32))
        store(PAD, PAD + rows, own)
        store(PAD - width, PAD, before[at : at + width])
        store(PAD + rows, PAD + rows + width, after[at : at + width])

    for f, width in enumerate(HALO):
        def store(a, b, value, f=f):
            ext[f, a:b, :] = value
        extend(store, fields[f], HALO_AT[f], width)

    def store_cel(a, b, value):
        cel_ext[a:b, :] = value
    extend(store_cel, cel[...], CEL_AT, CEL_HALO)

    lane = lax.broadcasted_iota(jnp.int32, (tall, across), 1)
    first = lane == 0
    last = lane == across - 1
    speed = cel_ext[...]

    def horizontal(z):
        around = pltpu.roll(z, 1, 0) + pltpu.roll(z, tall - 1, 0)
        around += jnp.where(first, 0.0, pltpu.roll(z, 1, 1))
        around += jnp.where(last, 0.0, pltpu.roll(z, across - 1, 1))
        return speed * (around - 4.0 * z) + SHIFT * z

    def injected(n, k, a, b):
        total = None
        for tau in range(1, n - k + 1):
            r = n - tau
            term = coef[8 * r + k : 8 * r + k + 1, :] * inject[STEPS - tau][a:b]
            total = term if total is None else total + term
        return total

    base = horizontal(ext[0])
    for n in range(1, STEPS + 1):
        z = base
        for k in range(n - 1, 0, -1):
            z = horizontal(z + ext[FIELDS.index((n, k))] + injected(n, k, 0, tall))
        own = z[PAD : PAD + rows] + fields[FIELDS.index((n, 0))] + injected(n, 0, PAD, PAD + rows)
        t = STEPS - n
        for b in range(blocks):
            stage[b, part * t : part * t + part, :] = own[part * b : part * b + part]
    block = lax.axis_index("tblock")
    for r, out in enumerate(outs):
        out[...] = stage[block ^ r]


def prior_kernel(*refs):
    gots, (weight, out, whole, done, sems) = refs[:-5], refs[-5:]
    block = lax.axis_index("tblock")
    for r, got in enumerate(reversed(gots)):
        whole[block ^ r] = got[...]
    part = out.shape[1]
    length = out.shape[0]
    width = weight.shape[0]
    factor = [weight[j : j + 1, :] for j in range(width)]
    copies = []

    def finish(p):
        if (p + 1) % (length // 4) == 0:
            cut = pl.ds(p + 1 - length // 4, length // 4)
            copies.append(pltpu.make_async_copy(done.at[cut], out.at[cut], sems.at[len(copies)]))
            copies[-1].start()

    if 2 * part != 8:
        series = [whole[i // STEPS, part * (i % STEPS) : part * (i % STEPS) + part, :] for i in range(length)]
        for k in range(length):
            done[k] = sum(factor[j] * series[k + j] for j in range(min(width, length - k)))
            finish(k)
        for copy in copies:
            copy.wait()
        return
    pairs = length // 2
    even = [whole[p // 2, 8 * (p % 2) : 8 * (p % 2) + 8, :] for p in range(pairs)]
    half = lax.broadcasted_iota(jnp.int32, even[0].shape, 0) < part
    turned = [pltpu.roll(x, part, 0) for x in even] + [jnp.zeros(even[0].shape, jnp.float32)]
    odd = [jnp.where(half, turned[p], turned[p + 1]) for p in range(pairs)]
    for p in range(pairs):
        total = None
        for j in range(width):
            if p + j // 2 < pairs:
                term = factor[j] * (odd if j % 2 else even)[p + j // 2]
                total = term if total is None else total + term
        done[2 * p] = total[:part]
        done[2 * p + 1] = total[part:]
        finish(2 * p + 1)
    for copy in copies:
        copy.wait()


def shape(*dims, dtype=jnp.float32):
    return jax.ShapeDtypeStruct(dims, dtype)


def spec(space):
    return pl.BlockSpec(memory_space=space)


def body(
    adjoint_eta,
    adjoint_flow,
    residual,
    sensor_cell,
    sensor_count,
    depth_class,
    speed_table,
    damping,
    profile,
    band_weight,
):
    tiles = lax.axis_size("trench")
    blocks = lax.axis_size("tblock")
    levels, rows, across = adjoint_eta.shape[1:]
    tall = rows + 2 * PAD
    params = pltpu.CompilerParams(vmem_limit_bytes=LIMIT)

    def swaps(parts, axis):
        devices = lax.axis_size(axis)
        moved = {r: lax.ppermute(parts[r], axis, [(i, i ^ r) for i in range(devices)]) for r in range(devices - 1, 0, -1)}
        return [parts[0]] + [moved[r] for r in range(1, devices)]

    own = residual[0, 0]
    slots = own.shape[2]
    chips = tiles // 2

    def meet(x, d):
        pairs = [(2 * c + 1, 2 * ((c + d) % chips)) for c in range(chips)]
        return lax.ppermute(x, "trench", pairs + [(j, i) for i, j in pairs])

    partner = meet(own, 0)
    matrix = shape(16 * (len(FIELDS) + 1), 8 * levels, dtype=jnp.bfloat16)
    w_eta, w_flow, cel, coef, factor, own, eta, flow = pl.pallas_call(
        prepare_kernel,
        out_shape=(
            matrix,
            matrix,
            shape(rows, across),
            shape(8 * STEPS, across),
            shape(band_weight.shape[0], across),
            shape(*own.shape),
            shape(*adjoint_eta.shape),
            shape(*adjoint_flow.shape),
        ),
        in_specs=[spec(pltpu.HBM)] * 8,
        out_specs=(spec(VMEM),) * 8,
        scratch_shapes=[
            VMEM((rows, across), jnp.int32),
            SMEM(speed_table.shape, jnp.float32),
            VMEM((1, levels), jnp.float32),
            VMEM((1, levels), jnp.float32),
            VMEM((1, band_weight.shape[0]), jnp.float32),
            pltpu.SemaphoreType.DMA((8,)),
        ],
        compiler_params=params,
        cost_estimate=pl.CostEstimate(flops=10**7, bytes_accessed=4 * 10**6, transcendentals=0),
        name="prepare",
    )(
        *[
            pltpu.with_memory_space_constraint(x, pltpu.HBM)
            for x in (
                depth_class, speed_table, damping[None], profile[None], band_weight[None],
                own, adjoint_eta, adjoint_flow,
            )
        ]
    )
    fields, inner, outer, *relays = pl.pallas_call(
        contract_kernel,
        out_shape=(
            shape(len(FIELDS), rows, across),
            shape(ROWS, across),
            shape(STEPS + ROWS, across),
        ) + (shape(STEPS, 6 * slots),) * (chips - 2),
        in_specs=[spec(VMEM)] * 7,
        out_specs=(spec(VMEM),) * (1 + chips),
        compiler_params=params,
        cost_estimate=pl.CostEstimate(flops=10**9, bytes_accessed=4 * 10**6, transcendentals=0),
        name="contract",
    )(eta, flow, w_eta, w_flow, cel, own, partner)
    facing_out = meet(outer, 1)
    gots = [facing_out] + [meet(relay, d) for d, relay in enumerate(relays, 2)]
    facing_in = meet(inner, 0)

    def slot_shapes(count):
        return shape(across, 3 * slots * count, dtype=jnp.bfloat16), shape(8, 3 * slots * count, dtype=jnp.int32)

    hot, places, hot_late, places_late = pl.pallas_call(
        functools.partial(sensors_kernel, rows),
        out_shape=slot_shapes(tiles - 2) + slot_shapes(2),
        in_specs=[spec(VMEM), spec(SMEM)],
        out_specs=(spec(VMEM),) * 4,
        compiler_params=params,
        cost_estimate=pl.CostEstimate(flops=10**6, bytes_accessed=2 * 10**6, transcendentals=0),
        name="sensors",
    )(sensor_cell, sensor_count)
    planes = pl.pallas_call(
        inject_kernel,
        out_shape=shape(STEPS * (rows + 2 * PAD), across),
        in_specs=[spec(VMEM)] * (3 + len(gots)),
        out_specs=spec(VMEM),
        compiler_params=params,
        cost_estimate=pl.CostEstimate(flops=1000, bytes_accessed=1000, transcendentals=0),
        name="inject",
    )(hot, places, own, partner, *gots[:-1])
    series = pl.pallas_call(
        functools.partial(advance_kernel, tiles),
        out_shape=(shape(STEPS * rows // blocks, across),) * blocks,
        in_specs=[spec(VMEM)] * 9,
        out_specs=(spec(VMEM),) * blocks,
        scratch_shapes=[
            VMEM((blocks, STEPS * rows // blocks, across), jnp.float32),
            VMEM((len(HALO), tall, across), jnp.float32),
            VMEM((tall, across), jnp.float32),
        ],
        compiler_params=params,
        name="advance",
    )(fields, cel, coef, hot_late, places_late, facing_in, facing_out, gots[-1], planes)
    gots = swaps(series, "tblock")
    return pl.pallas_call(
        prior_kernel,
        out_shape=shape(STEPS * blocks, rows // blocks, across),
        in_specs=[spec(VMEM)] * (blocks + 1),
        out_specs=spec(pl.ANY),
        scratch_shapes=[
            VMEM((blocks, STEPS * rows // blocks, across), jnp.float32),
            VMEM((STEPS * blocks, rows // blocks, across), jnp.float32),
            pltpu.SemaphoreType.DMA((4,)),
        ],
        compiler_params=params,
        name="prior",
    )(*reversed(gots), factor)


def solution(mesh):
    in_specs = (
        P("tblock", None, "trench", None),
        P("tblock", None, "trench", None),
        P("tblock", "trench", None, None, None),
        P(),
        P(),
        P("trench", None),
        P(),
        P(),
        P(),
        P(),
    )
    out_specs = P(None, ("trench", "tblock"), None)
    return jax.shard_map(body, mesh=mesh, in_specs=in_specs, out_specs=out_specs, check_vma=False)
```

```python
import functools
import math

import jax
import jax.numpy as jnp
from jax import lax
from jax.experimental import pallas as pl
from jax.experimental.pallas import tpu as pltpu
from jax.sharding import PartitionSpec as P

VERT = 0.2
STEPS = 4
PAD = 8
VMEM = pltpu.VMEM
SMEM = pltpu.SMEM
LIMIT = 32 * 1024 * 1024

SHIFT = 1.2

FIELDS = [(4, 4), (4, 3), (4, 2), (3, 2), (4, 1), (3, 1), (2, 1), (4, 0), (3, 0), (2, 0), (1, 0)]
HALO = [4, 3, 2, 2, 1, 1, 1]
HALO_AT = [0, 4, 7, 9, 11, 12, 13]
CEL_AT = 14
CEL_HALO = 3
ROWS = 17


def split(x):
    hi = x.astype(jnp.bfloat16)
    return hi, (x - hi.astype(jnp.float32)).astype(jnp.bfloat16)


def dot(a, b, dims=((1,), (0,))):
    return lax.dot_general(a, b, (dims, ((), ())), preferred_element_type=jnp.float32)


def prepare_kernel(
    depth, table, damping, profile, band, residual, eta, flow,
    w_eta, w_flow, cel, coef, factor, own, eta_v, flow_v,
    depth_v, table_s, damping_v, profile_v, band_v, sems,
):
    rows, across = cel.shape
    levels = damping.shape[1]
    copies = [
        pltpu.make_async_copy(src, dst, sems.at[i])
        for i, (src, dst) in enumerate((
            (damping, damping_v), (profile, profile_v), (table, table_s), (depth, depth_v),
            (band, band_v), (residual, own), (eta, eta_v), (flow, flow_v),
        ))
    ]
    for copy in copies:
        copy.start()
    for copy in copies[:2]:
        copy.wait()

    lane = lax.broadcasted_iota(jnp.int32, (8, 128), 1)
    sub = lax.broadcasted_iota(jnp.int32, (8, 128), 0)
    inside = lane < levels
    fill = jnp.zeros((1, 128 - levels), jnp.float32)
    keep = jnp.broadcast_to(jnp.concatenate([damping_v[...], fill], axis=1), (8, 128))
    weight = jnp.broadcast_to(jnp.concatenate([profile_v[...], fill], axis=1), (8, 128))
    u = jnp.zeros((8, 128), jnp.float32)
    v = jnp.where(sub == 0, weight * (1.0 / math.sqrt(levels)), 0.0)
    us, vs = [u], [v]
    for r in range(STEPS):
        s = u + v
        bottom = jnp.sum(jnp.where(lane == levels - 1, s, 0.0), axis=1, keepdims=True)
        coef[8 * r : 8 * r + 8, :] = jnp.broadcast_to(bottom, (8, coef.shape[1]))
        vertical = pltpu.roll(s, 1, 1) + pltpu.roll(s, 127, 1) - 2.0 * s
        u = jnp.where(inside, u + VERT * vertical - SHIFT * s + pltpu.roll(s, 1, 0), 0.0)
        v = s * keep
        us.append(u)
        vs.append(v)

    wide = w_eta.shape[1]
    spread = (
        lax.broadcasted_iota(jnp.int32, (128, wide), 1) // 8
        == lax.broadcasted_iota(jnp.int32, (128, wide), 0)
    ).astype(jnp.bfloat16)
    count_f = len(FIELDS) + 1
    diagonal = (
        lax.broadcasted_iota(jnp.int32, (8 * count_f, wide), 1) % 8
        == lax.broadcasted_iota(jnp.int32, (8 * count_f, wide), 0) % 8
    )

    def matrix(vectors):
        blocks = [jnp.broadcast_to(vectors[n][k : k + 1, :], (8, 128)) for n, k in FIELDS]
        blocks.append(jnp.zeros((8, 128), jnp.float32))
        hi, lo = split(jnp.concatenate(blocks, axis=0))
        zero = jnp.zeros((8 * count_f, wide), jnp.float32)
        hi = jnp.where(diagonal, dot(hi, spread), zero).astype(jnp.bfloat16)
        lo = jnp.where(diagonal, dot(lo, spread), zero).astype(jnp.bfloat16)
        return jnp.concatenate([hi, lo], axis=0)

    w_eta[...] = matrix(us)
    w_flow[...] = matrix(vs)

    for copy in copies[2:-2]:
        copy.wait()

    classes = depth_v[...]
    speed = jnp.zeros(classes.shape, jnp.float32)
    for c in range(table_s.shape[0]):
        speed = jnp.where(classes == c, table_s[c], speed)
    cel[...] = speed
    for j in range(factor.shape[0]):
        factor[j : j + 1, :] = jnp.broadcast_to(band_v[:, j : j + 1], (1, across))

    for copy in copies[-2:]:
        copy.wait()


def contract_kernel(eta, flow, w_eta, w_flow, cel, own, partner, fields, inner, outer, *relays):
    levels, rows, across = eta.shape[1:]
    wide = w_eta.shape[1]
    half = w_eta.shape[0] // 2
    for h in range(rows // 8):
        hi, lo = split(eta[0, :, 8 * h : 8 * h + 8, :].reshape(wide, across))
        total = dot(w_eta[...], hi)
        part = dot(w_eta[0:half, :], lo)
        hi, lo = split(flow[0, :, 8 * h : 8 * h + 8, :].reshape(wide, across))
        total += dot(w_flow[...], hi)
        part += dot(w_flow[0:half, :], lo)
        part = part + total[:half] + total[half:]
        for f in range(len(FIELDS)):
            fields[f, 8 * h : 8 * h + 8, :] = part[8 * f : 8 * f + 8]

    me = lax.axis_index("trench")
    tiles = own.shape[0]
    for d, out in enumerate((outer, *relays), 1):
        out[0:STEPS, :] = widen([both_rows(met(me, d, tiles), own, partner)], out.shape[1])

    def edge(out, at, last):
        for f, width in enumerate(HALO):
            start = rows - width if last else 0
            out[at + HALO_AT[f] : at + HALO_AT[f] + width, :] = fields[f, start : start + width, :]
        start = rows - CEL_HALO if last else 0
        out[at + CEL_AT : at + CEL_AT + CEL_HALO, :] = cel[start : start + CEL_HALO, :]

    @pl.when(me % 2 == 0)
    def _():
        edge(inner, 0, True)
        edge(outer, STEPS, False)

    @pl.when(me % 2 == 1)
    def _():
        edge(inner, 0, False)
        edge(outer, STEPS, True)


def met(me, d, tiles):
    odd = me % 2
    chip = (me // 2 + jnp.where(odd == 1, d, tiles // 2 - d)) % (tiles // 2)
    return jnp.where(d == 0, me, 2 * chip + 1 - odd)


def sources(me, tiles):
    listed = [met(me, d, tiles) ^ core for d in range(tiles // 2) for core in range(2)]
    return listed[:-2], listed[-2:]


def widen(values, lanes):
    fill = lanes - sum(value.shape[1] for value in values)
    if fill:
        values = values + [jnp.zeros((STEPS, fill), jnp.float32)]
    return jnp.concatenate(values, axis=1)


def residual_rows(owner, own):
    tiles = own.shape[0]
    return jnp.concatenate([own[jnp.clip(owner + d - 1, 0, tiles - 1)] for d in range(3)], axis=1)


def both_rows(owner, own, partner):
    return jnp.concatenate([residual_rows(owner, own), residual_rows(owner, partner)], axis=1)


def sensors_kernel(rows, cells, count, hot_early, places_early, hot_late, places_late):
    me = lax.axis_index("trench")
    tiles, _, slots = cells.shape
    across = hot_early.shape[0]
    slot = lax.broadcasted_iota(jnp.int32, (1, slots), 1)
    bits = across.bit_length() - 1

    def list_slots(listed_sources, hot, places):
        listed = []
        for source in listed_sources:
            for d in range(3):
                owner = me + d - 1
                inside = (owner >= 0) & (owner < tiles)
                owner = jnp.clip(owner, 0, tiles - 1)
                live = jnp.where(inside, count[source, owner], 0)
                listed.append(jnp.where(slot < live, cells[source, pl.ds(owner, 1), :], -1))
        listed = jnp.concatenate(listed, axis=1)
        tile = (lax.broadcasted_iota(jnp.int32, listed.shape, 1) // slots) % 3
        at = jnp.where(listed < 0, -1, (listed >> bits) + (rows * (tile - 1) + PAD))
        places[...] = jnp.broadcast_to(at, places.shape)
        columns = listed & (across - 1)
        hot[...] = jnp.where(lax.broadcasted_iota(jnp.int32, hot.shape, 0) == columns, 1.0, 0.0).astype(jnp.bfloat16)

    early, late = sources(me, tiles)
    list_slots(early, hot_early, places_early)
    list_slots(late, hot_late, places_late)


def planes_of(values, hot, places, tall):
    here = lax.broadcasted_iota(jnp.int32, (tall, values.shape[1]), 0) == places[0:1, :]
    left = jnp.concatenate([jnp.where(here, values[t : t + 1, :], 0.0) for t in range(STEPS)], axis=0)
    both = dot(jnp.concatenate(split(left), axis=0), hot[...], ((1,), (1,)))
    return both[: STEPS * tall] + both[STEPS * tall :]


def inject_kernel(hot, places, own, partner, *refs):
    gots, planes = refs[:-1], refs[-1]
    per = 6 * own.shape[2]
    values = [both_rows(lax.axis_index("trench"), own, partner)] + [got[0:STEPS, 0:per] for got in gots]
    planes[...] = planes_of(jnp.concatenate(values, axis=1), hot, places, planes.shape[0] // STEPS)


def advance_kernel(tiles, fields, cel, coef, hot, places, facing_in, facing_out, last, planes, *refs):
    outs, (stage, ext, cel_ext) = refs[:-3], refs[-3:]
    blocks = len(outs)
    me = lax.axis_index("trench")
    rows, across = cel.shape
    tall = rows + 2 * PAD
    part = rows // blocks
    odd = me % 2 == 1
    facing = me // 2 + jnp.where(odd, 1, -1)
    inner = facing_in[...]
    outer = jnp.where((facing >= 0) & (facing < tiles // 2), facing_out[STEPS:, :], 0.0)
    before = jnp.where(odd, inner, outer)
    after = jnp.where(odd, outer, inner)

    all_planes = planes[...] + planes_of(last[0:STEPS, 0 : hot.shape[1]], hot, places, tall)
    inject = [all_planes[tall * t : tall * t + tall] for t in range(STEPS)]

    def extend(store, own, at, width):
        store(0, PAD, jnp.zeros((PAD, across), jnp.float32))
        store(PAD + rows, tall, jnp.zeros((PAD, across), jnp.float32))
        store(PAD, PAD + rows, own)
        store(PAD - width, PAD, before[at : at + width])
        store(PAD + rows, PAD + rows + width, after[at : at + width])

    for f, width in enumerate(HALO):
        def store(a, b, value, f=f):
            ext[f, a:b, :] = value
        extend(store, fields[f], HALO_AT[f], width)

    def store_cel(a, b, value):
        cel_ext[a:b, :] = value
    extend(store_cel, cel[...], CEL_AT, CEL_HALO)

    lane = lax.broadcasted_iota(jnp.int32, (tall, across), 1)
    first = lane == 0
    last = lane == across - 1
    speed = cel_ext[...]

    def horizontal(z):
        around = pltpu.roll(z, 1, 0) + pltpu.roll(z, tall - 1, 0)
        around += jnp.where(first, 0.0, pltpu.roll(z, 1, 1))
        around += jnp.where(last, 0.0, pltpu.roll(z, across - 1, 1))
        return speed * (around - 4.0 * z) + SHIFT * z

    def injected(n, k, a, b):
        total = None
        for tau in range(1, n - k + 1):
            r = n - tau
            term = coef[8 * r + k : 8 * r + k + 1, :] * inject[STEPS - tau][a:b]
            total = term if total is None else total + term
        return total

    base = horizontal(ext[0])
    for n in range(1, STEPS + 1):
        z = base
        for k in range(n - 1, 0, -1):
            z = horizontal(z + ext[FIELDS.index((n, k))] + injected(n, k, 0, tall))
        own = z[PAD : PAD + rows] + fields[FIELDS.index((n, 0))] + injected(n, 0, PAD, PAD + rows)
        t = STEPS - n
        for b in range(blocks):
            stage[b, part * t : part * t + part, :] = own[part * b : part * b + part]
    block = lax.axis_index("tblock")
    for r, out in enumerate(outs):
        out[...] = stage[block ^ r]


def prior_kernel(*refs):
    gots, (weight, out, whole, done, sems) = refs[:-5], refs[-5:]
    block = lax.axis_index("tblock")
    for r, got in enumerate(reversed(gots)):
        whole[block ^ r] = got[...]
    part = out.shape[1]
    length = out.shape[0]
    width = weight.shape[0]
    factor = [weight[j : j + 1, :] for j in range(width)]
    copies = []

    def finish(p):
        if (p + 1) % (length // 4) == 0:
            cut = pl.ds(p + 1 - length // 4, length // 4)
            copies.append(pltpu.make_async_copy(done.at[cut], out.at[cut], sems.at[len(copies)]))
            copies[-1].start()

    if 2 * part != 8:
        series = [whole[i // STEPS, part * (i % STEPS) : part * (i % STEPS) + part, :] for i in range(length)]
        for k in range(length):
            done[k] = sum(factor[j] * series[k + j] for j in range(min(width, length - k)))
            finish(k)
        for copy in copies:
            copy.wait()
        return
    pairs = length // 2
    even = [whole[p // 2, 8 * (p % 2) : 8 * (p % 2) + 8, :] for p in range(pairs)]
    half = lax.broadcasted_iota(jnp.int32, even[0].shape, 0) < part
    turned = [pltpu.roll(x, part, 0) for x in even] + [jnp.zeros(even[0].shape, jnp.float32)]
    odd = [jnp.where(half, turned[p], turned[p + 1]) for p in range(pairs)]
    for p in range(pairs):
        total = None
        for j in range(width):
            if p + j // 2 < pairs:
                term = factor[j] * (odd if j % 2 else even)[p + j // 2]
                total = term if total is None else total + term
        done[2 * p] = total[:part]
        done[2 * p + 1] = total[part:]
        finish(2 * p + 1)
    for copy in copies:
        copy.wait()


def shape(*dims, dtype=jnp.float32):
    return jax.ShapeDtypeStruct(dims, dtype)


def spec(space):
    return pl.BlockSpec(memory_space=space)


def body(
    adjoint_eta,
    adjoint_flow,
    residual,
    sensor_cell,
    sensor_count,
    depth_class,
    speed_table,
    damping,
    profile,
    band_weight,
):
    tiles = lax.axis_size("trench")
    blocks = lax.axis_size("tblock")
    levels, rows, across = adjoint_eta.shape[1:]
    tall = rows + 2 * PAD
    params = pltpu.CompilerParams(vmem_limit_bytes=LIMIT)

    def swaps(parts, axis):
        devices = lax.axis_size(axis)
        moved = {r: lax.ppermute(parts[r], axis, [(i, i ^ r) for i in range(devices)]) for r in range(devices - 1, 0, -1)}
        return [parts[0]] + [moved[r] for r in range(1, devices)]

    own = residual[0, 0]
    slots = own.shape[2]
    chips = tiles // 2

    def meet(x, d):
        pairs = [(2 * c + 1, 2 * ((c + d) % chips)) for c in range(chips)]
        return lax.ppermute(x, "trench", pairs + [(j, i) for i, j in pairs])

    partner = meet(own, 0)
    matrix = shape(16 * (len(FIELDS) + 1), 8 * levels, dtype=jnp.bfloat16)
    w_eta, w_flow, cel, coef, factor, own, eta, flow = pl.pallas_call(
        prepare_kernel,
        out_shape=(
            matrix,
            matrix,
            shape(rows, across),
            shape(8 * STEPS, across),
            shape(band_weight.shape[0], across),
            shape(*own.shape),
            shape(*adjoint_eta.shape),
            shape(*adjoint_flow.shape),
        ),
        in_specs=[spec(pltpu.HBM)] * 8,
        out_specs=(spec(VMEM),) * 8,
        scratch_shapes=[
            VMEM((rows, across), jnp.int32),
            SMEM(speed_table.shape, jnp.float32),
            VMEM((1, levels), jnp.float32),
            VMEM((1, levels), jnp.float32),
            VMEM((1, band_weight.shape[0]), jnp.float32),
            pltpu.SemaphoreType.DMA((8,)),
        ],
        compiler_params=params,
        cost_estimate=pl.CostEstimate(flops=10**7, bytes_accessed=4 * 10**6, transcendentals=0),
        name="prepare",
    )(
        *[
            pltpu.with_memory_space_constraint(x, pltpu.HBM)
            for x in (
                depth_class, speed_table, damping[None], profile[None], band_weight[None],
                own, adjoint_eta, adjoint_flow,
            )
        ]
    )
    fields, inner, outer, *relays = pl.pallas_call(
        contract_kernel,
        out_shape=(
            shape(len(FIELDS), rows, across),
            shape(ROWS, across),
            shape(STEPS + ROWS, across),
        ) + (shape(STEPS, 6 * slots),) * (chips - 2),
        in_specs=[spec(VMEM)] * 7,
        out_specs=(spec(VMEM),) * (1 + chips),
        compiler_params=params,
        cost_estimate=pl.CostEstimate(flops=10**9, bytes_accessed=4 * 10**6, transcendentals=0),
        name="contract",
    )(eta, flow, w_eta, w_flow, cel, own, partner)
    facing_out = meet(outer, 1)
    gots = [facing_out] + [meet(relay, d) for d, relay in enumerate(relays, 2)]
    facing_in = meet(inner, 0)

    def slot_shapes(count):
        return shape(across, 3 * slots * count, dtype=jnp.bfloat16), shape(8, 3 * slots * count, dtype=jnp.int32)

    hot, places, hot_late, places_late = pl.pallas_call(
        functools.partial(sensors_kernel, rows),
        out_shape=slot_shapes(tiles - 2) + slot_shapes(2),
        in_specs=[spec(VMEM), spec(SMEM)],
        out_specs=(spec(VMEM),) * 4,
        compiler_params=params,
        cost_estimate=pl.CostEstimate(flops=10**6, bytes_accessed=2 * 10**6, transcendentals=0),
        name="sensors",
    )(sensor_cell, sensor_count)
    planes = pl.pallas_call(
        inject_kernel,
        out_shape=shape(STEPS * (rows + 2 * PAD), across),
        in_specs=[spec(VMEM)] * (3 + len(gots)),
        out_specs=spec(VMEM),
        compiler_params=params,
        cost_estimate=pl.CostEstimate(flops=1000, bytes_accessed=1000, transcendentals=0),
        name="inject",
    )(hot, places, own, partner, *gots[:-1])
    series = pl.pallas_call(
        functools.partial(advance_kernel, tiles),
        out_shape=(shape(STEPS * rows // blocks, across),) * blocks,
        in_specs=[spec(VMEM)] * 9,
        out_specs=(spec(VMEM),) * blocks,
        scratch_shapes=[
            VMEM((blocks, STEPS * rows // blocks, across), jnp.float32),
            VMEM((len(HALO), tall, across), jnp.float32),
            VMEM((tall, across), jnp.float32),
        ],
        compiler_params=params,
        name="advance",
    )(fields, cel, coef, hot_late, places_late, facing_in, facing_out, gots[-1], planes)
    gots = swaps(series, "tblock")
    return pl.pallas_call(
        prior_kernel,
        out_shape=shape(STEPS * blocks, rows // blocks, across),
        in_specs=[spec(VMEM)] * (blocks + 1),
        out_specs=spec(pl.ANY),
        scratch_shapes=[
            VMEM((blocks, STEPS * rows // blocks, across), jnp.float32),
            VMEM((STEPS * blocks, rows // blocks, across), jnp.float32),
            pltpu.SemaphoreType.DMA((4,)),
        ],
        compiler_params=params,
        name="prior",
    )(*reversed(gots), factor)


def solution(mesh):
    in_specs = (
        P("tblock", None, "trench", None),
        P("tblock", None, "trench", None),
        P("tblock", "trench", None, None, None),
        P(),
        P(),
        P("trench", None),
        P(),
        P(),
        P(),
        P(),
    )
    out_specs = P(None, ("trench", "tblock"), None)
    return jax.shard_map(body, mesh=mesh, in_specs=in_specs, out_specs=out_specs, check_vma=False)
```
